32 devices in a mesh: dp: 8 (over z, y), mp: 4 (over x, core).
Axes of the slice: x: 2, y: 2, z: 4, core: 2. Of those that a mesh axis runs over, the one named last changes fastest.
Arguments:
- tokens: bfloat16 [2, 8192, 1024], P(None, 'dp'), may hold values from -6 to 6
- cotangent: bfloat16 [2, 8192, 1024], P(None, 'dp'), may hold values from -6 to 6
- lengths: int32 [2, 8, 4], P(None, 'dp'), may hold values from 1 to 768, 1024 in all within a row
- placement_ids: int32 [2, 8192], replicated, may hold values from 0 to 8191, as said below
- block_slot_index: int32 [12], replicated, may hold values from 0 to 15, as said below
- matrices: float32 [1024, 12, 1024], P('dp', None, 'mp')
- norm_vectors: float32 [6, 1024], P(None, 'dp')
- head_vectors: float32 [6, 1024], P(None, 'mp'), may hold values from -3 to 3
- left_stats: float32 [16, 1024, 1024], P('dp', 'mp'), as said below
- right_stats: float32 [16, 1024, 1024], P('dp', 'mp'), as said below
- left_roots: float32 [16, 1024, 1024], P('dp'), as said below
- right_roots: float32 [16, 1024, 1024], P('dp', 'mp'), as said below
- norm_state: float32 [6, 1024], P(None, 'dp'), may hold values from 16384 to 65536
- head_state: float32 [6, 1024], P(None, 'mp'), may hold values from 2048 to 32768
Outputs:
- block_output: bfloat16 [2, 8192, 1024], P(None, 'dp')
- input_grad: bfloat16 [2, 8192, 1024], P(None, 'dp')
- slot_block_grads: float32 [1024, 16, 1024], P(None, 'dp', 'mp')
- new_left: float32 [16, 1024, 1024], P('dp', 'mp')
- new_right: float32 [16, 1024, 1024], P('dp', 'mp')
- updated_blocks: float32 [1024, 16, 1024], P(None, 'dp', 'mp')
- norm_grads: float32 [6, 1024], P(None, 'dp')
- new_norm_state: float32 [6, 1024], P(None, 'dp')
- new_norm_vectors: float32 [6, 1024], P(None, 'dp')
- head_grads: float32 [6, 1024], P(None, 'mp')
- new_head_state: float32 [6, 1024], P(None, 'mp')
- new_head_vectors: float32 [6, 1024], P(None, 'mp')
The draws below stay inside these ranges and needn't reach their ends.
Inputs may be any that keep to these rules, and one draw needn't show every extreme that they name: `placement_ids`: for each micro-batch a permutation of the rows; balanced rows q * 1024 to q * 1024 + 1023 belong to dp device q, and of the 1024 given rows that dp device p holds exactly 128 go to each dp device. `block_slot_index`: distinct slots; slot o belongs to dp device o // 2. `right_roots`: symmetric in its last two dimensions. `left_roots`: symmetric in its last two dimensions. `left_stats`: symmetric in its last two dimensions. `right_stats`: symmetric in its last two dimensions.
All inputs are finite; a program needn't handle non-finite values.
Results may differ from the reference program's by a relative error of at most 0.01.
The reference program's roundings to bfloat16 on the way count: a program that leaves them out, or rounds other values in their place, can miss the bound.
Values may be sent and summed in bfloat16 or wider, within the bound.
No kernel may reach another device: no remote copies, remote signals or barrier semaphores. Data moves between devices by JAX's collectives and lax.ppermute only.
A program may use at most 256 MiB of HBM per device.

```python
import math
import jax
import jax.numpy as jnp
import numpy as np
from jax import lax

MODEL_DIMENSION = 1024
HEADS = 16
HEAD_DIM = 64
FF = 4096
CAP = 1024
MB = 2
NSEG = 4
SEQ_MOST = 768
NROWS = 8192
TOKENS = 16384
WEIGHT_BLOCKS = 12
NHV = 6
OPTIMIZER_SLOTS = 16
N_DP = 8


def draw_placement_ids(key, part):
    key = jax.random.fold_in(key, 31)

    def one_batch(batch_key):
        random_key_one, random_key_two = jax.random.split(batch_key)
        slots_of = jax.vmap(lambda k: jax.random.permutation(k, CAP))(jax.random.split(random_key_one, N_DP))
        global_slots = slots_of + (jnp.arange(N_DP) * CAP)[:, None]
        global_slots = global_slots.reshape(N_DP, N_DP, CAP // N_DP).transpose(1, 0, 2).reshape(N_DP, CAP)
        shuffle = jax.vmap(lambda k: jax.random.permutation(k, CAP))(jax.random.split(random_key_two, N_DP))
        return jnp.take_along_axis(global_slots, shuffle, axis=1).reshape(N_DP * CAP)
    return jax.vmap(one_batch)(jax.random.split(key, MB)).astype(jnp.int32)


def owner_slots(key):
    base = jax.random.fold_in(key, 11)
    random_key_one, random_key_two = jax.random.split(base)
    midpoint_value = jax.random.permutation(random_key_one, OPTIMIZER_SLOTS - 2)[:WEIGHT_BLOCKS - 2] + 1
    picked_slot = jnp.concatenate([jnp.array([0, OPTIMIZER_SLOTS - 1], jnp.int32), midpoint_value.astype(jnp.int32)])
    return jax.random.permutation(random_key_two, picked_slot).astype(jnp.int32)


def draw_block_slot_index(key, part):
    return owner_slots(key)


def slot_level(key):
    owning_slots = owner_slots(key)
    ffn_count = FF // MODEL_DIMENSION
    block_index = jnp.arange(WEIGHT_BLOCKS)
    cost_guess = jnp.where(block_index < 2, 0.8, jnp.where(block_index == 2, 1.2, jnp.where(block_index == 3, 0.7, jnp.where(block_index < 4 + ffn_count, 0.3, 0.65))))
    each_slot_blocks = jnp.ones((OPTIMIZER_SLOTS,), jnp.float32).at[owning_slots].set(cost_guess.astype(jnp.float32))
    return each_slot_blocks * each_slot_blocks * float(TOKENS) * float(MODEL_DIMENSION)


def symmetric_part(drawn_sample):
    return (drawn_sample + jnp.swapaxes(drawn_sample, 1, 2)) * (0.3 / math.sqrt(2.0 * MODEL_DIMENSION))


def draw_left_stats(key, part):
    level_of = slot_level(key)
    random_key_one, random_key_two = jax.random.split(jax.random.fold_in(key, 21))
    several_factor = jax.random.uniform(random_key_one, (OPTIMIZER_SLOTS, 1, 1), jnp.float32, 1.0, 4.0)
    drawn_sample = jax.random.normal(random_key_two, (OPTIMIZER_SLOTS, MODEL_DIMENSION, MODEL_DIMENSION), jnp.float32)
    return level_of[:, None, None] * several_factor * (jnp.eye(MODEL_DIMENSION, dtype=jnp.float32)[None] + symmetric_part(drawn_sample))


def draw_right_stats(key, part):
    level_of = slot_level(key)
    random_key_one, random_key_two = jax.random.split(jax.random.fold_in(key, 22))
    several_factor = jax.random.uniform(random_key_one, (OPTIMIZER_SLOTS, 1, 1), jnp.float32, 1.0, 4.0)
    drawn_sample = jax.random.normal(random_key_two, (OPTIMIZER_SLOTS, MODEL_DIMENSION, MODEL_DIMENSION), jnp.float32)
    return level_of[:, None, None] * several_factor * (jnp.eye(MODEL_DIMENSION, dtype=jnp.float32)[None] + symmetric_part(drawn_sample))


def draw_left_roots(key, part):
    level_of = slot_level(key)
    random_key_one, random_key_two = jax.random.split(jax.random.fold_in(key, 23))
    several_factor = jax.random.uniform(random_key_one, (OPTIMIZER_SLOTS, 1, 1), jnp.float32, 0.7, 1.4)
    drawn_sample = jax.random.normal(random_key_two, (OPTIMIZER_SLOTS, MODEL_DIMENSION, MODEL_DIMENSION), jnp.float32)
    return (level_of ** (-0.25))[:, None, None] * several_factor * (jnp.eye(MODEL_DIMENSION, dtype=jnp.float32)[None] + symmetric_part(drawn_sample))


def draw_right_roots(key, part):
    level_of = slot_level(key)
    random_key_one, random_key_two = jax.random.split(jax.random.fold_in(key, 24))
    several_factor = jax.random.uniform(random_key_one, (OPTIMIZER_SLOTS, 1, 1), jnp.float32, 0.7, 1.4)
    drawn_sample = jax.random.normal(random_key_two, (OPTIMIZER_SLOTS, MODEL_DIMENSION, MODEL_DIMENSION), jnp.float32)
    return (level_of ** (-0.25))[:, None, None] * several_factor * (jnp.eye(MODEL_DIMENSION, dtype=jnp.float32)[None] + symmetric_part(drawn_sample))


def draw_matrices(key, part):
    key = jax.random.fold_in(key, 41)
    ffn_count = FF // MODEL_DIMENSION
    block_index = jnp.arange(WEIGHT_BLOCKS)
    scales = jnp.where(block_index < 2, (0.5 * MODEL_DIMENSION) ** (-0.5), jnp.where(block_index >= 4 + ffn_count, float(FF) ** (-0.5), float(MODEL_DIMENSION) ** (-0.5)))
    drawn_sample = jax.random.normal(key, (MODEL_DIMENSION, WEIGHT_BLOCKS, MODEL_DIMENSION), jnp.float32)
    return drawn_sample * scales.astype(jnp.float32)[None, :, None]


def draw_norm_vectors(key, part):
    key = jax.random.fold_in(key, 51)
    row_index = jnp.arange(6)[:, None]
    is_gain = (row_index == 0) | (row_index == 3)
    drawn_sample = jax.random.normal(key, (6, MODEL_DIMENSION), jnp.float32)
    return jnp.where(is_gain, 1.0 + 0.1 * drawn_sample, 0.2 * drawn_sample)


def block_levels(own_key, shape, shards, least, top_value):
    level = 1.0
    for dim, blocks in shards:
        draws = jax.random.uniform(jax.random.fold_in(jax.random.fold_in(own_key, 6), dim), (blocks,), jnp.float32, least / len(shards), top_value / len(shards))
        level = level * jnp.repeat(jnp.exp(draws), shape[dim] // blocks).reshape((-1,) + (1,) * (len(shape) - 1 - dim))
    return level


def profile(count, total, most, skew):
    portions = [(1 << 20) // math.isqrt(standing ** skew) + 1 for standing in range(2, count + 1)]
    spare, holding = total - most - (count - 1), [1] * (count - 1)
    while spare > 0:
        free = [i for i in range(count - 1) if holding[i] < most]
        mass, budget = sum([portions[i] for i in free]), spare
        for i in free:
            addition = min(most - holding[i], max(1, budget * portions[i] // mass), spare)
            holding[i] = holding[i] + addition
            spare = spare - addition
    return np.array([most] + holding)


def ragged_sizes(rng, number_of, total, reach, slope):
    if number_of == 2:
        one = jax.random.randint(rng, (), max(1, total - reach), min(reach, total - 1) + 1)
        return jnp.stack([one, total - one])
    tallies = jnp.asarray(profile(number_of, total, reach, slope), jnp.int32)
    pairs = (number_of - 1) // 2
    source_of, receiver = tallies[1:1 + 2 * pairs:2], tallies[2:2 + 2 * pairs:2]
    margin = jnp.minimum(source_of - 1, reach - receiver)
    moved = jax.random.randint(jax.random.fold_in(rng, 1), (pairs,), 0, 1 << 20) % (margin + 1)
    tallies = tallies.at[1:1 + 2 * pairs:2].set(source_of - moved).at[2:2 + 2 * pairs:2].set(receiver + moved)
    return tallies[jax.random.permutation(jax.random.fold_in(rng, 2), number_of)]


def noise(stream_key, dims, scale, most, cuts=(), held_as=jnp.bfloat16):
    values = jax.random.normal(stream_key, dims, jnp.float32) * scale
    if len(cuts) > 0:
        values = block_levels(stream_key, dims, cuts, -0.22, 0.18) * values
    return jnp.clip(values, min=-most, max=most).astype(held_as)


def setup_inputs(seed: int = 0) -> dict:
    arg_keys = jax.random.split(jax.random.key(seed), 15)
    return {
        "tokens": noise(arg_keys[0], (MB, NROWS, MODEL_DIMENSION), 1.0, 6.0, ((1, 8),)),
        "cotangent": noise(arg_keys[1], (MB, NROWS, MODEL_DIMENSION), 1.0, 6.0, ((1, 8),)),
        "lengths": jax.vmap(lambda own: ragged_sizes(own, NSEG, CAP, SEQ_MOST, 2))(jax.random.split(arg_keys[2], MB * N_DP)).reshape((MB, N_DP, NSEG)).astype(jnp.int32),
        "placement_ids": draw_placement_ids(jax.random.fold_in(arg_keys[14], 71), 0),
        "block_slot_index": draw_block_slot_index(jax.random.fold_in(arg_keys[14], 71), 0),
        "matrices": draw_matrices(jax.random.fold_in(arg_keys[14], 71), 0),
        "norm_vectors": draw_norm_vectors(jax.random.fold_in(arg_keys[14], 71), 0),
        "head_vectors": noise(arg_keys[7], (NHV, MODEL_DIMENSION), 0.2, 3.0, ((1, 4),), jnp.float32),
        "left_stats": draw_left_stats(jax.random.fold_in(arg_keys[14], 71), 0),
        "right_stats": draw_right_stats(jax.random.fold_in(arg_keys[14], 71), 0),
        "left_roots": draw_left_roots(jax.random.fold_in(arg_keys[14], 71), 0),
        "right_roots": draw_right_roots(jax.random.fold_in(arg_keys[14], 71), 0),
        "norm_state": jnp.clip(jnp.exp(math.log(65536.0) - 1.3862944 * jax.random.uniform(arg_keys[12], (6, MODEL_DIMENSION), jnp.float32) ** block_levels(arg_keys[12], (6, MODEL_DIMENSION), ((1, 8),), -0.2, 0.2)), 16384.0, 65536.0),
        "head_state": jnp.clip(jnp.exp(math.log(32768.0) - 2.7725887 * jax.random.uniform(arg_keys[13], (NHV, MODEL_DIMENSION), jnp.float32) ** block_levels(arg_keys[13], (NHV, MODEL_DIMENSION), ((1, 4),), -0.2, 0.2)), 2048.0, 32768.0),
    }


@jax.custom_vjp
def low(v):
    return lax.optimization_barrier(v.astype(jnp.bfloat16)).astype(jnp.float32)

@jax.custom_vjp
def low_back(v):
    return v

def low_keep(v):
    return (low(v), None)

def low_pass(kept, grad):
    return (grad,)

def back_keep(v):
    return (v, None)

def back_low(kept, grad):
    return (low(grad),)
low.defvjp(low_keep, low_pass)
low_back.defvjp(back_keep, back_low)
stat_decay = 0.5
matrix_rate = 0.02
vector_rate = 0.3
norm_eps = 1e-05
mean_eps = 1e-06
diag_eps = 1e-08
masked_score = -1000000000.0

def product(left_side, right_side):
    return jnp.dot(left_side, right_side, precision=lax.Precision.HIGHEST, preferred_element_type=jnp.float32)

def layer_norm(values, gain, shift):
    center = values - lax.optimization_barrier(jnp.mean(values, axis=-1, keepdims=True))
    spread = lax.optimization_barrier(jnp.mean(center * center, axis=-1, keepdims=True))
    return center * lax.rsqrt(spread + norm_eps) * gain + shift

def block_forward(matrices, norm_vectors, head_vectors, block_rows, segment):
    highest = lax.Precision.HIGHEST
    ffn_count = FF // MODEL_DIMENSION
    count = block_rows.shape[0]
    normed = low(layer_norm(block_rows, norm_vectors[0], norm_vectors[1]))
    queries = low(low_back(product(normed, matrices[:, 0, :]) + head_vectors[0]))
    keys_all = low(low_back(product(normed, matrices[:, 1, :])))
    values = low(low_back(product(normed, matrices[:, 2, :]) + head_vectors[1]))
    query_heads = queries.reshape(count, HEADS, HEAD_DIM)
    key_heads = keys_all.reshape(count, HEADS, HEAD_DIM)
    value_heads = values.reshape(count, HEADS, HEAD_DIM)
    raw_scores = jnp.einsum('qhd,khd->hqk', query_heads, key_heads, precision=highest)
    scores = low_back(raw_scores * (1.0 / math.sqrt(HEAD_DIM)))
    positions = jnp.arange(count)
    allowed = (segment[:, None] == segment[None, :]) & (positions[:, None] >= positions[None, :])
    scores = jnp.where(allowed[None], scores, masked_score)
    attention = jax.nn.softmax(scores, axis=-1)
    mixed = jnp.einsum('hqk,khd->qhd', low(attention), value_heads, precision=highest)
    attended = low(low_back(mixed.reshape(count, MODEL_DIMENSION)))
    branch = low_back(jnp.einsum('ql,ml->qm', attended, matrices[:, 3, :], precision=highest))
    hidden = block_rows + branch + norm_vectors[2]
    normed_two = low(layer_norm(hidden, norm_vectors[3], norm_vectors[4]))
    w_up = matrices[:, 4:4 + ffn_count, :].reshape(MODEL_DIMENSION, FF)
    w_down = matrices[:, 4 + ffn_count:, :].reshape(MODEL_DIMENSION, FF)
    up_in = low_back(product(normed_two, w_up) + head_vectors[2:].reshape(FF))
    active = low(jax.nn.gelu(up_in, approximate=True))
    return hidden + jnp.einsum('qf,mf->qm', active, w_down, precision=highest) + norm_vectors[5]

def reference(tokens, cotangent, lengths, placement_ids, block_slot_index, matrices, norm_vectors, head_vectors, left_stats, right_stats, left_roots, right_roots, norm_state, head_state):
    positions = jnp.arange(CAP)
    bounds = jnp.cumsum(lengths, axis=-1)
    segment = lax.optimization_barrier(jnp.sum((positions[None, None, :, None] >= bounds[:, :, None, :]).astype(jnp.int32), axis=-1))
    keep_rows = (segment < NSEG - 1).astype(jnp.float32)

    def to_balanced(given):
        return jax.vmap(lambda block_rows, destination: jnp.zeros_like(block_rows).at[destination].set(block_rows))(given, placement_ids)
    inputs = to_balanced(tokens.astype(jnp.float32)).reshape(MB * N_DP, CAP, MODEL_DIMENSION)
    grads_out = to_balanced(cotangent.astype(jnp.float32)).reshape(MB * N_DP, CAP, MODEL_DIMENSION)
    grads_out = grads_out * keep_rows.reshape(MB * N_DP, CAP, 1)
    segments = segment.reshape(MB * N_DP, CAP)

    def forward(params, all_rows):
        rounded_mats = low(params[0])
        rounded_norms = low(params[1])

        def one_block(operand_pair):
            return block_forward(rounded_mats, rounded_norms, params[2], operand_pair[0], operand_pair[1])
        return lax.map(jax.checkpoint(one_block), (all_rows, segments))
    params = (matrices, norm_vectors, head_vectors)
    outputs, pullback = jax.vjp(forward, params, inputs)
    param_grads, input_grads = pullback(grads_out)
    gradient_matrices, grad_norms, grad_heads = param_grads

    def to_given(balanced):
        balanced = balanced.reshape(MB, NROWS, MODEL_DIMENSION)
        return jax.vmap(lambda block_rows, destination: block_rows[destination])(balanced, placement_ids).astype(jnp.bfloat16)
    block_output = to_given(outputs)
    input_grad = to_given(input_grads)

    def refresh(block_index):
        gradient = gradient_matrices[:, block_index, :]
        slot_index = block_slot_index[block_index]
        left_new = stat_decay * left_stats[slot_index] + product(gradient, gradient.T)
        right_new = stat_decay * right_stats[slot_index] + product(gradient.T, gradient)
        direction = product(left_roots[slot_index], product(gradient, right_roots[slot_index]))
        factor = lax.rsqrt(jnp.mean(direction * direction) + mean_eps)
        return (left_new, right_new, matrices[:, block_index, :] - matrix_rate * factor * direction)
    lefts, rights, refreshed_weights = lax.map(refresh, jnp.arange(WEIGHT_BLOCKS))
    new_left = (stat_decay * left_stats).at[block_slot_index].set(lefts)
    new_right = (stat_decay * right_stats).at[block_slot_index].set(rights)
    updated_blocks = jnp.zeros((MODEL_DIMENSION, OPTIMIZER_SLOTS, MODEL_DIMENSION), jnp.float32).at[:, block_slot_index, :].set(jnp.moveaxis(refreshed_weights, 0, 1))
    slot_block_grads = jnp.zeros((MODEL_DIMENSION, OPTIMIZER_SLOTS, MODEL_DIMENSION), jnp.float32).at[:, block_slot_index, :].set(gradient_matrices)
    new_norm_state = stat_decay * norm_state + grad_norms * grad_norms
    new_norm_vectors = norm_vectors - vector_rate * grad_norms / (jnp.sqrt(new_norm_state) + diag_eps)
    new_head_state = stat_decay * head_state + grad_heads * grad_heads
    new_head_vectors = head_vectors - vector_rate * grad_heads / (jnp.sqrt(new_head_state) + diag_eps)
    return (block_output, input_grad, slot_block_grads, new_left, new_right, updated_blocks, grad_norms, new_norm_state, new_norm_vectors, grad_heads, new_head_state, new_head_vectors)
```

```python
import math

import jax
import jax.numpy as jnp
from jax import lax
from jax.sharding import PartitionSpec as P

HEAD_DIM = 64


stat_decay = 0.5
matrix_rate = 0.02
vector_rate = 0.3
norm_eps = 1e-05
mean_eps = 1e-06
diag_eps = 1e-08
masked_score = -1000000000.0

f32 = jnp.float32
low_type = jnp.bfloat16


def unit_rows_of(values):
    center = values - jnp.mean(values, axis=-1, keepdims=True)
    spread = jnp.mean(center * center, axis=-1, keepdims=True)
    scale_rows = lax.rsqrt(spread + norm_eps)
    return center * scale_rows, scale_rows


def layer_norm(values, gain, shift):
    unit_rows, _ = unit_rows_of(values)
    return unit_rows * gain + shift


def norm_back(values, gain, grad_normed):
    unit_rows, scale_rows = unit_rows_of(values)
    grad_unit = grad_normed * gain
    grad_values = scale_rows * (
        grad_unit
        - jnp.mean(grad_unit, axis=-1, keepdims=True)
        - unit_rows * jnp.mean(grad_unit * unit_rows, axis=-1, keepdims=True)
    )
    return (grad_values, grad_normed * unit_rows)


def dot(left, right):
    return lax.dot_general(left, right, (((1,), (0,)), ((), ())), preferred_element_type=f32)


def dot_nt(left, right):
    return lax.dot_general(left, right, (((1,), (1,)), ((), ())), preferred_element_type=f32)


def dot_tn(left, right):
    return lax.dot_general(left, right, (((0,), (0,)), ((), ())), preferred_element_type=f32)


def swap(values, axis, bit):
    count = lax.axis_size(axis)
    return lax.ppermute(values, axis, [(i, i ^ bit) for i in range(count)])


def gather_parts(share, axis):
    parts = {0: share}
    bit = lax.axis_size(axis) // 2
    while bit >= 1:
        parts.update({j | bit: swap(part, axis, bit) for j, part in list(parts.items())})
        bit //= 2
    return [parts[j] for j in range(len(parts))]


def gather_rows(share):
    return jnp.concatenate(gather_parts(share, "mp"), axis=0)


def scatter_rows(values):
    count = lax.axis_size("mp")
    own = values.shape[0] // count
    parts = {j: values[j * own : (j + 1) * own] for j in range(count)}
    bit = 1
    while bit < count:
        parts = {
            j: part + swap(parts[j ^ bit].astype(low_type), "mp", bit).astype(f32)
            for j, part in parts.items()
            if not j & bit
        }
        bit *= 2
    return parts[0]


def sum_over(values, axis):
    bit = 1
    while bit < lax.axis_size(axis):
        values = values + swap(values, axis, bit)
        bit *= 2
    return values


def gather_columns(share, axis):
    index = lax.axis_index(axis)
    bit = 1
    while bit < lax.axis_size(axis):
        other = swap(share, axis, bit)
        share = jnp.where(
            (index & bit) != 0,
            jnp.concatenate([other, share], axis=-1),
            jnp.concatenate([share, other], axis=-1),
        )
        bit *= 2
    return share


def exchange(rows):
    return lax.all_to_all(rows, "dp", split_axis=0, concat_axis=0, tiled=True)


def on_device(
    tokens,
    cotangent,
    lengths,
    placement_ids,
    block_slot_index,
    matrices,
    norm_vectors,
    head_vectors,
    left_stats,
    right_stats,
    left_roots,
    right_roots,
    norm_state,
    head_state,
):
    data_count = lax.axis_size("dp")
    data_index = lax.axis_index("dp")
    model_count = lax.axis_size("mp")
    model_index = lax.axis_index("mp")
    micro_count, rows_here, model_width = tokens.shape
    piece_rows = rows_here // data_count
    sub_rows = piece_rows // model_count
    own_rows = rows_here // model_count
    blocks = matrices.shape[1]
    local_cols = matrices.shape[2]
    shard_rows = matrices.shape[0]
    ffn_count = (blocks - 4) // 2
    ffn_cols = ffn_count * local_cols
    local_heads = local_cols // HEAD_DIM
    score_scale = 1.0 / math.sqrt(HEAD_DIM)

    matrices_low = matrices.astype(low_type)
    shipped_one = matrices_low[:, :4, :].reshape(shard_rows, 4 * local_cols)
    shipped_two = matrices_low[:, 4:, :].reshape(shard_rows, 2 * ffn_cols)
    norm_parts = jnp.stack(gather_parts(norm_vectors.astype(low_type), "dp"))
    norms = norm_parts[data_index ^ jnp.arange(data_count)]
    norms = jnp.swapaxes(norms, 0, 1).reshape(6, model_width).astype(f32)
    weights_one = lax.all_gather(shipped_one, "dp", axis=0, tiled=True)
    weights_two = lax.all_gather(shipped_two, "dp", axis=0, tiled=True)
    w_qkv = weights_one[:, : 3 * local_cols]
    w_out = weights_one[:, 3 * local_cols :]
    w_up = weights_two[:, :ffn_cols]
    w_down = weights_two[:, ffn_cols:]

    order = jnp.arange(rows_here)
    earlier = (order[:, None] < order[None, :]).astype(low_type)
    device_ids = jnp.arange(data_count)[:, None]
    slots_mine = []
    positions = []
    for micro in range(micro_count):
        dest_all = placement_ids[micro].reshape(data_count, rows_here)
        dest_mine = lax.dynamic_slice_in_dim(dest_all, data_index, 1, 0)
        target = dest_mine // rows_here
        to_each = target == device_ids
        to_me = (dest_all // rows_here) == data_index
        rank_both = dot(jnp.concatenate([to_each, to_me]).astype(low_type), earlier).astype(
            jnp.int32
        )
        rank_out = jnp.sum(jnp.where(to_each, rank_both[:data_count], 0), axis=0)
        slots_mine.append((rank_out, target[0]))
        rank_in = jnp.where(to_me, rank_both[data_count:], -1)
        place = jnp.sum(
            jnp.where(
                rank_in[:, None, :] == jnp.arange(piece_rows)[None, :, None],
                (dest_all - data_index * rows_here)[:, None, :],
                0,
            ),
            axis=2,
        )
        place = place.reshape(data_count, model_count, sub_rows).transpose(1, 0, 2)
        place = place.reshape(model_count, own_rows)[model_index ^ jnp.arange(model_count)]
        positions.append(place.reshape(rows_here))

    def send_rows(given, micro):
        rank, target = slots_mine[micro]
        wanted = jnp.arange(own_rows)
        here = (rank // sub_rows) == model_index
        slot = jnp.where(here, target * sub_rows + rank % sub_rows, -1)
        pick = (slot[None, :] == wanted[:, None]).astype(low_type)
        picked = dot(pick, given).astype(low_type)
        return exchange(picked.reshape(data_count, sub_rows, model_width)).reshape(
            own_rows, model_width
        )

    def return_rows(own, micro):
        rank, target = slots_mine[micro]
        slot = ((rank // sub_rows) ^ model_index) * own_rows + target * sub_rows + rank % sub_rows
        back = exchange(own.reshape(data_count, sub_rows, model_width))
        back = gather_rows(back.reshape(own_rows, model_width))
        pick = (slot[:, None] == order[None, :]).astype(low_type)
        return dot(pick, back).astype(low_type)

    micros = range(micro_count)
    rows_own = [send_rows(tokens[i], i).astype(f32) for i in micros]
    segments = []
    for i in micros:
        bounds = jnp.cumsum(lengths[i, 0])
        segments.append(
            jnp.sum((positions[i][:, None] >= bounds[None, :]).astype(jnp.int32), axis=1)
        )
    normed_one = [
        gather_rows(layer_norm(rows_own[i], norms[0], norms[1]).astype(low_type)) for i in micros
    ]
    keep = [
        (segments[i][:own_rows] < lengths.shape[2] - 1).astype(f32)[:, None] for i in micros
    ]
    grad_out_own = [send_rows(cotangent[i], i).astype(f32) * keep[i] for i in micros]
    grad_low = [gather_rows(grad_out_own[i].astype(low_type)) for i in micros]

    saved = []
    hidden_own = []
    for i in micros:
        qkv = dot(normed_one[i], w_qkv)
        queries = (qkv[:, :local_cols] + head_vectors[0]).astype(low_type)
        keys_all = qkv[:, local_cols : 2 * local_cols].astype(low_type)
        values = (qkv[:, 2 * local_cols :] + head_vectors[1]).astype(low_type)
        query_heads = queries.reshape(rows_here, local_heads, HEAD_DIM)
        key_heads = keys_all.reshape(rows_here, local_heads, HEAD_DIM)
        value_heads = values.reshape(rows_here, local_heads, HEAD_DIM)
        place, segment = positions[i], segments[i]
        allowed = (place[:, None] >= place[None, :]) & (segment[:, None] == segment[None, :])
        scores = (
            jnp.einsum("qhd,khd->hqk", query_heads, key_heads, preferred_element_type=f32)
            * score_scale
        )
        scores = jnp.where(allowed[None], scores, masked_score)
        attention = jax.nn.softmax(scores, axis=-1)
        attention_low = attention.astype(low_type)
        attended = jnp.einsum(
            "hqk,khd->qhd", attention_low, value_heads, preferred_element_type=f32
        )
        attended = attended.reshape(rows_here, local_cols).astype(low_type)
        branch = scatter_rows(dot_nt(attended, w_out))
        hidden_own.append(rows_own[i] + branch + norms[2])
        saved.append((query_heads, key_heads, value_heads, attention, attention_low, attended))

    normed_two = []
    active = []
    grad_up = []
    outputs_given = []
    grad_normed_two = []
    for i in micros:
        normed_two.append(
            gather_rows(layer_norm(hidden_own[i], norms[3], norms[4]).astype(low_type))
        )
        up_in = dot(normed_two[i], w_up) + head_vectors[2:].reshape(-1)
        active_full, gelu_pull = jax.vjp(lambda v: jax.nn.gelu(v, approximate=True), up_in)
        active.append(active_full.astype(low_type))
        grad_up.append(gelu_pull(dot(grad_low[i], w_down))[0].astype(low_type))
        grad_normed_two.append(scatter_rows(dot_nt(grad_up[i], w_up)))
        feed = scatter_rows(dot_nt(active[i], w_down))
        output_own = (hidden_own[i] + feed + norms[5]).astype(low_type)
        outputs_given.append(return_rows(output_own, i))

    up_grad = dot_tn(normed_two[0], grad_up[0])
    down_grad = dot_tn(grad_low[0], active[0])
    for i in micros[1:]:
        up_grad = up_grad + dot_tn(normed_two[i], grad_up[i])
        down_grad = down_grad + dot_tn(grad_low[i], active[i])
    summed_two = lax.psum_scatter(
        jnp.concatenate([up_grad, down_grad], axis=1).astype(low_type),
        "dp",
        scatter_dimension=0,
        tiled=True,
    )

    inputs_given = []
    grad_qkv = []
    grad_hidden_low = []
    norm_grads_own = 0.0
    for i in micros:
        query_heads, key_heads, value_heads, attention, attention_low, attended = saved[i]
        hidden_part, gain_two_rows = norm_back(hidden_own[i], norms[3], grad_normed_two[i])
        grad_hidden = grad_out_own[i] + hidden_part
        grad_hidden_low.append(gather_rows(grad_hidden.astype(low_type)))
        grad_attended = dot(grad_hidden_low[i], w_out).astype(low_type)
        grad_attended = grad_attended.reshape(rows_here, local_heads, HEAD_DIM)
        grad_attention = jnp.einsum(
            "qhd,khd->hqk", grad_attended, value_heads, preferred_element_type=f32
        )
        row_total = jnp.sum(grad_attention * attention, axis=-1, keepdims=True)
        grad_scores = (attention * (grad_attention - row_total)).astype(low_type)
        grad_values = jnp.einsum(
            "hqk,qhd->khd", attention_low, grad_attended, preferred_element_type=f32
        ).astype(low_type)
        grad_queries = (
            jnp.einsum("hqk,khd->qhd", grad_scores, key_heads, preferred_element_type=f32)
            * score_scale
        ).astype(low_type)
        grad_keys = (
            jnp.einsum("hqk,qhd->khd", grad_scores, query_heads, preferred_element_type=f32)
            * score_scale
        ).astype(low_type)
        grad_qkv.append(
            jnp.concatenate(
                [
                    grad_queries.reshape(rows_here, local_cols),
                    grad_keys.reshape(rows_here, local_cols),
                    grad_values.reshape(rows_here, local_cols),
                ],
                axis=1,
            )
        )
        grad_normed_one = scatter_rows(dot_nt(grad_qkv[i], w_qkv))
        rows_part, gain_one_rows = norm_back(rows_own[i], norms[0], grad_normed_one)
        grad_input = (grad_hidden + rows_part).astype(low_type)
        norm_grads_own = norm_grads_own + jnp.stack(
            [
                jnp.sum(gain_one_rows, axis=0),
                jnp.sum(grad_normed_one, axis=0),
                jnp.sum(grad_hidden, axis=0),
                jnp.sum(gain_two_rows, axis=0),
                jnp.sum(grad_normed_two[i], axis=0),
                jnp.sum(grad_out_own[i], axis=0),
            ]
        )
        inputs_given.append(return_rows(grad_input, i))

    qkv_grad = dot_tn(normed_one[0], grad_qkv[0])
    out_grad = dot_tn(grad_hidden_low[0], saved[0][5])
    for i in micros[1:]:
        qkv_grad = qkv_grad + dot_tn(normed_one[i], grad_qkv[i])
        out_grad = out_grad + dot_tn(grad_hidden_low[i], saved[i][5])
    summed_one = lax.psum_scatter(
        jnp.concatenate([qkv_grad, out_grad], axis=1).astype(low_type),
        "dp",
        scatter_dimension=0,
        tiled=True,
    )

    head_own = 0.0
    for i in micros:
        head_own = head_own + jnp.concatenate(
            [
                jnp.sum(grad_qkv[i][:, :local_cols].astype(f32), axis=0)[None],
                jnp.sum(grad_qkv[i][:, 2 * local_cols :].astype(f32), axis=0)[None],
                jnp.sum(grad_up[i].astype(f32), axis=0).reshape(ffn_count, local_cols),
            ],
            axis=0,
        )
    head_total = sum_over(head_own, "dp")
    norm_all = sum_over(sum_over(norm_grads_own, "mp"), "dp")
    norm_cols = norm_vectors.shape[1]
    norm_total = lax.dynamic_slice_in_dim(norm_all, data_index * norm_cols, norm_cols, 1)

    slot_count = left_stats.shape[0]
    all_slots = slot_count * data_count
    slot_match = block_slot_index[None, :] == jnp.arange(all_slots)[:, None]
    filled = jnp.any(slot_match, axis=1)
    block_of = jnp.sum(jnp.where(slot_match, jnp.arange(blocks)[None, :], 0), axis=1)
    summed = jnp.concatenate([summed_one, summed_two], axis=1)
    summed = jnp.swapaxes(summed.reshape(shard_rows, blocks, local_cols), 0, 1)
    slotted = jnp.where(filled[:, None, None], summed[block_of], 0.0).astype(low_type)
    owned = exchange(slotted.reshape(data_count, slot_count * shard_rows, local_cols))
    owned = owned.reshape(data_count, slot_count, shard_rows, local_cols)
    owned = jnp.swapaxes(owned, 0, 1).reshape(slot_count, model_width, local_cols)
    whole = gather_columns(owned, "mp")
    slot_match_own = lax.dynamic_slice_in_dim(slot_match, data_index * slot_count, slot_count, 0)
    weights_all = jnp.concatenate([weights_one, weights_two], axis=1)

    row_total_count = left_stats.shape[1]
    lefts, rights, directions, squares, owned_weights = [], [], [], [], []
    for s in range(slot_count):
        grads = whole[s]
        my_rows = lax.dynamic_slice_in_dim(
            grads, model_index * row_total_count, row_total_count, 0
        )
        lefts.append(stat_decay * left_stats[s] + dot_nt(my_rows, grads))
        rights.append(stat_decay * right_stats[s] + dot_tn(owned[s], grads))
        halfway = dot_nt(grads, right_roots[s].astype(low_type))
        direction = dot(left_roots[s].astype(low_type), halfway.astype(low_type))
        directions.append(direction)
        squares.append(jnp.sum(direction * direction))
        chosen = 0.0
        for b in range(blocks):
            chosen = chosen + jnp.where(
                slot_match_own[s, b],
                weights_all[:, b * local_cols : (b + 1) * local_cols].astype(f32),
                0.0,
            )
        owned_weights.append(chosen)
    square_total = sum_over(jnp.stack(squares).reshape(1, slot_count), "mp")[0]
    factor = lax.rsqrt(square_total / (model_width * model_width) + mean_eps)
    updated_blocks = jnp.stack(
        [
            owned_weights[s] - matrix_rate * factor[s] * directions[s]
            for s in range(slot_count)
        ],
        axis=1,
    )
    owned_grads = jnp.swapaxes(owned, 0, 1).astype(f32)
    new_norm_state = stat_decay * norm_state + norm_total * norm_total
    new_norm_vectors = norm_vectors - vector_rate * norm_total / (
        jnp.sqrt(new_norm_state) + diag_eps
    )
    new_head_state = stat_decay * head_state + head_total * head_total
    new_head_vectors = head_vectors - vector_rate * head_total / (
        jnp.sqrt(new_head_state) + diag_eps
    )
    return (
        jnp.stack(outputs_given),
        jnp.stack(inputs_given),
        owned_grads,
        jnp.stack(lefts),
        jnp.stack(rights),
        updated_blocks,
        norm_total,
        new_norm_state,
        new_norm_vectors,
        head_total,
        new_head_state,
        new_head_vectors,
    )


def solution(mesh):
    placed = (
        P(None, "dp", None),
        P(None, "dp", None),
        P(None, "dp", None),
        P(),
        P(),
        P("dp", None, "mp"),
        P(None, "dp"),
        P(None, "mp"),
        P("dp", "mp", None),
        P("dp", "mp", None),
        P("dp", None, None),
        P("dp", "mp", None),
        P(None, "dp"),
        P(None, "mp"),
    )
    return jax.shard_map(
        on_device,
        mesh=mesh,
        in_specs=placed,
        out_specs=(
            P(None, "dp", None),
            P(None, "dp", None),
            P(None, "dp", "mp"),
            P("dp", "mp", None),
            P("dp", "mp", None),
            P(None, "dp", "mp"),
            P(None, "dp"),
            P(None, "dp"),
            P(None, "dp"),
            P(None, "mp"),
            P(None, "mp"),
            P(None, "mp"),
        ),
        check_vma=False,
    )
```

```python
import functools
import math

import jax
import jax.numpy as jnp
from jax import lax
from jax.experimental import pallas as pl
from jax.experimental.pallas import tpu as pltpu
from jax.sharding import PartitionSpec as P

HEAD_DIM = 64


stat_decay = 0.5
matrix_rate = 0.02
vector_rate = 0.3
norm_eps = 1e-05
mean_eps = 1e-06
diag_eps = 1e-08
masked_score = -1000000000.0

f32 = jnp.float32
low_type = jnp.bfloat16


def unit_rows_of(values):
    center = values - jnp.mean(values, axis=-1, keepdims=True)
    spread = jnp.mean(center * center, axis=-1, keepdims=True)
    scale_rows = lax.rsqrt(spread + norm_eps)
    return center * scale_rows, scale_rows


def layer_norm(values, gain, shift):
    unit_rows, _ = unit_rows_of(values)
    return unit_rows * gain + shift


def norm_back(values, gain, grad_normed):
    unit_rows, scale_rows = unit_rows_of(values)
    grad_unit = grad_normed * gain
    grad_values = scale_rows * (
        grad_unit
        - jnp.mean(grad_unit, axis=-1, keepdims=True)
        - unit_rows * jnp.mean(grad_unit * unit_rows, axis=-1, keepdims=True)
    )
    return (grad_values, grad_normed * unit_rows)


def dot(left, right):
    return lax.dot_general(left, right, (((1,), (0,)), ((), ())), preferred_element_type=f32)


def dot_nt(left, right):
    return lax.dot_general(left, right, (((1,), (1,)), ((), ())), preferred_element_type=f32)


def dot_tn(left, right):
    return lax.dot_general(left, right, (((0,), (0,)), ((), ())), preferred_element_type=f32)


TILE = 256
STRIP = 64
VMEM_BYTES = 56 * 1024 * 1024
SMALL = pl.CostEstimate(flops=10**9, bytes_accessed=10**6, transcendentals=0)
LARGE = pl.CostEstimate(flops=20 * 10**9, bytes_accessed=10**6, transcendentals=0)
MEDIUM = pl.CostEstimate(flops=11 * 10**9, bytes_accessed=10**6, transcendentals=0)

def whole_spec():
    return pl.BlockSpec(memory_space=pltpu.VMEM)

def attention_forward_kernel(
    near_ref, far_ref, norm_ref, weights_ref, bias_ref,
    place_row_ref, place_col_ref, seg_row_ref, seg_col_ref,
    keep_ref, send_ref, normed_ref, attended_ref, qkv_ref, out_ref, lse_ref,
    arrived,
):
    rows = arrived.shape[0]
    half = rows // 2
    cols = attended_ref.shape[1]
    heads = cols // HEAD_DIM
    scale = 1.0 / math.sqrt(HEAD_DIM)
    tiles = rows // TILE
    for start, source in ((0, near_ref), (half, far_ref)):

        def norm_some(i, carry):
            values = source[pl.ds(pl.multiple_of(i * STRIP, STRIP), STRIP), :].astype(f32)
            normed = layer_norm(values, norm_ref[0:1, :], norm_ref[1:2, :])
            normed_ref[pl.ds(pl.multiple_of(start + i * STRIP, STRIP), STRIP), :] = (
                normed.astype(low_type)
            )
            return carry

        lax.fori_loop(0, half // STRIP, norm_some, 0)
    for t in range(tiles):
        part = normed_ref[pl.ds(t * TILE, TILE), :]
        arrived[pl.ds(t * TILE, TILE), :] = (
            dot(part, weights_ref[:, : 3 * cols]) + bias_ref[...]
        ).astype(low_type)
    for t in range(tiles):
        wanted = lax.broadcasted_iota(jnp.int32, (TILE, rows), 0) + t * TILE
        pick = jnp.where(wanted == place_row_ref[...], 1.0, 0.0).astype(low_type)
        qkv_ref[pl.ds(t * TILE, TILE), :] = dot(pick, arrived[...]).astype(low_type)
    for h in range(heads):
        lanes = slice(h * HEAD_DIM, (h + 1) * HEAD_DIM)
        key_lanes = slice(cols + h * HEAD_DIM, cols + (h + 1) * HEAD_DIM)
        value_lanes = slice(2 * cols + h * HEAD_DIM, 2 * cols + (h + 1) * HEAD_DIM)
        for t in range(tiles):
            here = slice(t * TILE, (t + 1) * TILE)
            query = qkv_ref[here, lanes]
            seg_q = seg_col_ref[here, :]
            scores = []
            top = None
            for c in range(t + 1):
                there = slice(c * TILE, (c + 1) * TILE)
                s = dot_nt(query, qkv_ref[there, key_lanes]) * scale
                allowed = seg_q == seg_row_ref[:, there]
                if c == t:
                    allowed = allowed & (
                        lax.broadcasted_iota(jnp.int32, (TILE, TILE), 0)
                        >= lax.broadcasted_iota(jnp.int32, (TILE, TILE), 1)
                    )
                s = jnp.where(allowed, s, masked_score)
                scores.append(s)
                m = jnp.max(s, axis=1, keepdims=True)
                top = m if top is None else jnp.maximum(top, m)
            total = 0.0
            out = 0.0
            for c in range(t + 1):
                there = slice(c * TILE, (c + 1) * TILE)
                e = jnp.exp(scores[c] - top)
                total = total + jnp.sum(e, axis=1, keepdims=True)
                out = out + dot(e.astype(low_type), qkv_ref[there, value_lanes])
            out_ref[here, lanes] = (out / total).astype(low_type)
            lse_ref[here, h : h + 1] = top + jnp.log(total)
    for t in range(tiles):
        wanted = lax.broadcasted_iota(jnp.int32, (TILE, rows), 1)
        pick = jnp.where(wanted == place_col_ref[pl.ds(t * TILE, TILE), :], 1.0, 0.0).astype(low_type)
        part = dot(pick, out_ref[...]).astype(low_type)
        attended_ref[pl.ds(t * TILE, TILE), :] = part
        branch = dot_nt(part, weights_ref[:, 3 * cols :])
        if t * TILE < half:
            keep_ref[pl.ds(t * TILE, TILE), :] = branch
        else:
            send_ref[pl.ds(t * TILE - half, TILE), :] = branch.astype(low_type)

def attention_forward(near, far, norms, weights, bias, place, segment):
    rows = 2 * near.shape[0]
    width = near.shape[1]
    cols = weights.shape[1] // 4
    heads = cols // HEAD_DIM
    shape = jax.ShapeDtypeStruct
    return pl.pallas_call(
        attention_forward_kernel,
        out_shape=(
            shape((rows // 2, width), f32),
            shape((rows // 2, width), low_type),
            shape((rows, width), low_type),
            shape((rows, cols), low_type),
            shape((rows, 3 * cols), low_type),
            shape((rows, cols), low_type),
            shape((rows, heads), f32),
        ),
        in_specs=[whole_spec()] * 9,
        out_specs=tuple([whole_spec()] * 7),
        scratch_shapes=[pltpu.VMEM((rows, 3 * cols), low_type)],
        compiler_params=pltpu.CompilerParams(vmem_limit_bytes=VMEM_BYTES),
        cost_estimate=LARGE,
    )(near, far, norms, weights, bias, place[None, :], place[:, None], segment[None, :], segment[:, None])

def attention_backward_kernel(
    near_ref, far_ref, weights_ref, place_row_ref, place_col_ref, seg_row_ref, seg_col_ref,
    qkv_ref, out_ref, lse_ref,
    keep_ref, send_ref, grads_ref, sums_ref,
    arrived, placed, grad_key, grad_value, moved,
):
    rows = arrived.shape[0]
    half = rows // 2
    cols = out_ref.shape[1]
    heads = cols // HEAD_DIM
    scale = 1.0 / math.sqrt(HEAD_DIM)
    tiles = rows // TILE
    for t in range(tiles):
        source = near_ref if t * TILE < half else far_ref
        part = source[pl.ds(t * TILE % half, TILE), :]
        arrived[pl.ds(t * TILE, TILE), :] = dot(part, weights_ref[:, 3 * cols :]).astype(low_type)
    for t in range(tiles):
        wanted = lax.broadcasted_iota(jnp.int32, (TILE, rows), 0) + t * TILE
        pick = jnp.where(wanted == place_row_ref[...], 1.0, 0.0).astype(low_type)
        placed[pl.ds(t * TILE, TILE), :] = dot(pick, arrived[...]).astype(low_type)
    for h in range(heads):
        lanes = slice(h * HEAD_DIM, (h + 1) * HEAD_DIM)
        key_lanes = slice(cols + h * HEAD_DIM, cols + (h + 1) * HEAD_DIM)
        value_lanes = slice(2 * cols + h * HEAD_DIM, 2 * cols + (h + 1) * HEAD_DIM)
        grad_key[...] = jnp.zeros_like(grad_key)
        grad_value[...] = jnp.zeros_like(grad_value)
        for t in range(tiles):
            here = slice(t * TILE, (t + 1) * TILE)
            query = qkv_ref[here, lanes]
            grad = placed[here, lanes]
            row_total = jnp.sum(grad.astype(f32) * out_ref[here, lanes].astype(f32), axis=1, keepdims=True)
            seg_q = seg_col_ref[here, :]
            lse = lse_ref[here, h : h + 1]
            grad_query = 0.0
            for c in range(t + 1):
                there = slice(c * TILE, (c + 1) * TILE)
                key = qkv_ref[there, key_lanes]
                s = dot_nt(query, key) * scale
                allowed = seg_q == seg_row_ref[:, there]
                if c == t:
                    allowed = allowed & (
                        lax.broadcasted_iota(jnp.int32, (TILE, TILE), 0)
                        >= lax.broadcasted_iota(jnp.int32, (TILE, TILE), 1)
                    )
                p = jnp.where(allowed, jnp.exp(s - lse), 0.0)
                dp = dot_nt(grad, qkv_ref[there, value_lanes])
                ds = (p * (dp - row_total)).astype(low_type)
                grad_query = grad_query + dot(ds, key)
                grad_key[there, :] += dot_tn(ds, query)
                grad_value[there, :] += dot_tn(p.astype(low_type), grad)
            moved[here, lanes] = (grad_query * scale).astype(low_type)
        moved[:, key_lanes] = (grad_key[...] * scale).astype(low_type)
        moved[:, value_lanes] = grad_value[...].astype(low_type)
    sums_ref[...] = jnp.sum(moved[...].astype(f32), axis=0, keepdims=True)
    for t in range(tiles):
        wanted = lax.broadcasted_iota(jnp.int32, (TILE, rows), 1)
        pick = jnp.where(wanted == place_col_ref[pl.ds(t * TILE, TILE), :], 1.0, 0.0).astype(low_type)
        part = dot(pick, moved[...]).astype(low_type)
        grads_ref[pl.ds(t * TILE, TILE), :] = part
        normed = dot_nt(part, weights_ref[:, : 3 * cols])
        if t * TILE < half:
            keep_ref[pl.ds(t * TILE, TILE), :] = normed
        else:
            send_ref[pl.ds(t * TILE - half, TILE), :] = normed.astype(low_type)

def attention_backward(near, far, weights, place, segment, qkv, out, lse):
    rows = 2 * near.shape[0]
    width = near.shape[1]
    cols = weights.shape[1] // 4
    heads = cols // HEAD_DIM
    shape = jax.ShapeDtypeStruct
    return pl.pallas_call(
        attention_backward_kernel,
        out_shape=(
            shape((rows // 2, width), f32),
            shape((rows // 2, width), low_type),
            shape((rows, 3 * cols), low_type),
            shape((1, 3 * cols), f32),
        ),
        in_specs=[whole_spec()] * 10,
        out_specs=tuple([whole_spec()] * 4),
        scratch_shapes=[
            pltpu.VMEM((rows, cols), low_type),
            pltpu.VMEM((rows, cols), low_type),
            pltpu.VMEM((rows, HEAD_DIM), f32),
            pltpu.VMEM((rows, HEAD_DIM), f32),
            pltpu.VMEM((rows, 3 * cols), low_type),
        ],
        compiler_params=pltpu.CompilerParams(vmem_limit_bytes=VMEM_BYTES),
        cost_estimate=LARGE,
    )(near, far, weights, place[None, :], place[:, None], segment[None, :], segment[:, None], qkv, out, lse)

def mlp_kernel(normed_ref, grad_ref, weights_ref, bias_ref, active_ref, grad_up_ref, feed_ref, back_ref, sums_ref):
    rows, width = normed_ref.shape
    cols = bias_ref.shape[1]
    step = TILE
    total = 0.0
    c0 = math.sqrt(2.0 / math.pi)
    for t in range(rows // step):
        here = slice(t * step, (t + 1) * step)
        pre = dot(normed_ref[here, :], weights_ref[:, :cols]) + bias_ref[...]
        square = pre * pre
        bent = jnp.tanh(c0 * (pre + 0.044715 * (square * pre)))
        active_ref[here, :] = (0.5 * pre * (1.0 + bent)).astype(low_type)
        slope = 0.5 * (1.0 + bent) + 0.5 * pre * (1.0 - bent * bent) * (c0 * (1.0 + 0.134145 * square))
        grad = dot(grad_ref[here, :], weights_ref[:, cols:]) * slope
        grad_low = grad.astype(low_type)
        grad_up_ref[here, :] = grad_low
        total = total + jnp.sum(grad_low.astype(f32), axis=0, keepdims=True)
    sums_ref[...] = total
    for t in range(rows // step):
        here = slice(t * step, (t + 1) * step)
        back_ref[here, :] = dot_nt(grad_up_ref[here, :], weights_ref[:, :cols]).astype(back_ref.dtype)
        feed_ref[here, :] = dot_nt(active_ref[here, :], weights_ref[:, cols:]).astype(feed_ref.dtype)

def mlp(normed, grad, weights, bias, kind):
    rows, width = normed.shape
    cols = bias.shape[1]
    shape = jax.ShapeDtypeStruct
    return pl.pallas_call(
        mlp_kernel,
        out_shape=(
            shape((rows, cols), low_type),
            shape((rows, cols), low_type),
            shape((rows, width), kind),
            shape((rows, width), kind),
            shape((1, cols), f32),
        ),
        in_specs=[whole_spec()] * 4,
        out_specs=tuple([whole_spec()] * 5),
        compiler_params=pltpu.CompilerParams(vmem_limit_bytes=VMEM_BYTES),
        cost_estimate=MEDIUM,
    )(normed, grad, weights, bias)


def grads_kernel(counts, *refs):
    out_ref = refs[-1]
    for t in range(out_ref.shape[0] // TILE):
        rows = slice(t * TILE, (t + 1) * TILE)
        start = 0
        place = 0
        for count in counts:
            total = 0.0
            for g in range(count):
                left, right = refs[place + g], refs[place + count + g]
                total = total + dot_tn(left[:, rows], right[...])
            out_ref[rows, start : start + total.shape[1]] = total.astype(out_ref.dtype)
            start = start + total.shape[1]
            place = place + 2 * count


def grads_of(*groups):
    width = groups[0][0][0].shape[1]
    cols = sum(right[0].shape[1] for _, right in groups)
    pieces = [piece for left, right in groups for piece in (*left, *right)]
    return pl.pallas_call(
        functools.partial(grads_kernel, [len(left) for left, _ in groups]),
        out_shape=jax.ShapeDtypeStruct((width, cols), low_type),
        in_specs=[whole_spec()] * len(pieces),
        out_specs=whole_spec(),
        compiler_params=pltpu.CompilerParams(vmem_limit_bytes=VMEM_BYTES),
        cost_estimate=MEDIUM,
    )(*pieces)


def slots_kernel(cols, slot_count, block_ref, *refs):
    outs, held = refs[-1 - slot_count : -1], refs[-1]
    start = 0
    for part in refs[: -1 - slot_count]:
        held[:, start : start + part.shape[1]] = part[...]
        start = start + part.shape[1]
    for s in range(block_ref.shape[0]):
        out = outs[s % slot_count]
        block = block_ref[s]
        lanes = pl.ds(pl.multiple_of(jnp.maximum(block, 0) * cols, cols), cols)
        rows = held[:, lanes]
        out[s // slot_count] = jnp.where(block >= 0, rows, jnp.zeros_like(rows))


def to_slots(block_of, slot_count, cols, *parts):
    count = block_of.shape[0] // slot_count
    rows = parts[0].shape[0]
    width = sum(part.shape[1] for part in parts)
    return pl.pallas_call(
        functools.partial(slots_kernel, cols, slot_count),
        out_shape=tuple(
            [jax.ShapeDtypeStruct((count, rows, cols), low_type) for _ in range(slot_count)]
        ),
        in_specs=[pl.BlockSpec(memory_space=pltpu.SMEM)] + [whole_spec()] * len(parts),
        out_specs=tuple([whole_spec()] * slot_count),
        scratch_shapes=[pltpu.VMEM((rows, width), low_type)],
        compiler_params=pltpu.CompilerParams(vmem_limit_bytes=VMEM_BYTES),
        cost_estimate=SMALL,
    )(block_of, *parts)


def swap(values, axis, bit):
    count = lax.axis_size(axis)
    return lax.ppermute(values, axis, [(i, i ^ bit) for i in range(count)])


def near_order(count):
    found = [0]
    bit = count // 2
    while bit >= 1:
        found = found + [j ^ bit for j in found]
        bit //= 2
    return found


def gather_chips(share):
    bit = lax.axis_size("mp") // 2
    while bit > 1:
        share = jnp.concatenate([share, swap(share, "mp", bit)], axis=0)
        bit //= 2
    return share


def other_core(values):
    return swap(values, "mp", 1)


def scatter_chips(keep, received):
    values = keep + received.astype(f32)
    bit = 2
    while bit < lax.axis_size("mp"):
        half = values.shape[0] // 2
        values = values[:half] + swap(values[half:].astype(low_type), "mp", bit).astype(f32)
        bit *= 2
    return values


def after(values, others):
    return lax.optimization_barrier((values, others))


def together(*values):
    return lax.optimization_barrier(values)


def scatter_grads(values):
    count = lax.axis_size("dp")
    index = lax.axis_index("dp")
    blocks = values.reshape(count, -1, values.shape[-1])
    bit = 1
    width = count
    while bit < count:
        blocks = blocks.reshape(width // 2, 2, -1, values.shape[-1])
        mine = lax.dynamic_index_in_dim(blocks, index // bit % 2, 1, keepdims=False)
        other = lax.dynamic_index_in_dim(blocks, 1 - index // bit % 2, 1, keepdims=False)
        blocks = mine.astype(f32) + swap(other.astype(low_type), "dp", bit).astype(f32)
        bit *= 2
        width //= 2
    return blocks.reshape(-1, values.shape[-1])


def sum_over(values, axis):
    bit = 1
    while bit < lax.axis_size(axis):
        values = values + swap(values, axis, bit)
        bit *= 2
    return values


def gather_columns(share, axis):
    index = lax.axis_index(axis)
    bit = 1
    while bit < lax.axis_size(axis):
        other = swap(share, axis, bit)
        share = jnp.where(
            (index & bit) != 0,
            jnp.concatenate([other, share], axis=-1),
            jnp.concatenate([share, other], axis=-1),
        )
        bit *= 2
    return share


def exchange(rows):
    return lax.all_to_all(rows, "dp", split_axis=0, concat_axis=0, tiled=True)


def on_device(
    tokens,
    cotangent,
    lengths,
    placement_ids,
    block_slot_index,
    matrices,
    norm_vectors,
    head_vectors,
    left_stats,
    right_stats,
    left_roots,
    right_roots,
    norm_state,
    head_state,
):
    data_count = lax.axis_size("dp")
    data_index = lax.axis_index("dp")
    model_count = lax.axis_size("mp")
    model_index = lax.axis_index("mp")
    micro_count, rows_here, model_width = tokens.shape
    piece_rows = rows_here // data_count
    sub_rows = piece_rows // model_count
    own_rows = rows_here // model_count
    blocks = matrices.shape[1]
    local_cols = matrices.shape[2]
    shard_rows = matrices.shape[0]
    ffn_count = (blocks - 4) // 2
    ffn_cols = ffn_count * local_cols

    matrices_low = matrices.astype(low_type)
    shipped_one = matrices_low[:, :4, :].reshape(shard_rows, 4 * local_cols)
    shipped_two = matrices_low[:, 4:, :].reshape(shard_rows, 2 * ffn_cols)
    lanes = 128
    norm_columns = jnp.swapaxes(norm_vectors.astype(low_type), 0, 1)
    shipped_one = jnp.concatenate(
        [shipped_one, jnp.pad(norm_columns, ((0, 0), (0, lanes - norm_columns.shape[1])))], axis=1
    )
    gathered = lax.all_gather(shipped_one, "dp", axis=0, tiled=True)
    order = jnp.arange(rows_here)
    earlier = (order[:, None] < order[None, :]).astype(low_type)
    device_ids = jnp.arange(data_count)[:, None]
    near = near_order(model_count)
    slots_mine = []
    positions = []
    for micro in range(micro_count):
        dest_all = placement_ids[micro].reshape(data_count, rows_here)
        dest_mine = lax.dynamic_slice_in_dim(dest_all, data_index, 1, 0)
        target = dest_mine // rows_here
        to_each = target == device_ids
        to_me = (dest_all // rows_here) == data_index
        rank_both = dot(jnp.concatenate([to_each, to_me]).astype(low_type), earlier).astype(
            jnp.int32
        )
        rank_out = jnp.sum(jnp.where(to_each, rank_both[:data_count], 0), axis=0)
        slots_mine.append((rank_out, target[0]))
        rank_in = jnp.where(to_me, rank_both[data_count:], -1)
        place = jnp.sum(
            jnp.where(
                rank_in[:, None, :] == jnp.arange(piece_rows)[None, :, None],
                (dest_all - data_index * rows_here)[:, None, :],
                0,
            ),
            axis=2,
        )
        place = place.reshape(data_count, model_count, sub_rows).transpose(1, 0, 2)
        place = place.reshape(model_count, own_rows)[model_index ^ jnp.array(near)]
        positions.append(place.reshape(rows_here))

    def send_rows(micro, *given):
        rank, target = slots_mine[micro]
        here = (rank // sub_rows) == model_index
        slot = jnp.where(here, target * sub_rows + rank % sub_rows, -1)
        pick = (slot[None, :] == jnp.arange(own_rows)[:, None]).astype(low_type)
        picked = [dot(pick, rows[micro]).astype(low_type) for rows in given]
        picked = [rows.reshape(data_count, sub_rows, model_width) for rows in picked]
        got = exchange(jnp.concatenate(picked, axis=1))
        got = got.reshape(data_count, len(given), sub_rows, model_width)
        return [got[:, i].reshape(own_rows, model_width).astype(f32) for i in range(len(given))]

    def exchange_back(own):
        sent = [rows.reshape(data_count, sub_rows, model_width) for rows in own]
        return exchange(jnp.concatenate(sent, axis=1))

    def return_rows(back, which):
        back = back.reshape(data_count, len(which), sub_rows, model_width)
        back = jnp.swapaxes(back, 0, 1).reshape(1, len(which) * own_rows, model_width)
        bit = model_count // 2
        while bit >= 1:
            back = jnp.concatenate([back, swap(back, "mp", bit)], axis=0)
            bit //= 2
        returned = []
        for i, micro in enumerate(which):
            rank, target = slots_mine[micro]
            block = jnp.sum(
                jnp.where(
                    ((rank // sub_rows) ^ model_index) == jnp.array(near)[:, None],
                    jnp.arange(model_count)[:, None],
                    0,
                ),
                axis=0,
            )
            slot = block * own_rows + target * sub_rows + rank % sub_rows
            pick = (slot[:, None] == order[None, :]).astype(low_type)
            rows = back[:, i * own_rows : (i + 1) * own_rows]
            returned.append(dot(pick, rows.reshape(rows_here, model_width)).astype(low_type))
        return jnp.stack(returned)

    micros = range(micro_count)
    bounds = [jnp.cumsum(lengths[i, 0]) for i in micros]
    segments = [
        jnp.sum((order[:, None] >= bounds[i][None, :]).astype(jnp.int32), axis=1) for i in micros
    ]
    bias_qkv = jnp.concatenate(
        [head_vectors[0], jnp.zeros((local_cols,), f32), head_vectors[1]]
    )[None]
    bias_up = head_vectors[2:].reshape(1, -1)
    half = rows_here // 2

    def arrived(i):
        rows, grads = send_rows(i, tokens, cotangent)
        keep = (positions[i][:own_rows] < bounds[i][-2]).astype(f32)[:, None]
        return rows, grads * keep

    def attend(i, near, far):
        return attention_forward(
            near, far, norms[:2], weights_one, bias_qkv, positions[i], segments[i]
        )

    def second_share(hidden):
        return layer_norm(hidden, norms[3], norms[4]).astype(low_type)

    def feed_forward(near, far, grad_near, grad_far):
        far_parts = mlp(far, grad_far, weights_two, bias_up, low_type)
        near_parts = mlp(near, grad_near, weights_two, bias_up, f32)
        active, grad_up, (feed_keep, feed_send), (back_keep, back_send), sums = zip(
            near_parts, far_parts
        )
        return active, grad_up, feed_keep, feed_send, back_keep, back_send, sum(sums)

    def second_back(i, hidden, grad_normed):
        hidden_part, gain_rows = norm_back(hidden, norms[3], grad_normed)
        grad_hidden = grad_out[i] + hidden_part
        sums = [
            jnp.sum(grad_hidden, axis=0),
            jnp.sum(gain_rows, axis=0),
            jnp.sum(grad_normed, axis=0),
            jnp.sum(grad_out[i], axis=0),
        ]
        return grad_hidden, grad_hidden.astype(low_type), jnp.stack(sums)

    def attend_back(i, near, far, kept):
        _, qkv, out, lse = kept
        return attention_backward(
            near, far, weights_one, positions[i], segments[i], qkv, out, lse
        )

    def first_back(i, grad_hidden, grad_normed):
        rows_part, gain_rows = norm_back(rows_own[i], norms[0], grad_normed)
        sums = [jnp.sum(gain_rows, axis=0), jnp.sum(grad_normed, axis=0)]
        return (grad_hidden + rows_part).astype(low_type), jnp.stack(sums)

    rows_0, grad_0 = arrived(0)
    rows_1, grad_1 = arrived(1)
    x_0 = gather_chips(rows_0.astype(low_type))
    g_0 = gather_chips(grad_0.astype(low_type))
    x_0, g_0, rows_1, grad_1 = together(x_0, g_0, rows_1, grad_1)
    rows_own = (rows_0, rows_1)
    grad_out = (grad_0, grad_1)
    xf_0, gf_0, gathered, shipped_two = together(
        other_core(x_0), other_core(g_0), gathered, shipped_two
    )
    weights_one = gathered[:, : 4 * local_cols]
    norms = jnp.swapaxes(gathered[:, 4 * local_cols :], 0, 1)[:6].astype(f32)
    weights_two = lax.all_gather(shipped_two, "dp", axis=0, tiled=True)

    keep_0, send_0, normed_0, *kept_0 = attend(0, x_0, xf_0)
    x_1 = gather_chips(rows_1.astype(low_type))
    g_1 = gather_chips(grad_1.astype(low_type))
    keep_0, send_0, x_1, g_1 = together(keep_0, send_0, x_1, g_1)
    core_0, xf_1 = together(other_core(send_0), other_core(x_1))
    keep_1, send_1, normed_1, *kept_1 = attend(1, x_1, xf_1)
    branch_0 = scatter_chips(keep_0, core_0)
    keep_1, send_1, branch_0, g_1 = together(keep_1, send_1, branch_0, g_1)
    core_1 = other_core(send_1)
    gf_1 = other_core(g_1)
    hidden_0 = rows_0 + branch_0 + norms[2]
    z_0 = second_share(hidden_0)
    z_0, core_1, gf_1 = together(z_0, core_1, gf_1)
    branch_1 = scatter_chips(keep_1, core_1)
    z_0 = gather_chips(z_0)
    z_0, branch_1 = together(z_0, branch_1)
    hidden_1 = rows_1 + branch_1 + norms[2]
    z_1, zf_0, weights_two = together(second_share(hidden_1), other_core(z_0), weights_two)

    active_0, grad_up_0, feed_keep_0, feed_0, keep_0, send_0, up_sums_0 = feed_forward(
        z_0, zf_0, g_0, gf_0
    )
    feed_0 = other_core(feed_0)
    core_0 = other_core(send_0)
    z_1 = gather_chips(z_1)
    grad_up_0, feed_0, core_0, z_1 = together(grad_up_0, feed_0, core_0, z_1)
    zf_1, core_0, feed_0 = together(other_core(z_1), core_0, feed_0)
    active_1, grad_up_1, feed_keep_1, feed_1, keep_1, send_1, up_sums_1 = feed_forward(
        z_1, zf_1, g_1, gf_1
    )
    core_1 = other_core(send_1)
    back_0 = scatter_chips(keep_0, core_0)
    feed_0 = scatter_chips(feed_keep_0, feed_0)
    grad_up_1, core_1, back_0, feed_0, feed_1 = together(
        grad_up_1, core_1, back_0, feed_0, feed_1
    )
    hidden_grad_0, h_0, second_sums_0 = second_back(0, hidden_0, back_0)
    h_0, core_1, grad_up_1, feed_1 = together(h_0, core_1, grad_up_1, feed_1)
    grads_two = grads_of(
        ([z_0, zf_0, z_1, zf_1], [*grad_up_0, *grad_up_1]),
        ([g_0, gf_0, g_1, gf_1], [*active_0, *active_1]),
    )
    back_1 = scatter_chips(keep_1, core_1)
    h_0 = gather_chips(h_0)
    feed_1 = other_core(feed_1)
    grads_two, back_1, h_0, feed_1 = together(grads_two, back_1, h_0, feed_1)
    summed_two = lax.psum_scatter(grads_two, "dp", scatter_dimension=0, tiled=True)
    hidden_grad_1, h_1, second_sums_1 = second_back(1, hidden_1, back_1)
    hf_0, h_1, feed_1 = together(other_core(h_0), h_1, feed_1)

    keep_0, send_0, grad_qkv_0, sums_0 = attend_back(0, h_0, hf_0, kept_0)
    h_1 = gather_chips(h_1)
    feed_1 = scatter_chips(feed_keep_1, feed_1)
    keep_0, send_0, h_1, feed_1, feed_0 = together(keep_0, send_0, h_1, feed_1, feed_0)
    outputs_back = exchange_back(
        [
            (hidden_0 + feed_0 + norms[5]).astype(low_type),
            (hidden_1 + feed_1 + norms[5]).astype(low_type),
        ]
    )
    core_0, hf_1 = together(other_core(send_0), other_core(h_1))
    keep_1, send_1, grad_qkv_1, sums_1 = attend_back(1, h_1, hf_1, kept_1)
    normed_back_0 = scatter_chips(keep_0, core_0)
    keep_1, send_1, normed_back_0, outputs_back = together(
        keep_1, send_1, normed_back_0, outputs_back
    )
    input_0, first_sums_0 = first_back(0, hidden_grad_0, normed_back_0)
    input_0, core_1 = together(input_0, other_core(send_1))
    inputs_back_0 = exchange_back([input_0])
    grads_one = grads_of(
        ([normed_0, normed_1], [grad_qkv_0, grad_qkv_1]),
        (
            [h_0, hf_0, h_1, hf_1],
            [kept[0][rows] for kept in (kept_0, kept_1) for rows in (slice(0, half), slice(half, rows_here))],
        ),
    )
    normed_back_1 = scatter_chips(keep_1, core_1)
    grads_one, normed_back_1, inputs_back_0 = together(grads_one, normed_back_1, inputs_back_0)
    input_1, first_sums_1 = first_back(1, hidden_grad_1, normed_back_1)
    summed_one = [
        scatter_grads(grads_one[:, h * 2 * local_cols : (h + 1) * 2 * local_cols])
        for h in range(2)
    ]
    norm_grads_own = jnp.concatenate(
        [first_sums_0 + first_sums_1, second_sums_0 + second_sums_1], axis=0
    )
    qkv_sums = sums_0 + sums_1
    up_sums = [up_sums_0, up_sums_1]

    head_own = jnp.concatenate(
        [
            qkv_sums[:, :local_cols],
            qkv_sums[:, 2 * local_cols :],
            sum(up_sums).reshape(ffn_count, local_cols),
        ],
        axis=0,
    )
    vectors = jnp.concatenate([sum_over(norm_grads_own, "mp"), head_own], axis=1)
    vectors = sum_over(vectors, "dp")
    norm_all = vectors[:, :model_width]
    head_total = vectors[:, model_width:]
    norm_cols = norm_vectors.shape[1]
    norm_total = lax.dynamic_slice_in_dim(norm_all, data_index * norm_cols, norm_cols, 1)

    slot_count = left_stats.shape[0]
    all_slots = slot_count * data_count
    slot_match = block_slot_index[None, :] == jnp.arange(all_slots)[:, None]
    filled = jnp.any(slot_match, axis=1)
    block_of = jnp.sum(jnp.where(slot_match, jnp.arange(blocks)[None, :], 0), axis=1)
    summed = [part.astype(low_type) for part in (*summed_one, summed_two)]
    owned = [
        exchange(rows).reshape(model_width, local_cols)
        for rows in to_slots(jnp.where(filled, block_of, -1), slot_count, local_cols, *summed)
    ]
    owned, input_1 = after(owned, input_1)
    inputs_back_1 = exchange_back([input_1])
    outputs_given = return_rows(outputs_back, micros)
    inputs_given = jnp.concatenate(
        [return_rows(inputs_back_0, [0]), return_rows(inputs_back_1, [1])], axis=0
    )
    whole = [gather_columns(owned[s], "mp") for s in range(slot_count)]
    slot_match_own = lax.dynamic_slice_in_dim(slot_match, data_index * slot_count, slot_count, 0)
    weights_all = jnp.concatenate([weights_one, weights_two], axis=1)

    row_total_count = left_stats.shape[1]
    lefts, rights, directions, squares, owned_weights = [], [], [], [], []
    for s in range(slot_count):
        grads = whole[s]
        my_rows = lax.dynamic_slice_in_dim(
            grads, model_index * row_total_count, row_total_count, 0
        )
        lefts.append(stat_decay * left_stats[s] + dot_nt(my_rows, grads))
        rights.append(stat_decay * right_stats[s] + dot_tn(owned[s], grads))
        halfway = dot_nt(grads.astype(f32), right_roots[s])
        direction = dot(left_roots[s], halfway)
        directions.append(direction)
        squares.append(jnp.sum(direction * direction))
        chosen = 0.0
        for b in range(blocks):
            chosen = chosen + jnp.where(
                slot_match_own[s, b],
                weights_all[:, b * local_cols : (b + 1) * local_cols].astype(f32),
                0.0,
            )
        owned_weights.append(chosen)
    square_total = sum_over(jnp.stack(squares).reshape(1, slot_count), "mp")[0]
    factor = lax.rsqrt(square_total / (model_width * model_width) + mean_eps)
    updated_blocks = jnp.stack(
        [
            owned_weights[s] - matrix_rate * factor[s] * directions[s]
            for s in range(slot_count)
        ],
        axis=1,
    )
    owned_grads = jnp.stack(owned, axis=1).astype(f32)
    new_norm_state = stat_decay * norm_state + norm_total * norm_total
    new_norm_vectors = norm_vectors - vector_rate * norm_total / (
        jnp.sqrt(new_norm_state) + diag_eps
    )
    new_head_state = stat_decay * head_state + head_total * head_total
    new_head_vectors = head_vectors - vector_rate * head_total / (
        jnp.sqrt(new_head_state) + diag_eps
    )
    return (
        outputs_given,
        inputs_given,
        owned_grads,
        jnp.stack(lefts),
        jnp.stack(rights),
        updated_blocks,
        norm_total,
        new_norm_state,
        new_norm_vectors,
        head_total,
        new_head_state,
        new_head_vectors,
    )


def solution(mesh):
    placed = (
        P(None, "dp", None),
        P(None, "dp", None),
        P(None, "dp", None),
        P(),
        P(),
        P("dp", None, "mp"),
        P(None, "dp"),
        P(None, "mp"),
        P("dp", "mp", None),
        P("dp", "mp", None),
        P("dp", None, None),
        P("dp", "mp", None),
        P(None, "dp"),
        P(None, "mp"),
    )
    return jax.shard_map(
        on_device,
        mesh=mesh,
        in_specs=placed,
        out_specs=(
            P(None, "dp", None),
            P(None, "dp", None),
            P(None, "dp", "mp"),
            P("dp", "mp", None),
            P("dp", "mp", None),
            P(None, "dp", "mp"),
            P(None, "dp"),
            P(None, "dp"),
            P(None, "dp"),
            P(None, "mp"),
            P(None, "mp"),
            P(None, "mp"),
        ),
        check_vma=False,
    )
```

```python
import functools
import math

import jax
import jax.numpy as jnp
from jax import lax
from jax.experimental import pallas as pl
from jax.experimental.pallas import tpu as pltpu
from jax.sharding import PartitionSpec as P

HEAD_DIM = 64


stat_decay = 0.5
matrix_rate = 0.02
vector_rate = 0.3
norm_eps = 1e-05
mean_eps = 1e-06
diag_eps = 1e-08
masked_score = -1000000000.0

f32 = jnp.float32
low_type = jnp.bfloat16


def unit_rows_of(values):
    center = values - jnp.mean(values, axis=-1, keepdims=True)
    spread = jnp.mean(center * center, axis=-1, keepdims=True)
    scale_rows = lax.rsqrt(spread + norm_eps)
    return center * scale_rows, scale_rows


def layer_norm(values, gain, shift):
    unit_rows, _ = unit_rows_of(values)
    return unit_rows * gain + shift


def norm_back(values, gain, grad_normed):
    unit_rows, scale_rows = unit_rows_of(values)
    grad_unit = grad_normed * gain
    grad_values = scale_rows * (
        grad_unit
        - jnp.mean(grad_unit, axis=-1, keepdims=True)
        - unit_rows * jnp.mean(grad_unit * unit_rows, axis=-1, keepdims=True)
    )
    return (grad_values, grad_normed * unit_rows)


def dot(left, right):
    return lax.dot_general(left, right, (((1,), (0,)), ((), ())), preferred_element_type=f32)


def dot_nt(left, right):
    return lax.dot_general(left, right, (((1,), (1,)), ((), ())), preferred_element_type=f32)


def dot_tn(left, right):
    return lax.dot_general(left, right, (((0,), (0,)), ((), ())), preferred_element_type=f32)


TILE = 256
STRIP = 64
VMEM_BYTES = 24 * 1024 * 1024
SMALL = pl.CostEstimate(flops=10**9, bytes_accessed=10**6, transcendentals=0)
LARGE = pl.CostEstimate(flops=20 * 10**9, bytes_accessed=10**6, transcendentals=0)
MEDIUM = pl.CostEstimate(flops=11 * 10**9, bytes_accessed=10**6, transcendentals=0)

def whole_spec():
    return pl.BlockSpec(memory_space=pltpu.VMEM)

def attention_forward_kernel(
    near_ref, far_ref, norm_ref, weights_ref, bias_ref,
    place_row_ref, place_col_ref, seg_row_ref, seg_col_ref,
    keep_ref, send_ref, normed_ref, attended_ref, qkv_ref, out_ref, lse_ref,
    arrived,
):
    rows = arrived.shape[0]
    half = rows // 2
    cols = attended_ref.shape[1]
    heads = cols // HEAD_DIM
    scale = 1.0 / math.sqrt(HEAD_DIM)
    tiles = rows // TILE
    for start, source in ((0, near_ref), (half, far_ref)):

        def norm_some(i, carry):
            values = source[pl.ds(pl.multiple_of(i * STRIP, STRIP), STRIP), :].astype(f32)
            normed = layer_norm(values, norm_ref[0:1, :], norm_ref[1:2, :])
            normed_ref[pl.ds(pl.multiple_of(start + i * STRIP, STRIP), STRIP), :] = (
                normed.astype(low_type)
            )
            return carry

        lax.fori_loop(0, half // STRIP, norm_some, 0)
    for t in range(tiles):
        part = normed_ref[pl.ds(t * TILE, TILE), :]
        arrived[pl.ds(t * TILE, TILE), :] = (
            dot(part, weights_ref[:, : 3 * cols]) + bias_ref[...]
        ).astype(low_type)
    for t in range(tiles):
        wanted = lax.broadcasted_iota(jnp.int32, (TILE, rows), 0) + t * TILE
        pick = jnp.where(wanted == place_row_ref[...], 1.0, 0.0).astype(low_type)
        qkv_ref[pl.ds(t * TILE, TILE), :] = dot(pick, arrived[...]).astype(low_type)
    for h in range(heads):
        lanes = slice(h * HEAD_DIM, (h + 1) * HEAD_DIM)
        key_lanes = slice(cols + h * HEAD_DIM, cols + (h + 1) * HEAD_DIM)
        value_lanes = slice(2 * cols + h * HEAD_DIM, 2 * cols + (h + 1) * HEAD_DIM)
        for t in range(tiles):
            here = slice(t * TILE, (t + 1) * TILE)
            query = qkv_ref[here, lanes]
            seg_q = seg_col_ref[here, :]
            scores = []
            top = None
            for c in range(t + 1):
                there = slice(c * TILE, (c + 1) * TILE)
                s = dot_nt(query, qkv_ref[there, key_lanes]) * scale
                allowed = seg_q == seg_row_ref[:, there]
                if c == t:
                    allowed = allowed & (
                        lax.broadcasted_iota(jnp.int32, (TILE, TILE), 0)
                        >= lax.broadcasted_iota(jnp.int32, (TILE, TILE), 1)
                    )
                s = jnp.where(allowed, s, masked_score)
                scores.append(s)
                m = jnp.max(s, axis=1, keepdims=True)
                top = m if top is None else jnp.maximum(top, m)
            total = 0.0
            out = 0.0
            for c in range(t + 1):
                there = slice(c * TILE, (c + 1) * TILE)
                e = jnp.exp(scores[c] - top)
                total = total + jnp.sum(e, axis=1, keepdims=True)
                out = out + dot(e.astype(low_type), qkv_ref[there, value_lanes])
            out_ref[here, lanes] = (out / total).astype(low_type)
            lse_ref[here, h : h + 1] = top + jnp.log(total)
    for t in range(tiles):
        wanted = lax.broadcasted_iota(jnp.int32, (TILE, rows), 1)
        pick = jnp.where(wanted == place_col_ref[pl.ds(t * TILE, TILE), :], 1.0, 0.0).astype(low_type)
        part = dot(pick, out_ref[...]).astype(low_type)
        attended_ref[pl.ds(t * TILE, TILE), :] = part
        branch = dot_nt(part, weights_ref[:, 3 * cols : 4 * cols])
        if t * TILE < half:
            keep_ref[pl.ds(t * TILE, TILE), :] = branch
        else:
            send_ref[pl.ds(t * TILE - half, TILE), :] = branch.astype(low_type)

def attention_forward(near, far, norms, weights, bias, place, segment):
    rows = 2 * near.shape[0]
    width = near.shape[1]
    cols = bias.shape[1] // 3
    heads = cols // HEAD_DIM
    shape = jax.ShapeDtypeStruct
    return pl.pallas_call(
        attention_forward_kernel,
        out_shape=(
            shape((rows // 2, width), f32),
            shape((rows // 2, width), low_type),
            shape((rows, width), low_type),
            shape((rows, cols), low_type),
            shape((rows, 3 * cols), low_type),
            shape((rows, cols), low_type),
            shape((rows, heads), f32),
        ),
        in_specs=[whole_spec()] * 9,
        out_specs=tuple([whole_spec()] * 7),
        scratch_shapes=[pltpu.VMEM((rows, 3 * cols), low_type)],
        compiler_params=pltpu.CompilerParams(vmem_limit_bytes=VMEM_BYTES),
        cost_estimate=LARGE,
    )(near, far, norms, weights, bias, place[None, :], place[:, None], segment[None, :], segment[:, None])

def attention_backward_kernel(
    near_ref, far_ref, weights_ref, place_row_ref, place_col_ref, seg_row_ref, seg_col_ref,
    qkv_ref, out_ref, lse_ref,
    keep_ref, send_ref, grads_ref, sums_ref,
    arrived, placed, grad_key, grad_value, moved,
):
    rows = arrived.shape[0]
    half = rows // 2
    cols = out_ref.shape[1]
    heads = cols // HEAD_DIM
    scale = 1.0 / math.sqrt(HEAD_DIM)
    tiles = rows // TILE
    for t in range(tiles):
        source = near_ref if t * TILE < half else far_ref
        part = source[pl.ds(t * TILE % half, TILE), :]
        arrived[pl.ds(t * TILE, TILE), :] = dot(
            part, weights_ref[:, 3 * cols : 4 * cols]
        ).astype(low_type)
    for t in range(tiles):
        wanted = lax.broadcasted_iota(jnp.int32, (TILE, rows), 0) + t * TILE
        pick = jnp.where(wanted == place_row_ref[...], 1.0, 0.0).astype(low_type)
        placed[pl.ds(t * TILE, TILE), :] = dot(pick, arrived[...]).astype(low_type)
    for h in range(heads):
        lanes = slice(h * HEAD_DIM, (h + 1) * HEAD_DIM)
        key_lanes = slice(cols + h * HEAD_DIM, cols + (h + 1) * HEAD_DIM)
        value_lanes = slice(2 * cols + h * HEAD_DIM, 2 * cols + (h + 1) * HEAD_DIM)
        grad_key[...] = jnp.zeros_like(grad_key)
        grad_value[...] = jnp.zeros_like(grad_value)
        for t in range(tiles):
            here = slice(t * TILE, (t + 1) * TILE)
            query = qkv_ref[here, lanes]
            grad = placed[here, lanes]
            row_total = jnp.sum(grad.astype(f32) * out_ref[here, lanes].astype(f32), axis=1, keepdims=True)
            seg_q = seg_col_ref[here, :]
            lse = lse_ref[here, h : h + 1]
            grad_query = 0.0
            for c in range(t + 1):
                there = slice(c * TILE, (c + 1) * TILE)
                key = qkv_ref[there, key_lanes]
                s = dot_nt(query, key) * scale
                allowed = seg_q == seg_row_ref[:, there]
                if c == t:
                    allowed = allowed & (
                        lax.broadcasted_iota(jnp.int32, (TILE, TILE), 0)
                        >= lax.broadcasted_iota(jnp.int32, (TILE, TILE), 1)
                    )
                p = jnp.where(allowed, jnp.exp(s - lse), 0.0)
                dp = dot_nt(grad, qkv_ref[there, value_lanes])
                ds = (p * (dp - row_total)).astype(low_type)
                grad_query = grad_query + dot(ds, key)
                grad_key[there, :] += dot_tn(ds, query)
                grad_value[there, :] += dot_tn(p.astype(low_type), grad)
            moved[here, lanes] = (grad_query * scale).astype(low_type)
        moved[:, key_lanes] = (grad_key[...] * scale).astype(low_type)
        moved[:, value_lanes] = grad_value[...].astype(low_type)
    sums_ref[...] = jnp.sum(moved[...].astype(f32), axis=0, keepdims=True)
    for t in range(tiles):
        wanted = lax.broadcasted_iota(jnp.int32, (TILE, rows), 1)
        pick = jnp.where(wanted == place_col_ref[pl.ds(t * TILE, TILE), :], 1.0, 0.0).astype(low_type)
        part = dot(pick, moved[...]).astype(low_type)
        grads_ref[pl.ds(t * TILE, TILE), :] = part
        normed = dot_nt(part, weights_ref[:, : 3 * cols])
        if t * TILE < half:
            keep_ref[pl.ds(t * TILE, TILE), :] = normed
        else:
            send_ref[pl.ds(t * TILE - half, TILE), :] = normed.astype(low_type)

def attention_backward(near, far, weights, place, segment, qkv, out, lse):
    rows = 2 * near.shape[0]
    width = near.shape[1]
    cols = out.shape[1]
    heads = cols // HEAD_DIM
    shape = jax.ShapeDtypeStruct
    return pl.pallas_call(
        attention_backward_kernel,
        out_shape=(
            shape((rows // 2, width), f32),
            shape((rows // 2, width), low_type),
            shape((rows, 3 * cols), low_type),
            shape((1, 3 * cols), f32),
        ),
        in_specs=[whole_spec()] * 10,
        out_specs=tuple([whole_spec()] * 4),
        scratch_shapes=[
            pltpu.VMEM((rows, cols), low_type),
            pltpu.VMEM((rows, cols), low_type),
            pltpu.VMEM((rows, HEAD_DIM), f32),
            pltpu.VMEM((rows, HEAD_DIM), f32),
            pltpu.VMEM((rows, 3 * cols), low_type),
        ],
        compiler_params=pltpu.CompilerParams(vmem_limit_bytes=VMEM_BYTES),
        cost_estimate=LARGE,
    )(near, far, weights, place[None, :], place[:, None], segment[None, :], segment[:, None], qkv, out, lse)

def mlp_kernel(normed_ref, grad_ref, weights_ref, bias_ref, active_ref, grad_up_ref, feed_ref, back_ref, sums_ref):
    rows, width = normed_ref.shape
    cols = bias_ref.shape[1]
    step = TILE
    total = 0.0
    c0 = math.sqrt(2.0 / math.pi)
    for t in range(rows // step):
        here = slice(t * step, (t + 1) * step)
        pre = dot(normed_ref[here, :], weights_ref[:, :cols]) + bias_ref[...]
        square = pre * pre
        bent = jnp.tanh(c0 * (pre + 0.044715 * (square * pre)))
        active_ref[here, :] = (0.5 * pre * (1.0 + bent)).astype(low_type)
        slope = 0.5 * (1.0 + bent) + 0.5 * pre * (1.0 - bent * bent) * (c0 * (1.0 + 0.134145 * square))
        grad = dot(grad_ref[here, :], weights_ref[:, cols:]) * slope
        grad_low = grad.astype(low_type)
        grad_up_ref[here, :] = grad_low
        total = total + jnp.sum(grad_low.astype(f32), axis=0, keepdims=True)
    sums_ref[...] = total
    for t in range(rows // step):
        here = slice(t * step, (t + 1) * step)
        back_ref[here, :] = dot_nt(grad_up_ref[here, :], weights_ref[:, :cols]).astype(back_ref.dtype)
        feed_ref[here, :] = dot_nt(active_ref[here, :], weights_ref[:, cols:]).astype(feed_ref.dtype)

def mlp(normed, grad, weights, bias, kind):
    rows, width = normed.shape
    cols = bias.shape[1]
    shape = jax.ShapeDtypeStruct
    return pl.pallas_call(
        mlp_kernel,
        out_shape=(
            shape((rows, cols), low_type),
            shape((rows, cols), low_type),
            shape((rows, width), kind),
            shape((rows, width), kind),
            shape((1, cols), f32),
        ),
        in_specs=[whole_spec()] * 4,
        out_specs=tuple([whole_spec()] * 5),
        compiler_params=pltpu.CompilerParams(vmem_limit_bytes=VMEM_BYTES),
        cost_estimate=MEDIUM,
    )(normed, grad, weights, bias)


def grads_kernel(groups, *refs):
    out_ref = refs[-1]
    for t in range(out_ref.shape[0] // TILE):
        rows = slice(t * TILE, (t + 1) * TILE)
        start = 0
        for group in groups:
            total = 0.0
            for left, right, at, count in group:
                total = total + dot_tn(refs[left][:, rows], refs[right][at : at + count, :])
            out_ref[rows, start : start + total.shape[1]] = total.astype(out_ref.dtype)
            start = start + total.shape[1]


def grads_of(*groups):
    width = groups[0][0][0].shape[1]
    cols = sum(right[0].shape[1] for _, right in groups)
    pieces = []
    plan = []
    for left, right in groups:
        start = len(pieces)
        pieces.extend((*left, *right))
        count = left[0].shape[0]
        fit = right[0].shape[0] // count
        plan.append(
            [
                (start + g, start + len(left) + g // fit, g % fit * count, count)
                for g in range(len(left))
            ]
        )
    return pl.pallas_call(
        functools.partial(grads_kernel, plan),
        out_shape=jax.ShapeDtypeStruct((width, cols), low_type),
        in_specs=[whole_spec()] * len(pieces),
        out_specs=whole_spec(),
        compiler_params=pltpu.CompilerParams(vmem_limit_bytes=VMEM_BYTES),
        cost_estimate=MEDIUM,
    )(*pieces)


def slots_kernel(cols, slot_count, block_ref, *refs):
    outs, held = refs[-1 - slot_count : -1], refs[-1]
    start = 0
    for part in refs[: -1 - slot_count]:
        held[:, start : start + part.shape[1]] = part[...]
        start = start + part.shape[1]
    for s in range(block_ref.shape[0]):
        out = outs[s % slot_count]
        block = block_ref[s]
        lanes = pl.ds(pl.multiple_of(jnp.maximum(block, 0) * cols, cols), cols)
        rows = held[:, lanes]
        out[s // slot_count] = jnp.where(block >= 0, rows, jnp.zeros_like(rows))


def to_slots(block_of, slot_count, cols, *parts):
    count = block_of.shape[0] // slot_count
    rows = parts[0].shape[0]
    width = sum(part.shape[1] for part in parts)
    return pl.pallas_call(
        functools.partial(slots_kernel, cols, slot_count),
        out_shape=tuple(
            [jax.ShapeDtypeStruct((count, rows, cols), low_type) for _ in range(slot_count)]
        ),
        in_specs=[pl.BlockSpec(memory_space=pltpu.SMEM)] + [whole_spec()] * len(parts),
        out_specs=tuple([whole_spec()] * slot_count),
        scratch_shapes=[pltpu.VMEM((rows, width), low_type)],
        compiler_params=pltpu.CompilerParams(vmem_limit_bytes=VMEM_BYTES),
        cost_estimate=SMALL,
    )(block_of, *parts)


def choose_kernel(cols, split, block_ref, first_ref, second_ref, *outs):
    for s, out in enumerate(outs):
        block = block_ref[s]

        @pl.when(block < 0)
        def _():
            out[...] = jnp.zeros_like(out)

        @pl.when((block >= 0) & (block < split))
        def _():
            lanes = pl.multiple_of(jnp.clip(block, 0, split - 1) * cols, cols)
            out[...] = first_ref[:, pl.ds(lanes, cols)]

        @pl.when(block >= split)
        def _():
            lanes = pl.multiple_of(jnp.maximum(block - split, 0) * cols, cols)
            out[...] = second_ref[:, pl.ds(lanes, cols)]


def choose_blocks(block_of, cols, first, second):
    slot_count = block_of.shape[0]
    return pl.pallas_call(
        functools.partial(choose_kernel, cols, 4),
        out_shape=tuple(
            [jax.ShapeDtypeStruct((first.shape[0], cols), low_type) for _ in range(slot_count)]
        ),
        in_specs=[pl.BlockSpec(memory_space=pltpu.SMEM), whole_spec(), whole_spec()],
        out_specs=tuple([whole_spec()] * slot_count),
        compiler_params=pltpu.CompilerParams(vmem_limit_bytes=VMEM_BYTES),
        cost_estimate=SMALL,
    )(block_of, first, second)


def precondition_kernel(slot, order, count, place_ref, near_ref, far_ref, *refs):
    stats_refs = refs[:4]
    new_left_ref, new_right_ref, direction_ref, square_ref = refs[4 + count : 8 + count]
    halfway_ref, left_ref, right_ref, left_root_ref, right_root_ref, sems = refs[8 + count :]
    held = (left_ref, right_ref, left_root_ref, right_root_ref)
    copies = [
        pltpu.make_async_copy(source.at[slot], target, sems.at[k])
        for k, (source, target) in enumerate(zip(stats_refs, held))
    ]
    for k in (3, 2, 0, 1):
        copies[k].start()
    cols = near_ref.shape[2]
    rows = left_ref.shape[0]
    width = near_ref.shape[1]
    place = place_ref[0]
    own_rows = pl.ds(pl.multiple_of(place * rows, rows), rows)
    pieces = [ref.at[k] for ref in (near_ref, far_ref) for k in range(near_ref.shape[0])]
    lanes = [pl.ds(pl.multiple_of((place ^ j) * cols, cols), cols) for j in order]
    copies[3].wait()
    halfway = 0.0
    for at, piece in zip(lanes, pieces):
        halfway = halfway + dot_nt(piece[...], right_root_ref[:, at].astype(low_type))
    halfway_ref[...] = halfway.astype(low_type)
    copies[2].wait()
    total = 0.0
    for t in range(width // TILE):
        here = slice(t * TILE, (t + 1) * TILE)
        part = dot(left_root_ref[here, :].astype(low_type), halfway_ref[...])
        direction_ref[here, :] = part
        total = total + jnp.sum(part * part, axis=0, keepdims=True)
    square_ref[...] = total
    copies[0].wait()
    left = stat_decay * left_ref[...]
    for piece in pieces:
        left = left + dot_nt(piece[own_rows, :], piece[...])
    new_left_ref[0] = left
    copies[1].wait()
    for at, piece in zip(lanes, pieces):
        new_right_ref[0, :, at] = stat_decay * right_ref[:, at] + dot_tn(
            pieces[0][...], piece[...]
        )


def precondition(s, place, near, far, stats, before):
    slot_count, rows, width = stats[0].shape
    cols = near.shape[2]
    shape = jax.ShapeDtypeStruct

    def of_slot(array):
        return pl.BlockSpec((1,) + array.shape[1:], lambda i: (s, 0, 0))

    def all_of(dims):
        return pl.BlockSpec(dims, lambda i: (0,) * len(dims))

    return pl.pallas_call(
        functools.partial(
            precondition_kernel, s, near_order(lax.axis_size("mp")), len(before)
        ),
        grid=(1,),
        out_shape=(
            shape(stats[0].shape, f32),
            shape(stats[1].shape, f32),
            shape((width, cols), f32),
            shape((1, cols), f32),
        ),
        in_specs=[pl.BlockSpec(memory_space=pltpu.SMEM), all_of(near.shape), all_of(far.shape)]
        + [pl.BlockSpec(memory_space=pl.ANY)] * (4 + len(before)),
        out_specs=(
            of_slot(stats[0]),
            of_slot(stats[1]),
            all_of((width, cols)),
            all_of((1, cols)),
        ),
        input_output_aliases={7 + k: k for k in range(len(before))},
        scratch_shapes=[pltpu.VMEM((width, cols), low_type)]
        + [pltpu.VMEM(array.shape[1:], f32) for array in stats]
        + [pltpu.SemaphoreType.DMA((4,))],
        compiler_params=pltpu.CompilerParams(vmem_limit_bytes=VMEM_BYTES),
        cost_estimate=SMALL,
    )(place, near, far, *stats, *before)


def give_back_kernel(slot_ref, near_ref, far_ref, *refs):
    out_ref = refs[-1]
    half = near_ref.shape[0]
    for t in range(out_ref.shape[1] // TILE):
        here = slice(t * TILE, (t + 1) * TILE)
        total = 0.0
        for start, source in ((0, near_ref), (half, far_ref)):
            wanted = lax.broadcasted_iota(jnp.int32, (TILE, half), 1) + start
            pick = jnp.where(wanted == slot_ref[here, :], 1.0, 0.0).astype(low_type)
            total = total + dot(pick, source[...])
        out_ref[0, here, :] = total.astype(low_type)


def give_back(micro, slots, near, far, micro_count, before):
    rows, width = 2 * near.shape[0], near.shape[1]

    def all_of(dims):
        return pl.BlockSpec(dims, lambda i: (0,) * len(dims))

    return [
        pl.pallas_call(
            give_back_kernel,
            grid=(1,),
            out_shape=jax.ShapeDtypeStruct((micro_count, rows, width), low_type),
            in_specs=[all_of((rows, 1)), all_of(near.shape), all_of(far.shape)]
            + [pl.BlockSpec(memory_space=pl.ANY)] * len(before),
            out_specs=pl.BlockSpec((1, rows, width), lambda i: (micro, 0, 0)),
            input_output_aliases={3 + k: k for k in range(len(before))},
            compiler_params=pltpu.CompilerParams(vmem_limit_bytes=VMEM_BYTES),
            cost_estimate=SMALL,
        )(slots[:, None], near, far, *before)
    ]


def swap(values, axis, bit):
    count = lax.axis_size(axis)
    return lax.ppermute(values, axis, [(i, i ^ bit) for i in range(count)])


def near_order(count):
    found = [0]
    bit = count // 2
    while bit >= 1:
        found = found + [j ^ bit for j in found]
        bit //= 2
    return found


def gather_chips(share):
    bit = lax.axis_size("mp") // 2
    while bit > 1:
        share = jnp.concatenate([share, swap(share, "mp", bit)], axis=0)
        bit //= 2
    return share


def other_core(values):
    return swap(values, "mp", 1)


def scatter_chips(keep, received):
    bit = 2
    count = lax.axis_size("mp")
    if bit == count:
        return keep + received.astype(f32)
    half = keep.shape[0] // 2
    sent = (keep[half:] + received[half:].astype(f32)).astype(low_type)
    got = swap(sent, "mp", bit)
    values = keep[:half] + received[:half].astype(f32)
    bit *= 2
    while bit < count:
        values = values + got.astype(f32)
        half = values.shape[0] // 2
        got = swap(values[half:].astype(low_type), "mp", bit)
        values, got = values[:half], got
        bit *= 2
    return values + got.astype(f32)


def after(values, others):
    return lax.optimization_barrier((values, others))


def together(*values):
    return lax.optimization_barrier(values)


def scatter_step(blocks, bit):
    index = lax.axis_index("dp") // bit % 2
    blocks = blocks.reshape(-1, 2, *blocks.shape[1:])
    mine = lax.dynamic_index_in_dim(blocks, index, 1, keepdims=False)
    other = lax.dynamic_index_in_dim(blocks, 1 - index, 1, keepdims=False)
    got = swap(other.astype(low_type), "dp", bit)
    return mine.astype(f32) + got.astype(f32)


def scatter_grads(blocks, bit):
    while bit < lax.axis_size("dp"):
        blocks = scatter_step(blocks, bit)
        bit *= 2
    return blocks[0].astype(low_type)


def sum_over(values, axis):
    bit = 1
    while bit < lax.axis_size(axis):
        values = values + swap(values, axis, bit)
        bit *= 2
    return values


def exchange(rows):
    return lax.all_to_all(rows, "dp", split_axis=0, concat_axis=0, tiled=True)


def on_device(
    tokens,
    cotangent,
    lengths,
    placement_ids,
    block_slot_index,
    matrices,
    norm_vectors,
    head_vectors,
    left_stats,
    right_stats,
    left_roots,
    right_roots,
    norm_state,
    head_state,
):
    data_count = lax.axis_size("dp")
    data_index = lax.axis_index("dp")
    model_count = lax.axis_size("mp")
    model_index = lax.axis_index("mp")
    micro_count, rows_here, model_width = tokens.shape
    piece_rows = rows_here // data_count
    sub_rows = piece_rows // model_count
    own_rows = rows_here // model_count
    blocks = matrices.shape[1]
    local_cols = matrices.shape[2]
    shard_rows = matrices.shape[0]
    ffn_count = (blocks - 4) // 2
    ffn_cols = ffn_count * local_cols

    matrices_low = matrices.astype(low_type)
    shipped_one = matrices_low[:, :4, :].reshape(shard_rows, 4 * local_cols)
    shipped_two = matrices_low[:, 4:, :].reshape(shard_rows, 2 * ffn_cols)
    lanes = 128
    norm_columns = jnp.swapaxes(norm_vectors.astype(low_type), 0, 1)
    shipped_one = jnp.concatenate(
        [shipped_one, jnp.pad(norm_columns, ((0, 0), (0, lanes - norm_columns.shape[1])))], axis=1
    )
    placement_ids, shipped_one = together(placement_ids, shipped_one)
    slot_count = left_stats.shape[0]
    all_slots = slot_count * data_count
    slot_match = block_slot_index[None, :] == jnp.arange(all_slots)[:, None]
    filled = jnp.any(slot_match, axis=1)
    block_of = jnp.sum(jnp.where(slot_match, jnp.arange(blocks)[None, :], 0), axis=1)
    block_of = jnp.where(filled, block_of, -1)
    own_blocks = lax.dynamic_slice_in_dim(block_of, data_index * slot_count, slot_count, 0)

    order = jnp.arange(rows_here)
    earlier = (order[:, None] < order[None, :]).astype(low_type)
    device_ids = jnp.arange(data_count)[:, None]
    near = near_order(model_count)
    slots_mine = []
    positions = []
    for micro in range(micro_count):
        dest_all = placement_ids[micro].reshape(data_count, rows_here)
        dest_mine = lax.dynamic_slice_in_dim(dest_all, data_index, 1, 0)
        target = dest_mine // rows_here
        to_each = target == device_ids
        to_me = (dest_all // rows_here) == data_index
        rank_both = dot(jnp.concatenate([to_each, to_me]).astype(low_type), earlier).astype(
            jnp.int32
        )
        rank_out = jnp.sum(jnp.where(to_each, rank_both[:data_count], 0), axis=0)
        slots_mine.append((rank_out, target[0]))
        rank_in = jnp.where(to_me, rank_both[data_count:], -1)
        place = jnp.sum(
            jnp.where(
                rank_in[:, None, :] == jnp.arange(piece_rows)[None, :, None],
                (dest_all - data_index * rows_here)[:, None, :],
                0,
            ),
            axis=2,
        )
        place = place.reshape(data_count, model_count, sub_rows).transpose(1, 0, 2)
        place = place.reshape(model_count, own_rows)[model_index ^ jnp.array(near)]
        positions.append(place.reshape(rows_here))

    def pick_rows(given):
        picked = []
        for micro in range(micro_count):
            rank, target = slots_mine[micro]
            here = (rank // sub_rows) == model_index
            slot = jnp.where(here, target * sub_rows + rank % sub_rows, -1)
            pick = (slot[None, :] == jnp.arange(own_rows)[:, None]).astype(low_type)
            rows = dot(pick, given[micro]).astype(low_type)
            picked.append(rows.reshape(data_count, sub_rows, model_width))
        return jnp.concatenate(picked, axis=1)

    def arrived(picked):
        got = exchange(picked).reshape(data_count, micro_count, sub_rows, model_width)
        return [got[:, i].reshape(own_rows, model_width) for i in range(micro_count)]

    def exchange_back(own):
        sent = [rows.reshape(data_count, 1, sub_rows, model_width) for rows in own]
        sent = jnp.concatenate(sent, axis=1)
        got = exchange(sent.reshape(data_count, -1, model_width))
        got = got.reshape(data_count, len(own), sub_rows, model_width)
        return [got[:, i].reshape(own_rows, model_width) for i in range(len(own))]

    def return_slots(micro):
        rank, target = slots_mine[micro]
        block = jnp.sum(
            jnp.where(
                ((rank // sub_rows) ^ model_index) == jnp.array(near)[:, None],
                jnp.arange(model_count)[:, None],
                0,
            ),
            axis=0,
        )
        return block * own_rows + target * sub_rows + rank % sub_rows

    micros = range(micro_count)
    bounds = [jnp.cumsum(lengths[i, 0]) for i in micros]
    segments = [
        jnp.sum((order[:, None] >= bounds[i][None, :]).astype(jnp.int32), axis=1) for i in micros
    ]
    bias_qkv = jnp.concatenate(
        [head_vectors[0], jnp.zeros((local_cols,), f32), head_vectors[1]]
    )[None]
    bias_up = head_vectors[2:].reshape(1, -1)
    half = rows_here // 2
    halves = (slice(0, half), slice(half, rows_here))

    def attend(i, near, far):
        return attention_forward(
            near, far, norms[:2], weights_one, bias_qkv, positions[i], segments[i]
        )

    def second_share(hidden):
        return layer_norm(hidden, norms[3], norms[4]).astype(low_type)

    def second_back(i, hidden, grad_normed):
        hidden_part, gain_rows = norm_back(hidden, norms[3], grad_normed)
        grad_hidden = grad_out[i] + hidden_part
        sums = [
            jnp.sum(grad_hidden, axis=0),
            jnp.sum(gain_rows, axis=0),
            jnp.sum(grad_normed, axis=0),
            jnp.sum(grad_out[i], axis=0),
        ]
        return grad_hidden, grad_hidden.astype(low_type), jnp.stack(sums)

    def attend_back(i, near, far, kept):
        _, qkv, out, lse = kept
        return attention_backward(
            near, far, weights_one, positions[i], segments[i], qkv, out, lse
        )

    def first_back(i, grad_hidden, grad_normed):
        rows_part, gain_rows = norm_back(rows_own[i], norms[0], grad_normed)
        sums = [jnp.sum(gain_rows, axis=0), jnp.sum(grad_normed, axis=0)]
        return (grad_hidden + rows_part).astype(low_type), jnp.stack(sums)

    picked, shipped_one = together(pick_rows(tokens), shipped_one)
    gathered = lax.all_gather(shipped_one, "dp", axis=0, tiled=True)
    x_0, x_1 = arrived(picked)
    rows_0, rows_1 = x_0.astype(f32), x_1.astype(f32)
    rows_own = (rows_0, rows_1)
    x_0 = gather_chips(x_0)
    x_1 = gather_chips(x_1)
    keep = [(positions[i][:own_rows] < bounds[i][-2])[:, None] for i in micros]
    picked, x_0 = together(pick_rows(cotangent), x_0)
    g_0, g_1 = (jnp.where(k, g, 0).astype(low_type) for g, k in zip(arrived(picked), keep))
    grad_out = (g_0.astype(f32), g_1.astype(f32))
    xf_0 = other_core(x_0)
    xf_1 = other_core(x_1)
    gathered, shipped_two, xf_0, xf_1, g_0, g_1 = together(
        gathered, shipped_two, xf_0, xf_1, g_0, g_1
    )
    weights_one = gathered
    norms = jnp.swapaxes(gathered[:, 4 * local_cols :], 0, 1)[:6].astype(f32)
    weights_two = lax.all_gather(shipped_two, "dp", axis=0, tiled=True)

    keep_0, send_0, normed_0, *kept_0 = attend(0, x_0, xf_0)
    g_0 = gather_chips(g_0)
    keep_0, send_0, g_0, g_1 = together(keep_0, send_0, g_0, g_1)
    core_0, gf_0, g_1 = together(other_core(send_0), other_core(g_0), g_1)
    branch_0 = scatter_chips(keep_0, core_0)
    keep_1, send_1, normed_1, *kept_1 = attend(1, x_1, xf_1)
    g_1 = gather_chips(g_1)
    keep_1, send_1, branch_0, g_1 = together(keep_1, send_1, branch_0, g_1)
    hidden_0 = rows_0 + branch_0 + norms[2]
    z_0, core_1, gf_1 = together(second_share(hidden_0), other_core(send_1), other_core(g_1))
    branch_1 = scatter_chips(keep_1, core_1)
    z_0 = gather_chips(z_0)
    z_0, branch_1, weights_two, gf_0, gf_1 = together(z_0, branch_1, weights_two, gf_0, gf_1)
    hidden_1 = rows_1 + branch_1 + norms[2]
    z_1, z_0 = together(second_share(hidden_1), z_0)

    zf_0 = other_core(z_0)
    near_parts = mlp(z_0, g_0, weights_two, bias_up, f32)
    z_1 = gather_chips(z_1)
    zf_0, near_parts = together(zf_0, near_parts)
    far_parts = mlp(zf_0, gf_0, weights_two, bias_up, low_type)
    active_0, grad_up_0, feed_0, back_0, up_sums_0 = zip(near_parts, far_parts)
    z_1, back_0, feed_0 = together(z_1, back_0, feed_0)
    zf_1 = other_core(z_1)
    core_0 = other_core(back_0[1])
    near_parts = mlp(z_1, g_1, weights_two, bias_up, f32)
    zf_1, core_0, near_parts = together(zf_1, core_0, near_parts)
    back_0 = scatter_chips(back_0[0], core_0)
    core_feed_0 = other_core(feed_0[1])
    far_parts = mlp(zf_1, gf_1, weights_two, bias_up, low_type)
    active_1, grad_up_1, feed_1, back_1, up_sums_1 = zip(near_parts, far_parts)
    back_0, back_1, feed_1, core_feed_0 = together(back_0, back_1, feed_1, core_feed_0)
    hidden_grad_0, h_0, second_sums_0 = second_back(0, hidden_0, back_0)
    h_0, grad_up_1, back_1 = together(h_0, grad_up_1, back_1)
    h_0 = gather_chips(h_0)
    grads_two = grads_of(
        ([z_0, zf_0, z_1, zf_1], [*grad_up_0, *grad_up_1]),
        ([g_0, gf_0, g_1, gf_1], [*active_0, *active_1]),
    )
    core_1 = other_core(back_1[1])
    grads_two, h_0, core_1, core_feed_0 = together(grads_two, h_0, core_1, core_feed_0)
    summed_two = lax.psum_scatter(grads_two, "dp", scatter_dimension=0, tiled=True)
    chosen = choose_blocks(own_blocks, local_cols, weights_one, weights_two)
    hf_0, chosen, core_1, core_feed_0 = together(other_core(h_0), chosen, core_1, core_feed_0)

    back_1 = scatter_chips(back_1[0], core_1)
    output_0 = scatter_chips(feed_0[0], core_feed_0)
    keep_0, send_0, grad_qkv_0, sums_0 = attend_back(0, h_0, hf_0, kept_0)
    core_feed_1 = other_core(feed_1[1])
    keep_0, send_0, back_1, output_0, core_feed_1 = together(
        keep_0, send_0, back_1, output_0, core_feed_1
    )
    hidden_grad_1, h_1, second_sums_1 = second_back(1, hidden_1, back_1)
    h_1, keep_0, send_0, output_0 = together(h_1, keep_0, send_0, output_0)
    h_1 = gather_chips(h_1)
    core_0 = other_core(send_0)
    output_0 = (hidden_0 + output_0 + norms[5]).astype(low_type)
    h_1, core_0, output_0, core_feed_1 = together(h_1, core_0, output_0, core_feed_1)
    output_0 = exchange_back([output_0])[0]
    hf_1, core_0, core_feed_1 = together(other_core(h_1), core_0, core_feed_1)
    normed_back_0 = scatter_chips(keep_0, core_0)
    output_1 = scatter_chips(feed_1[0], core_feed_1)
    grads_out = grads_of(([h_0, hf_0, h_1, hf_1], [kept_0[0], kept_1[0]]))
    hf_1, grads_out = together(hf_1, grads_out)
    blocks_out = scatter_step(grads_out.reshape(data_count, shard_rows, local_cols), 1)
    keep_1, send_1, grad_qkv_1, sums_1 = attend_back(1, h_1, hf_1, kept_1)
    keep_1, send_1, normed_back_0, output_1, output_0, summed_two, blocks_out = together(
        keep_1, send_1, normed_back_0, output_1, output_0, summed_two, blocks_out
    )
    core_1 = other_core(send_1)
    grads_qkv = grads_of(([normed_0, normed_1], [grad_qkv_0, grad_qkv_1]))
    core_1, grads_qkv = together(core_1, grads_qkv)
    normed_back_1 = scatter_chips(keep_1, core_1)
    input_0, first_sums_0 = first_back(0, hidden_grad_0, normed_back_0)
    output_1 = (hidden_1 + output_1 + norms[5]).astype(low_type)
    cut = 3 * local_cols // 2 // 128 * 128
    grads_one = [
        scatter_step(part.reshape(data_count, shard_rows, -1), 1)
        for part in (grads_qkv[:, :cut], grads_qkv[:, cut:])
    ]
    blocks_out = scatter_step(blocks_out, 2)
    normed_back_1, grads_one, input_0, output_1, output_0, blocks_out = together(
        normed_back_1, grads_one, input_0, output_1, output_0, blocks_out
    )
    input_0, output_1 = exchange_back([input_0, output_1])
    input_1, first_sums_1 = first_back(1, hidden_grad_1, normed_back_1)
    summed_one = [scatter_grads(part, 2) for part in (*grads_one,)]
    summed_one.append(scatter_grads(blocks_out, 4))
    norm_grads_own = jnp.concatenate(
        [first_sums_0 + first_sums_1, second_sums_0 + second_sums_1], axis=0
    )
    qkv_sums = sums_0 + sums_1
    up_sums = [*up_sums_0, *up_sums_1]

    norm_grads_sum = sum_over(norm_grads_own, "mp")
    output_0 = gather_chips(output_0)
    summed_one, output_0, norm_grads_sum, input_1 = together(
        summed_one, output_0, norm_grads_sum, input_1
    )
    slotted = to_slots(block_of, slot_count, local_cols, *summed_one, summed_two)
    stats = (left_stats, right_stats, left_roots, right_roots)
    place = model_index.astype(jnp.int32).reshape(1)
    returns = [return_slots(i) for i in micros]

    def own_slot(s):
        return exchange(slotted[s]).reshape(1, model_width, local_cols)

    owned_0 = own_slot(0)
    outputs_given = give_back(0, returns[0], output_0, other_core(output_0), micro_count, [])
    owned_0, outputs_given, slotted, input_0, output_1 = together(
        owned_0, outputs_given, slotted, input_0, output_1
    )
    near_0 = gather_chips(owned_0)
    owned = [owned_0] + [own_slot(s) for s in range(1, slot_count)]
    near_0, owned, input_1, input_0, output_1 = together(
        near_0, owned, input_1, input_0, output_1
    )
    input_1 = exchange_back([input_1])[0]
    far_0 = other_core(near_0)
    *fresh, direction, square = precondition(0, place, near_0, far_0, stats, [])
    directions, squares = [direction], [square]
    for s in range(1, slot_count):
        near_part = gather_chips(owned[s])
        near_part, fresh, input_0, output_1 = together(near_part, fresh, input_0, output_1)
        *fresh, direction, square = precondition(
            s, place, near_part, other_core(near_part), stats, fresh
        )
        directions.append(direction)
        squares.append(square)
    head_own = jnp.concatenate(
        [
            qkv_sums[:, :local_cols],
            qkv_sums[:, 2 * local_cols :],
            sum(up_sums).reshape(ffn_count, local_cols),
        ],
        axis=0,
    )
    vectors = jnp.concatenate([norm_grads_sum, head_own], axis=1)
    vectors, input_1 = together(vectors, input_1)
    vectors = sum_over(vectors, "dp")
    norm_all = vectors[:, :model_width]
    head_total = vectors[:, model_width:]
    norm_cols = norm_vectors.shape[1]
    norm_total = lax.dynamic_slice_in_dim(norm_all, data_index * norm_cols, norm_cols, 1)

    input_0, output_1, input_1 = [gather_chips(rows) for rows in (input_0, output_1, input_1)]
    inputs_given = give_back(0, returns[0], input_0, other_core(input_0), micro_count, [])
    outputs_given = give_back(
        1, returns[1], output_1, other_core(output_1), micro_count, outputs_given
    )
    inputs_given = give_back(
        1, returns[1], input_1, other_core(input_1), micro_count, inputs_given
    )[0]
    outputs_given = outputs_given[0]
    new_left, new_right = fresh
    squares = [jnp.sum(square) for square in squares]
    square_total = sum_over(jnp.stack(squares).reshape(1, slot_count), "mp")[0]
    factor = lax.rsqrt(square_total / (model_width * model_width) + mean_eps)
    updated_blocks = jnp.stack(
        [
            chosen[s].astype(f32) - matrix_rate * factor[s] * directions[s]
            for s in range(slot_count)
        ],
        axis=1,
    )
    owned_grads = jnp.stack([rows[0] for rows in owned], axis=1).astype(f32)
    new_norm_state = stat_decay * norm_state + norm_total * norm_total
    new_norm_vectors = norm_vectors - vector_rate * norm_total / (
        jnp.sqrt(new_norm_state) + diag_eps
    )
    new_head_state = stat_decay * head_state + head_total * head_total
    new_head_vectors = head_vectors - vector_rate * head_total / (
        jnp.sqrt(new_head_state) + diag_eps
    )
    return (
        outputs_given,
        inputs_given,
        owned_grads,
        new_left,
        new_right,
        updated_blocks,
        norm_total,
        new_norm_state,
        new_norm_vectors,
        head_total,
        new_head_state,
        new_head_vectors,
    )


def solution(mesh):
    placed = (
        P(None, "dp", None),
        P(None, "dp", None),
        P(None, "dp", None),
        P(),
        P(),
        P("dp", None, "mp"),
        P(None, "dp"),
        P(None, "mp"),
        P("dp", "mp", None),
        P("dp", "mp", None),
        P("dp", None, None),
        P("dp", "mp", None),
        P(None, "dp"),
        P(None, "mp"),
    )
    return jax.shard_map(
        on_device,
        mesh=mesh,
        in_specs=placed,
        out_specs=(
            P(None, "dp", None),
            P(None, "dp", None),
            P(None, "dp", "mp"),
            P("dp", "mp", None),
            P("dp", "mp", None),
            P(None, "dp", "mp"),
            P(None, "dp"),
            P(None, "dp"),
            P(None, "dp"),
            P(None, "mp"),
            P(None, "mp"),
            P(None, "mp"),
        ),
        check_vma=False,
    )
```

```python
import functools
import math

import jax
import jax.numpy as jnp
from jax import lax
from jax.experimental import pallas as pl
from jax.experimental.pallas import tpu as pltpu
from jax.sharding import PartitionSpec as P

HEAD_DIM = 64


stat_decay = 0.5
matrix_rate = 0.02
vector_rate = 0.3
norm_eps = 1e-05
mean_eps = 1e-06
diag_eps = 1e-08
masked_score = -1000000000.0

f32 = jnp.float32
low_type = jnp.bfloat16


def unit_rows_of(values):
    center = values - jnp.mean(values, axis=-1, keepdims=True)
    spread = jnp.mean(center * center, axis=-1, keepdims=True)
    scale_rows = lax.rsqrt(spread + norm_eps)
    return center * scale_rows, scale_rows


def layer_norm(values, gain, shift):
    unit_rows, _ = unit_rows_of(values)
    return unit_rows * gain + shift


def norm_back(values, gain, grad_normed):
    unit_rows, scale_rows = unit_rows_of(values)
    grad_unit = grad_normed * gain
    grad_values = scale_rows * (
        grad_unit
        - jnp.mean(grad_unit, axis=-1, keepdims=True)
        - unit_rows * jnp.mean(grad_unit * unit_rows, axis=-1, keepdims=True)
    )
    return (grad_values, grad_normed * unit_rows)


def dot(left, right):
    return lax.dot_general(left, right, (((1,), (0,)), ((), ())), preferred_element_type=f32)


def dot_nt(left, right):
    return lax.dot_general(left, right, (((1,), (1,)), ((), ())), preferred_element_type=f32)


def dot_tn(left, right):
    return lax.dot_general(left, right, (((0,), (0,)), ((), ())), preferred_element_type=f32)


TILE = 256
STRIP = 64
VMEM_BYTES = 20 * 1024 * 1024
SMALL = pl.CostEstimate(flops=10**9, bytes_accessed=10**6, transcendentals=0)
LARGE = pl.CostEstimate(flops=20 * 10**9, bytes_accessed=10**6, transcendentals=0)
MEDIUM = pl.CostEstimate(flops=11 * 10**9, bytes_accessed=10**6, transcendentals=0)

def whole_spec():
    return pl.BlockSpec(memory_space=pltpu.VMEM)

def attention_forward_kernel(
    near_ref, far_ref, norm_ref, weights_ref, bias_ref,
    place_row_ref, place_col_ref, seg_row_ref, seg_col_ref,
    keep_ref, send_ref, normed_ref, attended_ref, qkv_ref, out_ref, lse_ref,
    arrived,
):
    rows = arrived.shape[0]
    half = rows // 2
    cols = attended_ref.shape[1]
    heads = cols // HEAD_DIM
    scale = 1.0 / math.sqrt(HEAD_DIM)
    tiles = rows // TILE
    for start, source in ((0, near_ref), (half, far_ref)):

        def norm_some(i, carry):
            values = source[pl.ds(pl.multiple_of(i * STRIP, STRIP), STRIP), :].astype(f32)
            normed = layer_norm(values, norm_ref[0:1, :], norm_ref[1:2, :])
            normed_ref[pl.ds(pl.multiple_of(start + i * STRIP, STRIP), STRIP), :] = (
                normed.astype(low_type)
            )
            return carry

        lax.fori_loop(0, half // STRIP, norm_some, 0)
    for t in range(tiles):
        part = normed_ref[pl.ds(t * TILE, TILE), :]
        arrived[pl.ds(t * TILE, TILE), :] = (
            dot(part, weights_ref[:, : 3 * cols]) + bias_ref[...]
        ).astype(low_type)
    for t in range(tiles):
        wanted = lax.broadcasted_iota(jnp.int32, (TILE, rows), 0) + t * TILE
        pick = jnp.where(wanted == place_row_ref[...], 1.0, 0.0).astype(low_type)
        qkv_ref[pl.ds(t * TILE, TILE), :] = dot(pick, arrived[...]).astype(low_type)
    for h in range(heads):
        lanes = slice(h * HEAD_DIM, (h + 1) * HEAD_DIM)
        key_lanes = slice(cols + h * HEAD_DIM, cols + (h + 1) * HEAD_DIM)
        value_lanes = slice(2 * cols + h * HEAD_DIM, 2 * cols + (h + 1) * HEAD_DIM)
        for t in range(tiles):
            here = slice(t * TILE, (t + 1) * TILE)
            query = qkv_ref[here, lanes]
            seg_q = seg_col_ref[here, :]
            scores = []
            top = None
            for c in range(t + 1):
                there = slice(c * TILE, (c + 1) * TILE)
                s = dot_nt(query, qkv_ref[there, key_lanes]) * scale
                allowed = seg_q == seg_row_ref[:, there]
                if c == t:
                    allowed = allowed & (
                        lax.broadcasted_iota(jnp.int32, (TILE, TILE), 0)
                        >= lax.broadcasted_iota(jnp.int32, (TILE, TILE), 1)
                    )
                s = jnp.where(allowed, s, masked_score)
                scores.append(s)
                m = jnp.max(s, axis=1, keepdims=True)
                top = m if top is None else jnp.maximum(top, m)
            total = 0.0
            out = 0.0
            for c in range(t + 1):
                there = slice(c * TILE, (c + 1) * TILE)
                e = jnp.exp(scores[c] - top)
                total = total + jnp.sum(e, axis=1, keepdims=True)
                out = out + dot(e.astype(low_type), qkv_ref[there, value_lanes])
            out_ref[here, lanes] = (out / total).astype(low_type)
            lse_ref[here, h : h + 1] = top + jnp.log(total)
    for t in range(tiles):
        wanted = lax.broadcasted_iota(jnp.int32, (TILE, rows), 1)
        pick = jnp.where(wanted == place_col_ref[pl.ds(t * TILE, TILE), :], 1.0, 0.0).astype(low_type)
        part = dot(pick, out_ref[...]).astype(low_type)
        attended_ref[pl.ds(t * TILE, TILE), :] = part
        branch = dot_nt(part, weights_ref[:, 3 * cols : 4 * cols])
        if t * TILE < half:
            keep_ref[pl.ds(t * TILE, TILE), :] = branch
        else:
            send_ref[pl.ds(t * TILE - half, TILE), :] = branch.astype(low_type)

def attention_forward(near, far, norms, weights, bias, place, segment):
    rows = 2 * near.shape[0]
    width = near.shape[1]
    cols = bias.shape[1] // 3
    heads = cols // HEAD_DIM
    shape = jax.ShapeDtypeStruct
    return pl.pallas_call(
        attention_forward_kernel,
        out_shape=(
            shape((rows // 2, width), f32),
            shape((rows // 2, width), low_type),
            shape((rows, width), low_type),
            shape((rows, cols), low_type),
            shape((rows, 3 * cols), low_type),
            shape((rows, cols), low_type),
            shape((rows, heads), f32),
        ),
        in_specs=[whole_spec()] * 9,
        out_specs=tuple([whole_spec()] * 7),
        scratch_shapes=[pltpu.VMEM((rows, 3 * cols), low_type)],
        compiler_params=pltpu.CompilerParams(vmem_limit_bytes=VMEM_BYTES),
        cost_estimate=LARGE,
    )(near, far, norms, weights, bias, place[None, :], place[:, None], segment[None, :], segment[:, None])

def attention_backward_kernel(
    near_ref, far_ref, weights_ref, place_row_ref, place_col_ref, seg_row_ref, seg_col_ref,
    qkv_ref, out_ref, lse_ref,
    keep_ref, send_ref, grads_ref, sums_ref,
    arrived, placed, grad_key, grad_value, moved,
):
    rows = arrived.shape[0]
    half = rows // 2
    cols = out_ref.shape[1]
    heads = cols // HEAD_DIM
    scale = 1.0 / math.sqrt(HEAD_DIM)
    tiles = rows // TILE
    for t in range(tiles):
        source = near_ref if t * TILE < half else far_ref
        part = source[pl.ds(t * TILE % half, TILE), :]
        arrived[pl.ds(t * TILE, TILE), :] = dot(
            part, weights_ref[:, 3 * cols : 4 * cols]
        ).astype(low_type)
    for t in range(tiles):
        wanted = lax.broadcasted_iota(jnp.int32, (TILE, rows), 0) + t * TILE
        pick = jnp.where(wanted == place_row_ref[...], 1.0, 0.0).astype(low_type)
        placed[pl.ds(t * TILE, TILE), :] = dot(pick, arrived[...]).astype(low_type)
    for h in range(heads):
        lanes = slice(h * HEAD_DIM, (h + 1) * HEAD_DIM)
        key_lanes = slice(cols + h * HEAD_DIM, cols + (h + 1) * HEAD_DIM)
        value_lanes = slice(2 * cols + h * HEAD_DIM, 2 * cols + (h + 1) * HEAD_DIM)
        grad_key[...] = jnp.zeros_like(grad_key)
        grad_value[...] = jnp.zeros_like(grad_value)
        for t in range(tiles):
            here = slice(t * TILE, (t + 1) * TILE)
            query = qkv_ref[here, lanes]
            grad = placed[here, lanes]
            row_total = jnp.sum(grad.astype(f32) * out_ref[here, lanes].astype(f32), axis=1, keepdims=True)
            seg_q = seg_col_ref[here, :]
            lse = lse_ref[here, h : h + 1]
            grad_query = 0.0
            for c in range(t + 1):
                there = slice(c * TILE, (c + 1) * TILE)
                key = qkv_ref[there, key_lanes]
                s = dot_nt(query, key) * scale
                allowed = seg_q == seg_row_ref[:, there]
                if c == t:
                    allowed = allowed & (
                        lax.broadcasted_iota(jnp.int32, (TILE, TILE), 0)
                        >= lax.broadcasted_iota(jnp.int32, (TILE, TILE), 1)
                    )
                p = jnp.where(allowed, jnp.exp(s - lse), 0.0)
                dp = dot_nt(grad, qkv_ref[there, value_lanes])
                ds = (p * (dp - row_total)).astype(low_type)
                grad_query = grad_query + dot(ds, key)
                grad_key[there, :] += dot_tn(ds, query)
                grad_value[there, :] += dot_tn(p.astype(low_type), grad)
            moved[here, lanes] = (grad_query * scale).astype(low_type)
        moved[:, key_lanes] = (grad_key[...] * scale).astype(low_type)
        moved[:, value_lanes] = grad_value[...].astype(low_type)
    sums_ref[...] = jnp.sum(moved[...].astype(f32), axis=0, keepdims=True)
    for t in range(tiles):
        wanted = lax.broadcasted_iota(jnp.int32, (TILE, rows), 1)
        pick = jnp.where(wanted == place_col_ref[pl.ds(t * TILE, TILE), :], 1.0, 0.0).astype(low_type)
        part = dot(pick, moved[...]).astype(low_type)
        grads_ref[pl.ds(t * TILE, TILE), :] = part
        normed = dot_nt(part, weights_ref[:, : 3 * cols])
        if t * TILE < half:
            keep_ref[pl.ds(t * TILE, TILE), :] = normed
        else:
            send_ref[pl.ds(t * TILE - half, TILE), :] = normed.astype(low_type)

def attention_backward(near, far, weights, place, segment, qkv, out, lse):
    rows = 2 * near.shape[0]
    width = near.shape[1]
    cols = out.shape[1]
    heads = cols // HEAD_DIM
    shape = jax.ShapeDtypeStruct
    return pl.pallas_call(
        attention_backward_kernel,
        out_shape=(
            shape((rows // 2, width), f32),
            shape((rows // 2, width), low_type),
            shape((rows, 3 * cols), low_type),
            shape((1, 3 * cols), f32),
        ),
        in_specs=[whole_spec()] * 10,
        out_specs=tuple([whole_spec()] * 4),
        scratch_shapes=[
            pltpu.VMEM((rows, cols), low_type),
            pltpu.VMEM((rows, cols), low_type),
            pltpu.VMEM((rows, HEAD_DIM), f32),
            pltpu.VMEM((rows, HEAD_DIM), f32),
            pltpu.VMEM((rows, 3 * cols), low_type),
        ],
        compiler_params=pltpu.CompilerParams(vmem_limit_bytes=VMEM_BYTES),
        cost_estimate=LARGE,
    )(near, far, weights, place[None, :], place[:, None], segment[None, :], segment[:, None], qkv, out, lse)

def mlp_kernel(normed_ref, grad_ref, weights_ref, bias_ref, active_ref, grad_up_ref, feed_ref, back_ref, sums_ref):
    rows, width = normed_ref.shape
    cols = bias_ref.shape[1]
    step = TILE
    total = 0.0
    c0 = math.sqrt(2.0 / math.pi)
    for t in range(rows // step):
        here = slice(t * step, (t + 1) * step)
        pre = dot(normed_ref[here, :], weights_ref[:, :cols]) + bias_ref[...]
        square = pre * pre
        bent = jnp.tanh(c0 * (pre + 0.044715 * (square * pre)))
        active_ref[here, :] = (0.5 * pre * (1.0 + bent)).astype(low_type)
        slope = 0.5 * (1.0 + bent) + 0.5 * pre * (1.0 - bent * bent) * (c0 * (1.0 + 0.134145 * square))
        grad = dot(grad_ref[here, :], weights_ref[:, cols:]) * slope
        grad_low = grad.astype(low_type)
        grad_up_ref[here, :] = grad_low
        total = total + jnp.sum(grad_low.astype(f32), axis=0, keepdims=True)
    sums_ref[...] = total
    for t in range(rows // step):
        here = slice(t * step, (t + 1) * step)
        back_ref[here, :] = dot_nt(grad_up_ref[here, :], weights_ref[:, :cols]).astype(back_ref.dtype)
        feed_ref[here, :] = dot_nt(active_ref[here, :], weights_ref[:, cols:]).astype(feed_ref.dtype)

def mlp(normed, grad, weights, bias, kind):
    rows, width = normed.shape
    cols = bias.shape[1]
    shape = jax.ShapeDtypeStruct
    return pl.pallas_call(
        mlp_kernel,
        out_shape=(
            shape((rows, cols), low_type),
            shape((rows, cols), low_type),
            shape((rows, width), kind),
            shape((rows, width), kind),
            shape((1, cols), f32),
        ),
        in_specs=[whole_spec()] * 4,
        out_specs=tuple([whole_spec()] * 5),
        compiler_params=pltpu.CompilerParams(vmem_limit_bytes=VMEM_BYTES),
        cost_estimate=MEDIUM,
    )(normed, grad, weights, bias)


def grads_kernel(groups, *refs):
    out_ref = refs[-1]
    for t in range(out_ref.shape[0] // TILE):
        rows = slice(t * TILE, (t + 1) * TILE)
        start = 0
        for group in groups:
            total = 0.0
            for left, right, at, count in group:
                total = total + dot_tn(refs[left][:, rows], refs[right][at : at + count, :])
            out_ref[rows, start : start + total.shape[1]] = total.astype(out_ref.dtype)
            start = start + total.shape[1]


def grads_of(*groups):
    width = groups[0][0][0].shape[1]
    cols = sum(right[0].shape[1] for _, right in groups)
    pieces = []
    plan = []
    for left, right in groups:
        start = len(pieces)
        pieces.extend((*left, *right))
        count = left[0].shape[0]
        fit = right[0].shape[0] // count
        plan.append(
            [
                (start + g, start + len(left) + g // fit, g % fit * count, count)
                for g in range(len(left))
            ]
        )
    return pl.pallas_call(
        functools.partial(grads_kernel, plan),
        out_shape=jax.ShapeDtypeStruct((width, cols), low_type),
        in_specs=[whole_spec()] * len(pieces),
        out_specs=whole_spec(),
        compiler_params=pltpu.CompilerParams(vmem_limit_bytes=VMEM_BYTES),
        cost_estimate=MEDIUM if cols > 1024 else SMALL,
    )(*pieces)


def slots_kernel(cols, slot_count, block_ref, *refs):
    *parts, out, held = refs
    rows = held.shape[0]
    start = 0
    for part in parts:
        held[:, start : start + part.shape[1]] = part[...]
        start = start + part.shape[1]
    for s in range(block_ref.shape[0]):
        block = block_ref[s]
        lanes = pl.ds(pl.multiple_of(jnp.maximum(block, 0) * cols, cols), cols)
        taken = held[:, lanes]
        at = s % slot_count * rows
        out[s // slot_count, at : at + rows, :] = jnp.where(block >= 0, taken, jnp.zeros_like(taken))


def to_slots(block_of, slot_count, cols, *parts):
    count = block_of.shape[0] // slot_count
    rows = parts[0].shape[0]
    width = sum(part.shape[1] for part in parts)
    return pl.pallas_call(
        functools.partial(slots_kernel, cols, slot_count),
        out_shape=jax.ShapeDtypeStruct((count, slot_count * rows, cols), low_type),
        in_specs=[pl.BlockSpec(memory_space=pltpu.SMEM)] + [whole_spec()] * len(parts),
        out_specs=whole_spec(),
        scratch_shapes=[pltpu.VMEM((rows, width), low_type)],
        compiler_params=pltpu.CompilerParams(vmem_limit_bytes=VMEM_BYTES),
        cost_estimate=SMALL,
    )(block_of, *parts)


def choose_kernel(cols, split, block_ref, first_ref, second_ref, *outs):
    for s, out in enumerate(outs):
        block = block_ref[s]

        @pl.when(block < 0)
        def _():
            out[...] = jnp.zeros_like(out)

        @pl.when((block >= 0) & (block < split))
        def _():
            lanes = pl.multiple_of(jnp.clip(block, 0, split - 1) * cols, cols)
            out[...] = first_ref[:, pl.ds(lanes, cols)]

        @pl.when(block >= split)
        def _():
            lanes = pl.multiple_of(jnp.maximum(block - split, 0) * cols, cols)
            out[...] = second_ref[:, pl.ds(lanes, cols)]


def choose_blocks(block_of, cols, first, second):
    slot_count = block_of.shape[0]
    return pl.pallas_call(
        functools.partial(choose_kernel, cols, 4),
        out_shape=tuple(
            [jax.ShapeDtypeStruct((first.shape[0], cols), low_type) for _ in range(slot_count)]
        ),
        in_specs=[pl.BlockSpec(memory_space=pltpu.SMEM), whole_spec(), whole_spec()],
        out_specs=tuple([whole_spec()] * slot_count),
        compiler_params=pltpu.CompilerParams(vmem_limit_bytes=VMEM_BYTES),
        cost_estimate=SMALL,
    )(block_of, first, second)


def precondition_kernel(
    order, place_ref, near_ref, far_ref, left_ref, right_ref, left_root_ref, right_root_ref, *refs
):
    new_left_ref, new_right_ref, direction_ref, square_ref, halfway_ref = refs
    count, parts, rows_part, cols = near_ref.shape
    width = parts * rows_part
    rows = left_ref.shape[1]
    place = place_ref[0]
    pieces = [
        ref[k].reshape(width, cols) for ref in (near_ref, far_ref) for k in range(count)
    ]
    lanes = [pl.ds(pl.multiple_of((place ^ j) * cols, cols), cols) for j in order]
    halfway = 0.0
    for at, piece in zip(lanes, pieces):
        halfway = halfway + dot_nt(piece, right_root_ref[0, :, at].astype(low_type))
    halfway_ref[...] = halfway.astype(low_type)
    total = 0.0
    for t in range(width // TILE):
        here = slice(t * TILE, (t + 1) * TILE)
        part = dot(left_root_ref[0, here, :].astype(low_type), halfway_ref[...])
        direction_ref[0, here, :] = part
        total = total + jnp.sum(part * part, axis=0, keepdims=True)
    square_ref[0] = total
    left = stat_decay * left_ref[0]
    groups = rows // rows_part
    for g, piece in enumerate(pieces):
        ref = near_ref if g < count else far_ref
        own = ref[g % count, pl.ds(place * groups, groups)].reshape(rows, cols)
        left = left + dot_nt(own, piece)
    new_left_ref[0] = left
    for at, piece in zip(lanes, pieces):
        new_right_ref[0, :, at] = stat_decay * right_ref[0, :, at] + dot_tn(pieces[0], piece)


def precondition(place, near, far, stats):
    slot_count, rows, width = stats[0].shape
    count, parts, held_rows, cols = near.shape
    rows_part = held_rows // slot_count
    shape = jax.ShapeDtypeStruct

    def of_slot(dims):
        return pl.BlockSpec((1,) + dims[1:], lambda s: (s, 0, 0))

    pieces_spec = pl.BlockSpec((count, parts, rows_part, cols), lambda s: (0, 0, s, 0))
    return pl.pallas_call(
        functools.partial(precondition_kernel, near_order(lax.axis_size("mp"))),
        grid=(slot_count,),
        out_shape=(
            shape(stats[0].shape, f32),
            shape(stats[1].shape, f32),
            shape((slot_count, width, cols), f32),
            shape((slot_count, 1, cols), f32),
        ),
        in_specs=[pl.BlockSpec(memory_space=pltpu.SMEM), pieces_spec, pieces_spec]
        + [of_slot(array.shape) for array in stats],
        out_specs=(
            of_slot(stats[0].shape),
            of_slot(stats[1].shape),
            of_slot((slot_count, width, cols)),
            of_slot((slot_count, 1, cols)),
        ),
        scratch_shapes=[pltpu.VMEM((width, cols), low_type)],
        compiler_params=pltpu.CompilerParams(vmem_limit_bytes=2 * VMEM_BYTES),
        cost_estimate=MEDIUM,
    )(place, near, far, *stats)


def give_back_kernel(slot_ref, near_ref, far_ref, *refs):
    out_ref = refs[-1]
    half = near_ref.shape[0]
    for t in range(out_ref.shape[1] // TILE):
        here = slice(t * TILE, (t + 1) * TILE)
        total = 0.0
        for start, source in ((0, near_ref), (half, far_ref)):
            wanted = lax.broadcasted_iota(jnp.int32, (TILE, half), 1) + start
            pick = jnp.where(wanted == slot_ref[here, :], 1.0, 0.0).astype(low_type)
            total = total + dot(pick, source[...])
        out_ref[0, here, :] = total.astype(low_type)


def give_back(micro, slots, near, far, micro_count, before):
    rows, width = 2 * near.shape[0], near.shape[1]

    def all_of(dims):
        return pl.BlockSpec(dims, lambda i: (0,) * len(dims))

    return [
        pl.pallas_call(
            give_back_kernel,
            grid=(1,),
            out_shape=jax.ShapeDtypeStruct((micro_count, rows, width), low_type),
            in_specs=[all_of((rows, 1)), all_of(near.shape), all_of(far.shape)]
            + [pl.BlockSpec(memory_space=pl.ANY)] * len(before),
            out_specs=pl.BlockSpec((1, rows, width), lambda i: (micro, 0, 0)),
            input_output_aliases={3 + k: k for k in range(len(before))},
            compiler_params=pltpu.CompilerParams(vmem_limit_bytes=VMEM_BYTES),
            cost_estimate=SMALL,
        )(slots[:, None], near, far, *before)
    ]


def swap(values, axis, bit):
    count = lax.axis_size(axis)
    return lax.ppermute(values, axis, [(i, i ^ bit) for i in range(count)])


def near_order(count):
    found = [0]
    bit = count // 2
    while bit >= 1:
        found = found + [j ^ bit for j in found]
        bit //= 2
    return found


def gather_chips(share):
    bit = lax.axis_size("mp") // 2
    while bit > 1:
        share = jnp.concatenate([share, swap(share, "mp", bit)], axis=0)
        bit //= 2
    return share


def other_core(values):
    return swap(values, "mp", 1)


def scatter_chips(keep, received):
    bit = 2
    count = lax.axis_size("mp")
    if bit == count:
        return keep + received.astype(f32)
    half = keep.shape[0] // 2
    sent = (keep[half:] + received[half:].astype(f32)).astype(low_type)
    got = swap(sent, "mp", bit)
    values = keep[:half] + received[:half].astype(f32)
    bit *= 2
    while bit < count:
        values = values + got.astype(f32)
        half = values.shape[0] // 2
        got = swap(values[half:].astype(low_type), "mp", bit)
        values, got = values[:half], got
        bit *= 2
    return values + got.astype(f32)


def after(values, others):
    return lax.optimization_barrier((values, others))


def together(*values):
    return lax.optimization_barrier(values)


def scatter_step(blocks, bit):
    index = lax.axis_index("dp") // bit % 2
    blocks = blocks.reshape(-1, 2, *blocks.shape[1:])
    mine = lax.dynamic_index_in_dim(blocks, index, 1, keepdims=False)
    other = lax.dynamic_index_in_dim(blocks, 1 - index, 1, keepdims=False)
    got = swap(other.astype(low_type), "dp", bit)
    return mine.astype(f32) + got.astype(f32)


def scatter_grads(blocks, bit):
    while bit < lax.axis_size("dp"):
        blocks = scatter_step(blocks, bit)
        bit *= 2
    return blocks[0].astype(low_type)


def sum_over(values, axis, bit=1):
    while bit < lax.axis_size(axis):
        values = values + swap(values, axis, bit)
        bit *= 2
    return values


def exchange(rows):
    return lax.all_to_all(rows, "dp", split_axis=0, concat_axis=0, tiled=True)


def on_device(
    tokens,
    cotangent,
    lengths,
    placement_ids,
    block_slot_index,
    matrices,
    norm_vectors,
    head_vectors,
    left_stats,
    right_stats,
    left_roots,
    right_roots,
    norm_state,
    head_state,
):
    data_count = lax.axis_size("dp")
    data_index = lax.axis_index("dp")
    model_count = lax.axis_size("mp")
    model_index = lax.axis_index("mp")
    micro_count, rows_here, model_width = tokens.shape
    piece_rows = rows_here // data_count
    sub_rows = piece_rows // model_count
    own_rows = rows_here // model_count
    blocks = matrices.shape[1]
    local_cols = matrices.shape[2]
    shard_rows = matrices.shape[0]
    ffn_count = (blocks - 4) // 2
    ffn_cols = ffn_count * local_cols

    matrices_low = matrices.astype(low_type)
    shipped_one = matrices_low[:, :4, :].reshape(shard_rows, 4 * local_cols)
    shipped_two = matrices_low[:, 4:, :].reshape(shard_rows, 2 * ffn_cols)
    lanes = 128
    norm_columns = jnp.swapaxes(norm_vectors.astype(low_type), 0, 1)
    shipped_one = jnp.concatenate(
        [shipped_one, jnp.pad(norm_columns, ((0, 0), (0, lanes - norm_columns.shape[1])))], axis=1
    )
    placement_ids, shipped_one = together(placement_ids, shipped_one)
    slot_count = left_stats.shape[0]
    all_slots = slot_count * data_count
    slot_match = block_slot_index[None, :] == jnp.arange(all_slots)[:, None]
    filled = jnp.any(slot_match, axis=1)
    block_of = jnp.sum(jnp.where(slot_match, jnp.arange(blocks)[None, :], 0), axis=1)
    block_of = jnp.where(filled, block_of, -1)
    own_blocks = lax.dynamic_slice_in_dim(block_of, data_index * slot_count, slot_count, 0)

    order = jnp.arange(rows_here)
    earlier = (order[:, None] < order[None, :]).astype(low_type)
    device_ids = jnp.arange(data_count)[:, None]
    near = near_order(model_count)
    slots_mine = []
    positions = []
    for micro in range(micro_count):
        dest_all = placement_ids[micro].reshape(data_count, rows_here)
        dest_mine = lax.dynamic_slice_in_dim(dest_all, data_index, 1, 0)
        target = dest_mine // rows_here
        to_each = target == device_ids
        to_me = (dest_all // rows_here) == data_index
        rank_both = dot(jnp.concatenate([to_each, to_me]).astype(low_type), earlier).astype(
            jnp.int32
        )
        rank_out = jnp.sum(jnp.where(to_each, rank_both[:data_count], 0), axis=0)
        slots_mine.append((rank_out, target[0]))
        rank_in = jnp.where(to_me, rank_both[data_count:], -1)
        place = jnp.sum(
            jnp.where(
                rank_in[:, None, :] == jnp.arange(piece_rows)[None, :, None],
                (dest_all - data_index * rows_here)[:, None, :],
                0,
            ),
            axis=2,
        )
        place = place.reshape(data_count, model_count, sub_rows).transpose(1, 0, 2)
        place = place.reshape(model_count, own_rows)[model_index ^ jnp.array(near)]
        positions.append(place.reshape(rows_here))

    def pick_rows(given):
        picked = []
        for micro in range(micro_count):
            rank, target = slots_mine[micro]
            here = (rank // sub_rows) == model_index
            slot = jnp.where(here, target * sub_rows + rank % sub_rows, -1)
            pick = (slot[None, :] == jnp.arange(own_rows)[:, None]).astype(low_type)
            rows = dot(pick, given[micro]).astype(low_type)
            picked.append(rows.reshape(data_count, sub_rows, model_width))
        return jnp.concatenate(picked, axis=1)

    def arrived(picked):
        got = exchange(picked).reshape(data_count, micro_count, sub_rows, model_width)
        return [got[:, i].reshape(own_rows, model_width) for i in range(micro_count)]

    def exchange_back(own):
        sent = [rows.reshape(data_count, 1, sub_rows, model_width) for rows in own]
        sent = jnp.concatenate(sent, axis=1)
        got = exchange(sent.reshape(data_count, -1, model_width))
        got = got.reshape(data_count, len(own), sub_rows, model_width)
        return [got[:, i].reshape(own_rows, model_width) for i in range(len(own))]

    def return_slots(micro):
        rank, target = slots_mine[micro]
        block = jnp.sum(
            jnp.where(
                ((rank // sub_rows) ^ model_index) == jnp.array(near)[:, None],
                jnp.arange(model_count)[:, None],
                0,
            ),
            axis=0,
        )
        return block * own_rows + target * sub_rows + rank % sub_rows

    micros = range(micro_count)
    bounds = [jnp.cumsum(lengths[i, 0]) for i in micros]
    segments = [
        jnp.sum((order[:, None] >= bounds[i][None, :]).astype(jnp.int32), axis=1) for i in micros
    ]
    bias_qkv = jnp.concatenate(
        [head_vectors[0], jnp.zeros((local_cols,), f32), head_vectors[1]]
    )[None]
    bias_up = head_vectors[2:].reshape(1, -1)
    half = rows_here // 2
    halves = (slice(0, half), slice(half, rows_here))

    def attend(i, near, far):
        return attention_forward(
            near, far, norms[:2], weights_one, bias_qkv, positions[i], segments[i]
        )

    def second_share(hidden):
        return layer_norm(hidden, norms[3], norms[4]).astype(low_type)

    def second_back(i, hidden, grad_normed):
        hidden_part, gain_rows = norm_back(hidden, norms[3], grad_normed)
        grad_hidden = grad_out[i] + hidden_part
        sums = [
            jnp.sum(grad_hidden, axis=0),
            jnp.sum(gain_rows, axis=0),
            jnp.sum(grad_normed, axis=0),
            jnp.sum(grad_out[i], axis=0),
        ]
        return grad_hidden, grad_hidden.astype(low_type), jnp.stack(sums)

    def attend_back(i, near, far, kept):
        _, qkv, out, lse = kept
        return attention_backward(
            near, far, weights_one, positions[i], segments[i], qkv, out, lse
        )

    def first_back(i, grad_hidden, grad_normed):
        rows_part, gain_rows = norm_back(rows_own[i], norms[0], grad_normed)
        sums = [jnp.sum(gain_rows, axis=0), jnp.sum(grad_normed, axis=0)]
        return (grad_hidden + rows_part).astype(low_type), jnp.stack(sums)

    picked, shipped_one = together(pick_rows(tokens), shipped_one)
    gathered = lax.all_gather(shipped_one, "dp", axis=0, tiled=True)
    x_0, x_1 = arrived(picked)
    rows_0, rows_1 = x_0.astype(f32), x_1.astype(f32)
    rows_own = (rows_0, rows_1)
    x_0 = gather_chips(x_0)
    x_1 = gather_chips(x_1)
    keep = [(positions[i][:own_rows] < bounds[i][-2])[:, None] for i in micros]
    picked, x_0 = together(pick_rows(cotangent), x_0)
    g_0, g_1 = (jnp.where(k, g, 0).astype(low_type) for g, k in zip(arrived(picked), keep))
    grad_out = (g_0.astype(f32), g_1.astype(f32))
    xf_0 = other_core(x_0)
    xf_1 = other_core(x_1)
    gathered, shipped_two, xf_0, xf_1, g_0, g_1 = together(
        gathered, shipped_two, xf_0, xf_1, g_0, g_1
    )
    weights_one = gathered
    norms = jnp.swapaxes(gathered[:, 4 * local_cols :], 0, 1)[:6].astype(f32)
    weights_two = lax.all_gather(shipped_two, "dp", axis=0, tiled=True)

    keep_0, send_0, normed_0, *kept_0 = attend(0, x_0, xf_0)
    g_0 = gather_chips(g_0)
    keep_0, send_0, g_0, g_1 = together(keep_0, send_0, g_0, g_1)
    core_0, gf_0, g_1 = together(other_core(send_0), other_core(g_0), g_1)
    branch_0 = scatter_chips(keep_0, core_0)
    keep_1, send_1, normed_1, *kept_1 = attend(1, x_1, xf_1)
    g_1 = gather_chips(g_1)
    keep_1, send_1, branch_0, g_1 = together(keep_1, send_1, branch_0, g_1)
    hidden_0 = rows_0 + branch_0 + norms[2]
    z_0, core_1, gf_1 = together(second_share(hidden_0), other_core(send_1), other_core(g_1))
    branch_1 = scatter_chips(keep_1, core_1)
    z_0 = gather_chips(z_0)
    z_0, branch_1, weights_two, gf_0, gf_1 = together(z_0, branch_1, weights_two, gf_0, gf_1)
    hidden_1 = rows_1 + branch_1 + norms[2]
    z_1, z_0 = together(second_share(hidden_1), z_0)

    zf_0 = other_core(z_0)
    near_parts = mlp(z_0, g_0, weights_two, bias_up, f32)
    z_1 = gather_chips(z_1)
    zf_0, near_parts = together(zf_0, near_parts)
    far_parts = mlp(zf_0, gf_0, weights_two, bias_up, low_type)
    active_0, grad_up_0, feed_0, back_0, up_sums_0 = zip(near_parts, far_parts)
    z_1, back_0, feed_0 = together(z_1, back_0, feed_0)
    zf_1 = other_core(z_1)
    core_0 = other_core(back_0[1])
    near_parts = mlp(z_1, g_1, weights_two, bias_up, f32)
    zf_1, core_0, near_parts = together(zf_1, core_0, near_parts)
    back_0 = scatter_chips(back_0[0], core_0)
    core_feed_0 = other_core(feed_0[1])
    far_parts = mlp(zf_1, gf_1, weights_two, bias_up, low_type)
    active_1, grad_up_1, feed_1, back_1, up_sums_1 = zip(near_parts, far_parts)
    back_0, back_1, feed_1, core_feed_0 = together(back_0, back_1, feed_1, core_feed_0)
    hidden_grad_0, h_0, second_sums_0 = second_back(0, hidden_0, back_0)
    h_0, grad_up_1, back_1 = together(h_0, grad_up_1, back_1)
    h_0 = gather_chips(h_0)
    grads_two = grads_of(
        ([z_0, zf_0, z_1, zf_1], [*grad_up_0, *grad_up_1]),
        ([g_0, gf_0, g_1, gf_1], [*active_0, *active_1]),
    )
    core_1 = other_core(back_1[1])
    grads_two, h_0, core_1, core_feed_0 = together(grads_two, h_0, core_1, core_feed_0)
    summed_two = lax.psum_scatter(grads_two, "dp", scatter_dimension=0, tiled=True)
    chosen = choose_blocks(own_blocks, local_cols, weights_one, weights_two)
    hf_0, chosen, core_1, core_feed_0 = together(other_core(h_0), chosen, core_1, core_feed_0)

    back_1 = scatter_chips(back_1[0], core_1)
    output_0 = scatter_chips(feed_0[0], core_feed_0)
    keep_0, send_0, grad_qkv_0, sums_0 = attend_back(0, h_0, hf_0, kept_0)
    core_feed_1 = other_core(feed_1[1])
    keep_0, send_0, back_1, output_0, core_feed_1 = together(
        keep_0, send_0, back_1, output_0, core_feed_1
    )
    hidden_grad_1, h_1, second_sums_1 = second_back(1, hidden_1, back_1)
    h_1, keep_0, send_0, output_0 = together(h_1, keep_0, send_0, output_0)
    h_1 = gather_chips(h_1)
    core_0 = other_core(send_0)
    output_0 = (hidden_0 + output_0 + norms[5]).astype(low_type)
    h_1, core_0, output_0, core_feed_1 = together(h_1, core_0, output_0, core_feed_1)
    output_0 = exchange_back([output_0])[0]
    hf_1, core_0, core_feed_1 = together(other_core(h_1), core_0, core_feed_1)
    normed_back_0 = scatter_chips(keep_0, core_0)
    output_1 = scatter_chips(feed_1[0], core_feed_1)
    grads_out = grads_of(([h_0, hf_0, h_1, hf_1], [kept_0[0], kept_1[0]]))
    hf_1, grads_out = together(hf_1, grads_out)
    blocks_out = scatter_step(grads_out.reshape(data_count, shard_rows, local_cols), 1)
    keep_1, send_1, grad_qkv_1, sums_1 = attend_back(1, h_1, hf_1, kept_1)
    keep_1, send_1, normed_back_0, output_1, output_0, summed_two, blocks_out = together(
        keep_1, send_1, normed_back_0, output_1, output_0, summed_two, blocks_out
    )
    core_1 = other_core(send_1)
    grads_qkv = grads_of(([normed_0, normed_1], [grad_qkv_0, grad_qkv_1]))
    core_1, grads_qkv = together(core_1, grads_qkv)
    normed_back_1 = scatter_chips(keep_1, core_1)
    input_0, first_sums_0 = first_back(0, hidden_grad_0, normed_back_0)
    output_1 = (hidden_1 + output_1 + norms[5]).astype(low_type)
    input_0, output_1 = exchange_back([input_0, output_1])
    cut = 3 * local_cols // 2 // 128 * 128
    grads_one = [
        scatter_step(part.reshape(data_count, shard_rows, -1), 1)
        for part in (grads_qkv[:, :cut], grads_qkv[:, cut:])
    ]
    blocks_out = scatter_step(blocks_out, 2)
    output_0 = gather_chips(output_0)
    normed_back_1, grads_one, input_0, output_1, output_0, blocks_out = together(
        normed_back_1, grads_one, input_0, output_1, output_0, blocks_out
    )
    input_0, output_1 = gather_chips(input_0), gather_chips(output_1)
    input_1, first_sums_1 = first_back(1, hidden_grad_1, normed_back_1)
    summed_one = [scatter_grads(part, 2) for part in (*grads_one,)]
    summed_one.append(scatter_grads(blocks_out, 4))
    norm_grads_own = jnp.concatenate(
        [first_sums_0 + first_sums_1, second_sums_0 + second_sums_1], axis=0
    )
    qkv_sums = sums_0 + sums_1
    up_sums = [*up_sums_0, *up_sums_1]

    summed_one, input_1, norm_grads_own = together(summed_one, input_1, norm_grads_own)
    owned = exchange(
        to_slots(block_of, slot_count, local_cols, *summed_one, summed_two)
    )
    stats = (left_stats, right_stats, left_roots, right_roots)
    place = model_index.astype(jnp.int32).reshape(1)
    returns = [return_slots(i) for i in micros]
    outputs_given = give_back(0, returns[0], output_0, other_core(output_0), micro_count, [])
    inputs_given = give_back(0, returns[0], input_0, other_core(input_0), micro_count, [])
    outputs_given = give_back(
        1, returns[1], output_1, other_core(output_1), micro_count, outputs_given
    )
    norm_grads_sum = sum_over(norm_grads_own, "mp")
    owned, outputs_given, inputs_given, norm_grads_sum, input_1 = together(
        owned, outputs_given, inputs_given, norm_grads_sum, input_1
    )
    input_1 = exchange_back([input_1])[0]
    head_own = jnp.concatenate(
        [
            qkv_sums[:, :local_cols],
            qkv_sums[:, 2 * local_cols :],
            sum(up_sums).reshape(ffn_count, local_cols),
        ],
        axis=0,
    )
    vectors = jnp.concatenate([norm_grads_sum, head_own], axis=1)
    owned_grads = owned.reshape(data_count, slot_count, shard_rows, local_cols)
    owned_grads = jnp.swapaxes(owned_grads, 1, 2).reshape(model_width, slot_count, local_cols)
    owned_grads = owned_grads.astype(f32)
    near_part = gather_chips(owned[None])
    near_part, input_1, owned_grads = together(near_part, input_1, owned_grads)
    far_part = other_core(near_part)
    new_left, new_right, directions, squares = precondition(place, near_part, far_part, stats)
    squares, input_1, vectors = together(squares, input_1, vectors)
    input_1 = gather_chips(input_1)
    vectors = sum_over(vectors, "dp")
    inputs_given = give_back(
        1, returns[1], input_1, other_core(input_1), micro_count, inputs_given
    )[0]
    outputs_given = outputs_given[0]
    norm_all = vectors[:, :model_width]
    head_total = vectors[:, model_width:]
    norm_cols = norm_vectors.shape[1]
    norm_total = lax.dynamic_slice_in_dim(norm_all, data_index * norm_cols, norm_cols, 1)
    squares = jnp.sum(squares, axis=(1, 2))
    square_total = sum_over(squares.reshape(1, slot_count), "mp")[0]
    factor = lax.rsqrt(square_total / (model_width * model_width) + mean_eps)
    updated_blocks = jnp.stack(
        [
            chosen[s].astype(f32) - matrix_rate * factor[s] * directions[s]
            for s in range(slot_count)
        ],
        axis=1,
    )
    new_norm_state = stat_decay * norm_state + norm_total * norm_total
    new_norm_vectors = norm_vectors - vector_rate * norm_total / (
        jnp.sqrt(new_norm_state) + diag_eps
    )
    new_head_state = stat_decay * head_state + head_total * head_total
    new_head_vectors = head_vectors - vector_rate * head_total / (
        jnp.sqrt(new_head_state) + diag_eps
    )
    return (
        outputs_given,
        inputs_given,
        owned_grads,
        new_left,
        new_right,
        updated_blocks,
        norm_total,
        new_norm_state,
        new_norm_vectors,
        head_total,
        new_head_state,
        new_head_vectors,
    )


def solution(mesh):
    placed = (
        P(None, "dp", None),
        P(None, "dp", None),
        P(None, "dp", None),
        P(),
        P(),
        P("dp", None, "mp"),
        P(None, "dp"),
        P(None, "mp"),
        P("dp", "mp", None),
        P("dp", "mp", None),
        P("dp", None, None),
        P("dp", "mp", None),
        P(None, "dp"),
        P(None, "mp"),
    )
    return jax.shard_map(
        on_device,
        mesh=mesh,
        in_specs=placed,
        out_specs=(
            P(None, "dp", None),
            P(None, "dp", None),
            P(None, "dp", "mp"),
            P("dp", "mp", None),
            P("dp", "mp", None),
            P(None, "dp", "mp"),
            P(None, "dp"),
            P(None, "dp"),
            P(None, "dp"),
            P(None, "mp"),
            P(None, "mp"),
            P(None, "mp"),
        ),
        check_vma=False,
    )
```

```python
import functools
import math

import jax
import jax.numpy as jnp
from jax import lax
from jax.experimental import pallas as pl
from jax.experimental.pallas import tpu as pltpu
from jax.sharding import PartitionSpec as P

HEAD_DIM = 64


stat_decay = 0.5
matrix_rate = 0.02
vector_rate = 0.3
norm_eps = 1e-05
mean_eps = 1e-06
diag_eps = 1e-08
masked_score = -1000000000.0

f32 = jnp.float32
low_type = jnp.bfloat16


def unit_rows_of(values):
    center = values - jnp.mean(values, axis=-1, keepdims=True)
    spread = jnp.mean(center * center, axis=-1, keepdims=True)
    scale_rows = lax.rsqrt(spread + norm_eps)
    return center * scale_rows, scale_rows


def layer_norm(values, gain, shift):
    unit_rows, _ = unit_rows_of(values)
    return unit_rows * gain + shift


def norm_back(values, gain, grad_normed):
    unit_rows, scale_rows = unit_rows_of(values)
    grad_unit = grad_normed * gain
    grad_values = scale_rows * (
        grad_unit
        - jnp.mean(grad_unit, axis=-1, keepdims=True)
        - unit_rows * jnp.mean(grad_unit * unit_rows, axis=-1, keepdims=True)
    )
    return (grad_values, grad_normed * unit_rows)


def dot(left, right):
    return lax.dot_general(left, right, (((1,), (0,)), ((), ())), preferred_element_type=f32)


def dot_nt(left, right):
    return lax.dot_general(left, right, (((1,), (1,)), ((), ())), preferred_element_type=f32)


def dot_tn(left, right):
    return lax.dot_general(left, right, (((0,), (0,)), ((), ())), preferred_element_type=f32)


TILE = 256
STRIP = 64
VMEM_BYTES = 28 * 1024 * 1024
SMALL = pl.CostEstimate(flops=10**9, bytes_accessed=10**6, transcendentals=0)
LARGE = pl.CostEstimate(flops=20 * 10**9, bytes_accessed=10**6, transcendentals=0)
MEDIUM = pl.CostEstimate(flops=11 * 10**9, bytes_accessed=10**6, transcendentals=0)

def whole_spec():
    return pl.BlockSpec(memory_space=pltpu.VMEM)

def attention_forward_kernel(
    near_ref, far_ref, norm_ref, weights_ref, bias_ref,
    place_row_ref, place_col_ref, seg_row_ref, seg_col_ref,
    keep_ref, send_ref, normed_ref, attended_ref, qkv_ref, out_ref, lse_ref,
    arrived,
):
    rows = arrived.shape[0]
    half = rows // 2
    cols = attended_ref.shape[1]
    heads = cols // HEAD_DIM
    scale = 1.0 / math.sqrt(HEAD_DIM)
    tiles = rows // TILE
    for start, source in ((0, near_ref), (half, far_ref)):

        def norm_some(i, carry):
            values = source[pl.ds(pl.multiple_of(i * STRIP, STRIP), STRIP), :].astype(f32)
            normed = layer_norm(values, norm_ref[0:1, :], norm_ref[1:2, :])
            normed_ref[pl.ds(pl.multiple_of(start + i * STRIP, STRIP), STRIP), :] = (
                normed.astype(low_type)
            )
            return carry

        lax.fori_loop(0, half // STRIP, norm_some, 0)
    for t in range(tiles):
        part = normed_ref[pl.ds(t * TILE, TILE), :]
        arrived[pl.ds(t * TILE, TILE), :] = (
            dot(part, weights_ref[:, : 3 * cols]) + bias_ref[...]
        ).astype(low_type)
    for t in range(tiles):
        wanted = lax.broadcasted_iota(jnp.int32, (TILE, rows), 0) + t * TILE
        pick = jnp.where(wanted == place_row_ref[...], 1.0, 0.0).astype(low_type)
        qkv_ref[pl.ds(t * TILE, TILE), :] = dot(pick, arrived[...]).astype(low_type)
    for h in range(heads):
        lanes = slice(h * HEAD_DIM, (h + 1) * HEAD_DIM)
        key_lanes = slice(cols + h * HEAD_DIM, cols + (h + 1) * HEAD_DIM)
        value_lanes = slice(2 * cols + h * HEAD_DIM, 2 * cols + (h + 1) * HEAD_DIM)
        for t in range(tiles):
            here = slice(t * TILE, (t + 1) * TILE)
            query = qkv_ref[here, lanes] * jnp.asarray(scale, low_type)
            seg_q = seg_col_ref[here, :]
            scores = []
            top = None
            for c in range(t + 1):
                there = slice(c * TILE, (c + 1) * TILE)
                s = dot_nt(query, qkv_ref[there, key_lanes])
                allowed = seg_q == seg_row_ref[:, there]
                if c == t:
                    allowed = allowed & (
                        lax.broadcasted_iota(jnp.int32, (TILE, TILE), 0)
                        >= lax.broadcasted_iota(jnp.int32, (TILE, TILE), 1)
                    )
                s = jnp.where(allowed, s, masked_score)
                scores.append(s)
                m = jnp.max(s, axis=1, keepdims=True)
                top = m if top is None else jnp.maximum(top, m)
            total = 0.0
            out = 0.0
            for c in range(t + 1):
                there = slice(c * TILE, (c + 1) * TILE)
                e = jnp.exp(scores[c] - top)
                total = total + jnp.sum(e, axis=1, keepdims=True)
                out = out + dot(e.astype(low_type), qkv_ref[there, value_lanes])
            out_ref[here, lanes] = (out / total).astype(low_type)
            lse_ref[here, h : h + 1] = top + jnp.log(total)
    for t in range(tiles):
        wanted = lax.broadcasted_iota(jnp.int32, (TILE, rows), 1)
        pick = jnp.where(wanted == place_col_ref[pl.ds(t * TILE, TILE), :], 1.0, 0.0).astype(low_type)
        part = dot(pick, out_ref[...]).astype(low_type)
        attended_ref[pl.ds(t * TILE, TILE), :] = part
        branch = dot_nt(part, weights_ref[:, 3 * cols : 4 * cols])
        if t * TILE < half:
            keep_ref[pl.ds(t * TILE, TILE), :] = branch
        else:
            send_ref[pl.ds(t * TILE - half, TILE), :] = branch.astype(low_type)

def attention_forward(near, far, norms, weights, bias, place, segment):
    rows = 2 * near.shape[0]
    width = near.shape[1]
    cols = bias.shape[1] // 3
    heads = cols // HEAD_DIM
    shape = jax.ShapeDtypeStruct
    return pl.pallas_call(
        attention_forward_kernel,
        out_shape=(
            shape((rows // 2, width), f32),
            shape((rows // 2, width), low_type),
            shape((rows, width), low_type),
            shape((rows, cols), low_type),
            shape((rows, 3 * cols), low_type),
            shape((rows, cols), low_type),
            shape((rows, heads), f32),
        ),
        in_specs=[whole_spec()] * 9,
        out_specs=tuple([whole_spec()] * 7),
        scratch_shapes=[pltpu.VMEM((rows, 3 * cols), low_type)],
        compiler_params=pltpu.CompilerParams(vmem_limit_bytes=VMEM_BYTES),
        cost_estimate=LARGE,
    )(near, far, norms, weights, bias, place[None, :], place[:, None], segment[None, :], segment[:, None])

def attention_backward_kernel(
    near_ref, far_ref, weights_ref, place_row_ref, place_col_ref, seg_row_ref, seg_col_ref,
    qkv_ref, out_ref, lse_ref,
    keep_ref, send_ref, grads_ref, sums_ref,
    arrived, placed, grad_key, grad_value, moved,
):
    rows = arrived.shape[0]
    half = rows // 2
    cols = out_ref.shape[1]
    heads = cols // HEAD_DIM
    scale = 1.0 / math.sqrt(HEAD_DIM)
    tiles = rows // TILE
    for t in range(tiles):
        source = near_ref if t * TILE < half else far_ref
        part = source[pl.ds(t * TILE % half, TILE), :]
        arrived[pl.ds(t * TILE, TILE), :] = dot(
            part, weights_ref[:, 3 * cols : 4 * cols]
        ).astype(low_type)
    for t in range(tiles):
        wanted = lax.broadcasted_iota(jnp.int32, (TILE, rows), 0) + t * TILE
        pick = jnp.where(wanted == place_row_ref[...], 1.0, 0.0).astype(low_type)
        placed[pl.ds(t * TILE, TILE), :] = dot(pick, arrived[...]).astype(low_type)
    for h in range(heads):
        lanes = slice(h * HEAD_DIM, (h + 1) * HEAD_DIM)
        key_lanes = slice(cols + h * HEAD_DIM, cols + (h + 1) * HEAD_DIM)
        value_lanes = slice(2 * cols + h * HEAD_DIM, 2 * cols + (h + 1) * HEAD_DIM)
        grad_key[...] = jnp.zeros_like(grad_key)
        grad_value[...] = jnp.zeros_like(grad_value)
        for t in range(tiles):
            here = slice(t * TILE, (t + 1) * TILE)
            query = qkv_ref[here, lanes] * jnp.asarray(scale, low_type)
            grad = placed[here, lanes]
            row_total = jnp.sum(grad.astype(f32) * out_ref[here, lanes].astype(f32), axis=1, keepdims=True)
            seg_q = seg_col_ref[here, :]
            lse = lse_ref[here, h : h + 1]
            grad_query = 0.0
            for c in range(t + 1):
                there = slice(c * TILE, (c + 1) * TILE)
                key = qkv_ref[there, key_lanes]
                s = dot_nt(query, key)
                allowed = seg_q == seg_row_ref[:, there]
                if c == t:
                    allowed = allowed & (
                        lax.broadcasted_iota(jnp.int32, (TILE, TILE), 0)
                        >= lax.broadcasted_iota(jnp.int32, (TILE, TILE), 1)
                    )
                p = jnp.where(allowed, jnp.exp(s - lse), 0.0)
                dp = dot_nt(grad, qkv_ref[there, value_lanes])
                ds = (p * (dp - row_total)).astype(low_type)
                grad_query = grad_query + dot(ds, key)
                grad_key[there, :] += dot_tn(ds, query)
                grad_value[there, :] += dot_tn(p.astype(low_type), grad)
            moved[here, lanes] = (grad_query * scale).astype(low_type)
        moved[:, key_lanes] = grad_key[...].astype(low_type)
        moved[:, value_lanes] = grad_value[...].astype(low_type)
    sums_ref[...] = jnp.sum(moved[...].astype(f32), axis=0, keepdims=True)
    for t in range(tiles):
        wanted = lax.broadcasted_iota(jnp.int32, (TILE, rows), 1)
        pick = jnp.where(wanted == place_col_ref[pl.ds(t * TILE, TILE), :], 1.0, 0.0).astype(low_type)
        part = dot(pick, moved[...]).astype(low_type)
        grads_ref[pl.ds(t * TILE, TILE), :] = part
        normed = dot_nt(part, weights_ref[:, : 3 * cols])
        if t * TILE < half:
            keep_ref[pl.ds(t * TILE, TILE), :] = normed
        else:
            send_ref[pl.ds(t * TILE - half, TILE), :] = normed.astype(low_type)

def attention_backward(near, far, weights, place, segment, qkv, out, lse):
    rows = 2 * near.shape[0]
    width = near.shape[1]
    cols = out.shape[1]
    heads = cols // HEAD_DIM
    shape = jax.ShapeDtypeStruct
    return pl.pallas_call(
        attention_backward_kernel,
        out_shape=(
            shape((rows // 2, width), f32),
            shape((rows // 2, width), low_type),
            shape((rows, 3 * cols), low_type),
            shape((1, 3 * cols), f32),
        ),
        in_specs=[whole_spec()] * 10,
        out_specs=tuple([whole_spec()] * 4),
        scratch_shapes=[
            pltpu.VMEM((rows, cols), low_type),
            pltpu.VMEM((rows, cols), low_type),
            pltpu.VMEM((rows, HEAD_DIM), f32),
            pltpu.VMEM((rows, HEAD_DIM), f32),
            pltpu.VMEM((rows, 3 * cols), low_type),
        ],
        compiler_params=pltpu.CompilerParams(vmem_limit_bytes=VMEM_BYTES),
        cost_estimate=LARGE,
    )(near, far, weights, place[None, :], place[:, None], segment[None, :], segment[:, None], qkv, out, lse)

def mlp_kernel(normed_ref, grad_ref, weights_ref, bias_ref, active_ref, grad_up_ref, feed_ref, back_ref, sums_ref):
    rows, width = normed_ref.shape
    cols = bias_ref.shape[1]
    step = TILE
    total = 0.0
    c0 = math.sqrt(2.0 / math.pi)
    for t in range(rows // step):
        here = slice(t * step, (t + 1) * step)
        pre = dot(normed_ref[here, :], weights_ref[:, :cols]) + bias_ref[...]
        square = pre * pre
        bent = jnp.tanh(c0 * (pre + 0.044715 * (square * pre)))
        active_ref[here, :] = (0.5 * pre * (1.0 + bent)).astype(low_type)
        slope = 0.5 * (1.0 + bent) + 0.5 * pre * (1.0 - bent * bent) * (c0 * (1.0 + 0.134145 * square))
        grad = dot(grad_ref[here, :], weights_ref[:, cols:]) * slope
        grad_low = grad.astype(low_type)
        grad_up_ref[here, :] = grad_low
        total = total + jnp.sum(grad_low.astype(f32), axis=0, keepdims=True)
    sums_ref[...] = total
    for t in range(rows // step):
        here = slice(t * step, (t + 1) * step)
        back_ref[here, :] = dot_nt(grad_up_ref[here, :], weights_ref[:, :cols]).astype(back_ref.dtype)
        feed_ref[here, :] = dot_nt(active_ref[here, :], weights_ref[:, cols:]).astype(feed_ref.dtype)

def mlp(normed, grad, weights, bias, kind):
    rows, width = normed.shape
    cols = bias.shape[1]
    shape = jax.ShapeDtypeStruct
    return pl.pallas_call(
        mlp_kernel,
        out_shape=(
            shape((rows, cols), low_type),
            shape((rows, cols), low_type),
            shape((rows, width), kind),
            shape((rows, width), kind),
            shape((1, cols), f32),
        ),
        in_specs=[whole_spec()] * 4,
        out_specs=tuple([whole_spec()] * 5),
        compiler_params=pltpu.CompilerParams(vmem_limit_bytes=VMEM_BYTES),
        cost_estimate=MEDIUM,
    )(normed, grad, weights, bias)


def grads_kernel(groups, *refs):
    out_ref = refs[-1]
    for t in range(out_ref.shape[0] // TILE):
        rows = slice(t * TILE, (t + 1) * TILE)
        start = 0
        for group in groups:
            total = 0.0
            for left, right, at, count in group:
                total = total + dot_tn(refs[left][:, rows], refs[right][at : at + count, :])
            out_ref[rows, start : start + total.shape[1]] = total.astype(out_ref.dtype)
            start = start + total.shape[1]


def grads_of(*groups):
    width = groups[0][0][0].shape[1]
    cols = sum(right[0].shape[1] for _, right in groups)
    pieces = []
    plan = []
    for left, right in groups:
        start = len(pieces)
        pieces.extend((*left, *right))
        count = left[0].shape[0]
        fit = right[0].shape[0] // count
        plan.append(
            [
                (start + g, start + len(left) + g // fit, g % fit * count, count)
                for g in range(len(left))
            ]
        )
    return pl.pallas_call(
        functools.partial(grads_kernel, plan),
        out_shape=jax.ShapeDtypeStruct((width, cols), low_type),
        in_specs=[whole_spec()] * len(pieces),
        out_specs=whole_spec(),
        compiler_params=pltpu.CompilerParams(vmem_limit_bytes=VMEM_BYTES),
        cost_estimate=MEDIUM if cols > 1024 else SMALL,
    )(*pieces)


def slots_kernel(cols, slot_count, block_ref, *refs):
    *parts, out, held = refs
    rows = held.shape[0]
    start = 0
    for part in parts:
        held[:, start : start + part.shape[1]] = part[...]
        start = start + part.shape[1]
    for s in range(block_ref.shape[0]):
        block = block_ref[s]
        lanes = pl.ds(pl.multiple_of(jnp.maximum(block, 0) * cols, cols), cols)
        taken = held[:, lanes]
        at = s % slot_count * rows
        out[s // slot_count, at : at + rows, :] = jnp.where(block >= 0, taken, jnp.zeros_like(taken))


def to_slots(block_of, slot_count, cols, *parts):
    count = block_of.shape[0] // slot_count
    rows = parts[0].shape[0]
    width = sum(part.shape[1] for part in parts)
    return pl.pallas_call(
        functools.partial(slots_kernel, cols, slot_count),
        out_shape=jax.ShapeDtypeStruct((count, slot_count * rows, cols), low_type),
        in_specs=[pl.BlockSpec(memory_space=pltpu.SMEM)] + [whole_spec()] * len(parts),
        out_specs=whole_spec(),
        scratch_shapes=[pltpu.VMEM((rows, width), low_type)],
        compiler_params=pltpu.CompilerParams(vmem_limit_bytes=VMEM_BYTES),
        cost_estimate=SMALL,
    )(block_of, *parts)


def choose_kernel(cols, split, block_ref, first_ref, second_ref, *outs):
    for s, out in enumerate(outs):
        block = block_ref[s]

        @pl.when(block < 0)
        def _():
            out[...] = jnp.zeros_like(out)

        @pl.when((block >= 0) & (block < split))
        def _():
            lanes = pl.multiple_of(jnp.clip(block, 0, split - 1) * cols, cols)
            out[...] = first_ref[:, pl.ds(lanes, cols)]

        @pl.when(block >= split)
        def _():
            lanes = pl.multiple_of(jnp.maximum(block - split, 0) * cols, cols)
            out[...] = second_ref[:, pl.ds(lanes, cols)]


def choose_blocks(block_of, cols, first, second):
    slot_count = block_of.shape[0]
    return pl.pallas_call(
        functools.partial(choose_kernel, cols, 4),
        out_shape=tuple(
            [jax.ShapeDtypeStruct((first.shape[0], cols), low_type) for _ in range(slot_count)]
        ),
        in_specs=[pl.BlockSpec(memory_space=pltpu.SMEM), whole_spec(), whole_spec()],
        out_specs=tuple([whole_spec()] * slot_count),
        compiler_params=pltpu.CompilerParams(vmem_limit_bytes=VMEM_BYTES),
        cost_estimate=SMALL,
    )(block_of, first, second)


def precondition_kernel(
    order, place_ref, near_ref, far_ref, left_ref, right_ref, left_root_ref, right_root_ref, *refs
):
    new_left_ref, new_right_ref, direction_ref, square_ref, halfway_ref = refs
    count, parts, rows_part, cols = near_ref.shape
    width = parts * rows_part
    rows = left_ref.shape[1]
    place = place_ref[0]
    pieces = [
        ref[k].reshape(width, cols) for ref in (near_ref, far_ref) for k in range(count)
    ]
    lanes = [pl.ds(pl.multiple_of((place ^ j) * cols, cols), cols) for j in order]
    halfway = 0.0
    for at, piece in zip(lanes, pieces):
        halfway = halfway + dot_nt(piece, right_root_ref[0, :, at].astype(low_type))
    halfway_ref[...] = halfway.astype(low_type)
    total = 0.0
    for t in range(width // TILE):
        here = slice(t * TILE, (t + 1) * TILE)
        part = dot(left_root_ref[0, here, :].astype(low_type), halfway_ref[...])
        direction_ref[0, here, :] = part
        total = total + jnp.sum(part * part, axis=0, keepdims=True)
    square_ref[0] = total
    left = stat_decay * left_ref[0]
    groups = rows // rows_part
    for g, piece in enumerate(pieces):
        ref = near_ref if g < count else far_ref
        own = ref[g % count, pl.ds(place * groups, groups)].reshape(rows, cols)
        left = left + dot_nt(own, piece)
    new_left_ref[0] = left
    for at, piece in zip(lanes, pieces):
        new_right_ref[0, :, at] = stat_decay * right_ref[0, :, at] + dot_tn(pieces[0], piece)


def precondition(place, near, far, stats):
    slot_count, rows, width = stats[0].shape
    count, parts, held_rows, cols = near.shape
    rows_part = held_rows // slot_count
    shape = jax.ShapeDtypeStruct

    def of_slot(dims):
        return pl.BlockSpec((1,) + dims[1:], lambda s: (s, 0, 0))

    pieces_spec = pl.BlockSpec((count, parts, rows_part, cols), lambda s: (0, 0, s, 0))
    return pl.pallas_call(
        functools.partial(precondition_kernel, near_order(lax.axis_size("mp"))),
        grid=(slot_count,),
        out_shape=(
            shape(stats[0].shape, f32),
            shape(stats[1].shape, f32),
            shape((slot_count, width, cols), f32),
            shape((slot_count, 1, cols), f32),
        ),
        in_specs=[pl.BlockSpec(memory_space=pltpu.SMEM), pieces_spec, pieces_spec]
        + [of_slot(array.shape) for array in stats],
        out_specs=(
            of_slot(stats[0].shape),
            of_slot(stats[1].shape),
            of_slot((slot_count, width, cols)),
            of_slot((slot_count, 1, cols)),
        ),
        scratch_shapes=[pltpu.VMEM((width, cols), low_type)],
        compiler_params=pltpu.CompilerParams(vmem_limit_bytes=2 * VMEM_BYTES),
        cost_estimate=MEDIUM,
    )(place, near, far, *stats)


def give_back_kernel(slot_ref, near_ref, far_ref, *refs):
    out_ref = refs[-1]
    half = near_ref.shape[0]
    for t in range(out_ref.shape[1] // TILE):
        here = slice(t * TILE, (t + 1) * TILE)
        total = 0.0
        for start, source in ((0, near_ref), (half, far_ref)):
            wanted = lax.broadcasted_iota(jnp.int32, (TILE, half), 1) + start
            pick = jnp.where(wanted == slot_ref[here, :], 1.0, 0.0).astype(low_type)
            total = total + dot(pick, source[...])
        out_ref[0, here, :] = total.astype(low_type)


def give_back(micro, slots, near, far, micro_count, before):
    rows, width = 2 * near.shape[0], near.shape[1]

    def all_of(dims):
        return pl.BlockSpec(dims, lambda i: (0,) * len(dims))

    return [
        pl.pallas_call(
            give_back_kernel,
            grid=(1,),
            out_shape=jax.ShapeDtypeStruct((micro_count, rows, width), low_type),
            in_specs=[all_of((rows, 1)), all_of(near.shape), all_of(far.shape)]
            + [pl.BlockSpec(memory_space=pl.ANY)] * len(before),
            out_specs=pl.BlockSpec((1, rows, width), lambda i: (micro, 0, 0)),
            input_output_aliases={3 + k: k for k in range(len(before))},
            compiler_params=pltpu.CompilerParams(vmem_limit_bytes=VMEM_BYTES),
            cost_estimate=SMALL,
        )(slots[:, None], near, far, *before)
    ]


def swap(values, axis, bit):
    count = lax.axis_size(axis)
    return lax.ppermute(values, axis, [(i, i ^ bit) for i in range(count)])


def near_order(count):
    found = [0]
    bit = count // 2
    while bit >= 1:
        found = found + [j ^ bit for j in found]
        bit //= 2
    return found


def gather_chips(share):
    bit = lax.axis_size("mp") // 2
    while bit > 1:
        share = jnp.concatenate([share, swap(share, "mp", bit)], axis=0)
        bit //= 2
    return share


def other_core(values):
    return swap(values, "mp", 1)


def scatter_chips(keep, received):
    bit = 2
    count = lax.axis_size("mp")
    if bit == count:
        return keep + received.astype(f32)
    half = keep.shape[0] // 2
    sent = (keep[half:] + received[half:].astype(f32)).astype(low_type)
    got = swap(sent, "mp", bit)
    values = keep[:half] + received[:half].astype(f32)
    bit *= 2
    while bit < count:
        values = values + got.astype(f32)
        half = values.shape[0] // 2
        got = swap(values[half:].astype(low_type), "mp", bit)
        values, got = values[:half], got
        bit *= 2
    return values + got.astype(f32)


def after(values, others):
    return lax.optimization_barrier((values, others))


def together(*values):
    return lax.optimization_barrier(values)


def scatter_step(blocks, bit):
    index = lax.axis_index("dp") // bit % 2
    blocks = blocks.reshape(-1, 2, *blocks.shape[1:])
    mine = lax.dynamic_index_in_dim(blocks, index, 1, keepdims=False)
    other = lax.dynamic_index_in_dim(blocks, 1 - index, 1, keepdims=False)
    got = swap(other.astype(low_type), "dp", bit)
    return mine.astype(f32) + got.astype(f32)


def scatter_grads(blocks, bit):
    while bit < lax.axis_size("dp"):
        blocks = scatter_step(blocks, bit)
        bit *= 2
    return blocks[0].astype(low_type)


def sum_over(values, axis, bit=1):
    while bit < lax.axis_size(axis):
        values = values + swap(values, axis, bit)
        bit *= 2
    return values


def exchange(rows):
    return lax.all_to_all(rows, "dp", split_axis=0, concat_axis=0, tiled=True)


def on_device(
    tokens,
    cotangent,
    lengths,
    placement_ids,
    block_slot_index,
    matrices,
    norm_vectors,
    head_vectors,
    left_stats,
    right_stats,
    left_roots,
    right_roots,
    norm_state,
    head_state,
):
    data_count = lax.axis_size("dp")
    data_index = lax.axis_index("dp")
    model_count = lax.axis_size("mp")
    model_index = lax.axis_index("mp")
    micro_count, rows_here, model_width = tokens.shape
    piece_rows = rows_here // data_count
    sub_rows = piece_rows // model_count
    own_rows = rows_here // model_count
    blocks = matrices.shape[1]
    local_cols = matrices.shape[2]
    shard_rows = matrices.shape[0]
    ffn_count = (blocks - 4) // 2
    ffn_cols = ffn_count * local_cols

    matrices_low = matrices.astype(low_type)
    shipped_one = matrices_low[:, :4, :].reshape(shard_rows, 4 * local_cols)
    shipped_two = matrices_low[:, 4:, :].reshape(shard_rows, 2 * ffn_cols)
    lanes = 128
    norm_columns = jnp.swapaxes(norm_vectors.astype(low_type), 0, 1)
    shipped_one = jnp.concatenate(
        [shipped_one, jnp.pad(norm_columns, ((0, 0), (0, lanes - norm_columns.shape[1])))], axis=1
    )
    placement_ids, shipped_one = together(placement_ids, shipped_one)
    slot_count = left_stats.shape[0]
    all_slots = slot_count * data_count
    slot_match = block_slot_index[None, :] == jnp.arange(all_slots)[:, None]
    filled = jnp.any(slot_match, axis=1)
    block_of = jnp.sum(jnp.where(slot_match, jnp.arange(blocks)[None, :], 0), axis=1)
    block_of = jnp.where(filled, block_of, -1)
    own_blocks = lax.dynamic_slice_in_dim(block_of, data_index * slot_count, slot_count, 0)

    order = jnp.arange(rows_here)
    earlier = (order[:, None] < order[None, :]).astype(low_type)
    device_ids = jnp.arange(data_count)[:, None]
    near = near_order(model_count)
    slots_mine = []
    positions = []
    for micro in range(micro_count):
        dest_all = placement_ids[micro].reshape(data_count, rows_here)
        dest_mine = lax.dynamic_slice_in_dim(dest_all, data_index, 1, 0)
        target = dest_mine // rows_here
        to_each = target == device_ids
        to_me = (dest_all // rows_here) == data_index
        rank_both = dot(jnp.concatenate([to_each, to_me]).astype(low_type), earlier).astype(
            jnp.int32
        )
        rank_out = jnp.sum(jnp.where(to_each, rank_both[:data_count], 0), axis=0)
        slots_mine.append((rank_out, target[0]))
        rank_in = jnp.where(to_me, rank_both[data_count:], -1)
        place = jnp.sum(
            jnp.where(
                rank_in[:, None, :] == jnp.arange(piece_rows)[None, :, None],
                (dest_all - data_index * rows_here)[:, None, :],
                0,
            ),
            axis=2,
        )
        place = place.reshape(data_count, model_count, sub_rows).transpose(1, 0, 2)
        place = place.reshape(model_count, own_rows)[model_index ^ jnp.array(near)]
        positions.append(place.reshape(rows_here))

    def pick_rows(given):
        picked = []
        for micro in range(micro_count):
            rank, target = slots_mine[micro]
            here = (rank // sub_rows) == model_index
            slot = jnp.where(here, target * sub_rows + rank % sub_rows, -1)
            pick = (slot[None, :] == jnp.arange(own_rows)[:, None]).astype(low_type)
            rows = dot(pick, given[micro]).astype(low_type)
            picked.append(rows.reshape(data_count, sub_rows, model_width))
        return jnp.concatenate(picked, axis=1)

    def arrived(picked):
        got = exchange(picked).reshape(data_count, micro_count, sub_rows, model_width)
        return [got[:, i].reshape(own_rows, model_width) for i in range(micro_count)]

    def exchange_back(own):
        sent = [rows.reshape(data_count, 1, sub_rows, model_width) for rows in own]
        sent = jnp.concatenate(sent, axis=1)
        got = exchange(sent.reshape(data_count, -1, model_width))
        got = got.reshape(data_count, len(own), sub_rows, model_width)
        return [got[:, i].reshape(own_rows, model_width) for i in range(len(own))]

    def return_slots(micro):
        rank, target = slots_mine[micro]
        block = jnp.sum(
            jnp.where(
                ((rank // sub_rows) ^ model_index) == jnp.array(near)[:, None],
                jnp.arange(model_count)[:, None],
                0,
            ),
            axis=0,
        )
        return block * own_rows + target * sub_rows + rank % sub_rows

    micros = range(micro_count)
    bounds = [jnp.cumsum(lengths[i, 0]) for i in micros]
    segments = [
        jnp.sum((order[:, None] >= bounds[i][None, :]).astype(jnp.int32), axis=1) for i in micros
    ]
    bias_qkv = jnp.concatenate(
        [head_vectors[0], jnp.zeros((local_cols,), f32), head_vectors[1]]
    )[None]
    bias_up = head_vectors[2:].reshape(1, -1)
    half = rows_here // 2
    halves = (slice(0, half), slice(half, rows_here))

    def attend(i, near, far):
        return attention_forward(
            near, far, norms[:2], weights_one, bias_qkv, positions[i], segments[i]
        )

    def second_share(hidden):
        return layer_norm(hidden, norms[3], norms[4]).astype(low_type)

    def second_back(i, hidden, grad_normed):
        hidden_part, gain_rows = norm_back(hidden, norms[3], grad_normed)
        grad_hidden = grad_out[i] + hidden_part
        sums = [
            jnp.sum(grad_hidden, axis=0),
            jnp.sum(gain_rows, axis=0),
            jnp.sum(grad_normed, axis=0),
            jnp.sum(grad_out[i], axis=0),
        ]
        return grad_hidden, grad_hidden.astype(low_type), jnp.stack(sums)

    def attend_back(i, near, far, kept):
        _, qkv, out, lse = kept
        return attention_backward(
            near, far, weights_one, positions[i], segments[i], qkv, out, lse
        )

    def first_back(i, grad_hidden, grad_normed):
        rows_part, gain_rows = norm_back(rows_own[i], norms[0], grad_normed)
        sums = [jnp.sum(gain_rows, axis=0), jnp.sum(grad_normed, axis=0)]
        return (grad_hidden + rows_part).astype(low_type), jnp.stack(sums)

    picked, shipped_one = together(pick_rows(tokens), shipped_one)
    gathered = lax.all_gather(shipped_one, "dp", axis=0, tiled=True)
    x_0, x_1 = arrived(picked)
    rows_0, rows_1 = x_0.astype(f32), x_1.astype(f32)
    rows_own = (rows_0, rows_1)
    x_0 = gather_chips(x_0)
    x_1 = gather_chips(x_1)
    keep = [(positions[i][:own_rows] < bounds[i][-2])[:, None] for i in micros]
    picked, x_0 = together(pick_rows(cotangent), x_0)
    g_0, g_1 = (jnp.where(k, g, 0).astype(low_type) for g, k in zip(arrived(picked), keep))
    grad_out = (g_0.astype(f32), g_1.astype(f32))
    xf_0 = other_core(x_0)
    xf_1 = other_core(x_1)
    gathered, shipped_two, xf_0, xf_1, g_0, g_1 = together(
        gathered, shipped_two, xf_0, xf_1, g_0, g_1
    )
    weights_one = gathered
    norms = jnp.swapaxes(gathered[:, 4 * local_cols :], 0, 1)[:6].astype(f32)
    weights_two = lax.all_gather(shipped_two, "dp", axis=0, tiled=True)

    keep_0, send_0, normed_0, *kept_0 = attend(0, x_0, xf_0)
    g_0 = gather_chips(g_0)
    keep_0, send_0, g_0, g_1 = together(keep_0, send_0, g_0, g_1)
    core_0, gf_0, g_1 = together(other_core(send_0), other_core(g_0), g_1)
    branch_0 = scatter_chips(keep_0, core_0)
    keep_1, send_1, normed_1, *kept_1 = attend(1, x_1, xf_1)
    g_1 = gather_chips(g_1)
    keep_1, send_1, branch_0, g_1 = together(keep_1, send_1, branch_0, g_1)
    hidden_0 = rows_0 + branch_0 + norms[2]
    z_0, core_1, gf_1 = together(second_share(hidden_0), other_core(send_1), other_core(g_1))
    branch_1 = scatter_chips(keep_1, core_1)
    z_0 = gather_chips(z_0)
    z_0, branch_1, weights_two, gf_0, gf_1 = together(z_0, branch_1, weights_two, gf_0, gf_1)
    hidden_1 = rows_1 + branch_1 + norms[2]
    z_1, z_0 = together(second_share(hidden_1), z_0)

    zf_0 = other_core(z_0)
    near_parts = mlp(z_0, g_0, weights_two, bias_up, f32)
    z_1 = gather_chips(z_1)
    zf_0, near_parts = together(zf_0, near_parts)
    far_parts = mlp(zf_0, gf_0, weights_two, bias_up, low_type)
    active_0, grad_up_0, feed_0, back_0, up_sums_0 = zip(near_parts, far_parts)
    z_1, back_0, feed_0 = together(z_1, back_0, feed_0)
    zf_1 = other_core(z_1)
    core_0 = other_core(back_0[1])
    near_parts = mlp(z_1, g_1, weights_two, bias_up, f32)
    zf_1, core_0, near_parts = together(zf_1, core_0, near_parts)
    back_0 = scatter_chips(back_0[0], core_0)
    core_feed_0 = other_core(feed_0[1])
    far_parts = mlp(zf_1, gf_1, weights_two, bias_up, low_type)
    active_1, grad_up_1, feed_1, back_1, up_sums_1 = zip(near_parts, far_parts)
    back_0, back_1, feed_1, core_feed_0 = together(back_0, back_1, feed_1, core_feed_0)
    hidden_grad_0, h_0, second_sums_0 = second_back(0, hidden_0, back_0)
    h_0, grad_up_1, back_1 = together(h_0, grad_up_1, back_1)
    h_0 = gather_chips(h_0)
    grads_two = grads_of(
        ([z_0, zf_0, z_1, zf_1], [*grad_up_0, *grad_up_1]),
        ([g_0, gf_0, g_1, gf_1], [*active_0, *active_1]),
    )
    core_1 = other_core(back_1[1])
    grads_two, h_0, core_1, core_feed_0 = together(grads_two, h_0, core_1, core_feed_0)
    summed_two = lax.psum_scatter(grads_two, "dp", scatter_dimension=0, tiled=True)
    chosen = choose_blocks(own_blocks, local_cols, weights_one, weights_two)
    hf_0, chosen, core_1, core_feed_0 = together(other_core(h_0), chosen, core_1, core_feed_0)

    back_1 = scatter_chips(back_1[0], core_1)
    output_0 = scatter_chips(feed_0[0], core_feed_0)
    keep_0, send_0, grad_qkv_0, sums_0 = attend_back(0, h_0, hf_0, kept_0)
    core_feed_1 = other_core(feed_1[1])
    keep_0, send_0, back_1, output_0, core_feed_1 = together(
        keep_0, send_0, back_1, output_0, core_feed_1
    )
    hidden_grad_1, h_1, second_sums_1 = second_back(1, hidden_1, back_1)
    h_1, keep_0, send_0, output_0 = together(h_1, keep_0, send_0, output_0)
    h_1 = gather_chips(h_1)
    core_0 = other_core(send_0)
    output_0 = (hidden_0 + output_0 + norms[5]).astype(low_type)
    h_1, core_0, output_0, core_feed_1 = together(h_1, core_0, output_0, core_feed_1)
    output_0 = exchange_back([output_0])[0]
    hf_1, core_0, core_feed_1 = together(other_core(h_1), core_0, core_feed_1)
    normed_back_0 = scatter_chips(keep_0, core_0)
    output_1 = scatter_chips(feed_1[0], core_feed_1)
    grads_out = grads_of(([h_0, hf_0, h_1, hf_1], [kept_0[0], kept_1[0]]))
    hf_1, grads_out = together(hf_1, grads_out)
    blocks_out = scatter_step(grads_out.reshape(data_count, shard_rows, local_cols), 1)
    keep_1, send_1, grad_qkv_1, sums_1 = attend_back(1, h_1, hf_1, kept_1)
    keep_1, send_1, normed_back_0, output_1, output_0, summed_two, blocks_out = together(
        keep_1, send_1, normed_back_0, output_1, output_0, summed_two, blocks_out
    )
    core_1 = other_core(send_1)
    grads_qkv = grads_of(([normed_0, normed_1], [grad_qkv_0, grad_qkv_1]))
    core_1, grads_qkv = together(core_1, grads_qkv)
    normed_back_1 = scatter_chips(keep_1, core_1)
    input_0, first_sums_0 = first_back(0, hidden_grad_0, normed_back_0)
    output_1 = (hidden_1 + output_1 + norms[5]).astype(low_type)
    input_0, output_1 = exchange_back([input_0, output_1])
    cut = 3 * local_cols // 2 // 128 * 128
    grads_one = [
        scatter_step(part.reshape(data_count, shard_rows, -1), 1)
        for part in (grads_qkv[:, :cut], grads_qkv[:, cut:])
    ]
    blocks_out = scatter_step(blocks_out, 2)
    output_0 = gather_chips(output_0)
    normed_back_1, grads_one, input_0, output_1, output_0, blocks_out = together(
        normed_back_1, grads_one, input_0, output_1, output_0, blocks_out
    )
    input_0, output_1 = gather_chips(input_0), gather_chips(output_1)
    input_1, first_sums_1 = first_back(1, hidden_grad_1, normed_back_1)
    summed_one = [scatter_grads(part, 2) for part in (*grads_one,)]
    summed_one.append(scatter_grads(blocks_out, 4))
    norm_grads_own = jnp.concatenate(
        [first_sums_0 + first_sums_1, second_sums_0 + second_sums_1], axis=0
    )
    qkv_sums = sums_0 + sums_1
    up_sums = [*up_sums_0, *up_sums_1]

    summed_one, input_1, norm_grads_own = together(summed_one, input_1, norm_grads_own)
    owned = exchange(
        to_slots(block_of, slot_count, local_cols, *summed_one, summed_two)
    )
    stats = (left_stats, right_stats, left_roots, right_roots)
    place = model_index.astype(jnp.int32).reshape(1)
    returns = [return_slots(i) for i in micros]
    outputs_given = give_back(0, returns[0], output_0, other_core(output_0), micro_count, [])
    inputs_given = give_back(0, returns[0], input_0, other_core(input_0), micro_count, [])
    outputs_given = give_back(
        1, returns[1], output_1, other_core(output_1), micro_count, outputs_given
    )
    norm_grads_sum = sum_over(norm_grads_own, "mp")
    owned, outputs_given, inputs_given, norm_grads_sum, input_1 = together(
        owned, outputs_given, inputs_given, norm_grads_sum, input_1
    )
    input_1 = exchange_back([input_1])[0]
    head_own = jnp.concatenate(
        [
            qkv_sums[:, :local_cols],
            qkv_sums[:, 2 * local_cols :],
            sum(up_sums).reshape(ffn_count, local_cols),
        ],
        axis=0,
    )
    vectors = jnp.concatenate([norm_grads_sum, head_own], axis=1)
    owned_grads = owned.reshape(data_count, slot_count, shard_rows, local_cols)
    owned_grads = jnp.swapaxes(owned_grads, 1, 2).reshape(model_width, slot_count, local_cols)
    owned_grads = owned_grads.astype(f32)
    near_part = gather_chips(owned[None])
    near_part, input_1, owned_grads = together(near_part, input_1, owned_grads)
    far_part = other_core(near_part)
    new_left, new_right, directions, squares = precondition(place, near_part, far_part, stats)
    squares, input_1, vectors = together(squares, input_1, vectors)
    input_1 = gather_chips(input_1)
    vectors = sum_over(vectors, "dp")
    inputs_given = give_back(
        1, returns[1], input_1, other_core(input_1), micro_count, inputs_given
    )[0]
    outputs_given = outputs_given[0]
    norm_all = vectors[:, :model_width]
    head_total = vectors[:, model_width:]
    norm_cols = norm_vectors.shape[1]
    norm_total = lax.dynamic_slice_in_dim(norm_all, data_index * norm_cols, norm_cols, 1)
    squares = jnp.sum(squares, axis=(1, 2))
    square_total = sum_over(squares.reshape(1, slot_count), "mp")[0]
    factor = lax.rsqrt(square_total / (model_width * model_width) + mean_eps)
    updated_blocks = jnp.stack(
        [
            chosen[s].astype(f32) - matrix_rate * factor[s] * directions[s]
            for s in range(slot_count)
        ],
        axis=1,
    )
    new_norm_state = stat_decay * norm_state + norm_total * norm_total
    new_norm_vectors = norm_vectors - vector_rate * norm_total / (
        jnp.sqrt(new_norm_state) + diag_eps
    )
    new_head_state = stat_decay * head_state + head_total * head_total
    new_head_vectors = head_vectors - vector_rate * head_total / (
        jnp.sqrt(new_head_state) + diag_eps
    )
    return (
        outputs_given,
        inputs_given,
        owned_grads,
        new_left,
        new_right,
        updated_blocks,
        norm_total,
        new_norm_state,
        new_norm_vectors,
        head_total,
        new_head_state,
        new_head_vectors,
    )


def solution(mesh):
    placed = (
        P(None, "dp", None),
        P(None, "dp", None),
        P(None, "dp", None),
        P(),
        P(),
        P("dp", None, "mp"),
        P(None, "dp"),
        P(None, "mp"),
        P("dp", "mp", None),
        P("dp", "mp", None),
        P("dp", None, None),
        P("dp", "mp", None),
        P(None, "dp"),
        P(None, "mp"),
    )
    return jax.shard_map(
        on_device,
        mesh=mesh,
        in_specs=placed,
        out_specs=(
            P(None, "dp", None),
            P(None, "dp", None),
            P(None, "dp", "mp"),
            P("dp", "mp", None),
            P("dp", "mp", None),
            P(None, "dp", "mp"),
            P(None, "dp"),
            P(None, "dp"),
            P(None, "dp"),
            P(None, "mp"),
            P(None, "mp"),
            P(None, "mp"),
        ),
        check_vma=False,
    )
```

```python
import functools
import math

import jax
import jax.numpy as jnp
from jax import lax
from jax.experimental import pallas as pl
from jax.experimental.pallas import tpu as pltpu
from jax.sharding import PartitionSpec as P

HEAD_DIM = 64


stat_decay = 0.5
matrix_rate = 0.02
vector_rate = 0.3
norm_eps = 1e-05
mean_eps = 1e-06
diag_eps = 1e-08
masked_score = -1000000000.0

f32 = jnp.float32
low_type = jnp.bfloat16


def unit_rows_of(values):
    center = values - jnp.mean(values, axis=-1, keepdims=True)
    spread = jnp.mean(center * center, axis=-1, keepdims=True)
    scale_rows = lax.rsqrt(spread + norm_eps)
    return center * scale_rows, scale_rows


def layer_norm(values, gain, shift):
    unit_rows, _ = unit_rows_of(values)
    return unit_rows * gain + shift


def norm_back(values, gain, grad_normed):
    unit_rows, scale_rows = unit_rows_of(values)
    grad_unit = grad_normed * gain
    grad_values = scale_rows * (
        grad_unit
        - jnp.mean(grad_unit, axis=-1, keepdims=True)
        - unit_rows * jnp.mean(grad_unit * unit_rows, axis=-1, keepdims=True)
    )
    return (grad_values, grad_normed * unit_rows)


def dot(left, right):
    return lax.dot_general(left, right, (((1,), (0,)), ((), ())), preferred_element_type=f32)


def dot_nt(left, right):
    return lax.dot_general(left, right, (((1,), (1,)), ((), ())), preferred_element_type=f32)


def dot_tn(left, right):
    return lax.dot_general(left, right, (((0,), (0,)), ((), ())), preferred_element_type=f32)


TILE = 256
STRIP = 64
VMEM_BYTES = 28 * 1024 * 1024
SMALL = pl.CostEstimate(flops=10**9, bytes_accessed=10**6, transcendentals=0)
LARGE = pl.CostEstimate(flops=20 * 10**9, bytes_accessed=10**6, transcendentals=0)
MEDIUM = pl.CostEstimate(flops=11 * 10**9, bytes_accessed=10**6, transcendentals=0)

def whole_spec():
    return pl.BlockSpec(memory_space=pltpu.VMEM)

def attention_forward_kernel(
    near_ref, far_ref, norm_ref, weights_ref, bias_ref,
    place_row_ref, place_col_ref, seg_row_ref, seg_col_ref,
    keep_ref, send_ref, normed_ref, attended_ref, qkv_ref, out_ref, lse_ref,
    arrived,
):
    rows = arrived.shape[0]
    half = rows // 2
    cols = attended_ref.shape[1]
    heads = cols // HEAD_DIM
    scale = 1.0 / math.sqrt(HEAD_DIM)
    tiles = rows // TILE
    for start, source in ((0, near_ref), (half, far_ref)):

        def norm_some(i, carry):
            values = source[pl.ds(pl.multiple_of(i * STRIP, STRIP), STRIP), :].astype(f32)
            normed = layer_norm(values, norm_ref[0:1, :], norm_ref[1:2, :])
            normed_ref[pl.ds(pl.multiple_of(start + i * STRIP, STRIP), STRIP), :] = (
                normed.astype(low_type)
            )
            return carry

        lax.fori_loop(0, half // STRIP, norm_some, 0)
    for t in range(tiles):
        part = normed_ref[pl.ds(t * TILE, TILE), :]
        arrived[pl.ds(t * TILE, TILE), :] = (
            dot(part, weights_ref[:, : 3 * cols]) + bias_ref[...]
        ).astype(low_type)
    for t in range(tiles):
        wanted = lax.broadcasted_iota(jnp.int32, (TILE, rows), 0) + t * TILE
        pick = jnp.where(wanted == place_row_ref[...], 1.0, 0.0).astype(low_type)
        qkv_ref[pl.ds(t * TILE, TILE), :] = dot(pick, arrived[...]).astype(low_type)
    for h in range(heads):
        lanes = slice(h * HEAD_DIM, (h + 1) * HEAD_DIM)
        key_lanes = slice(cols + h * HEAD_DIM, cols + (h + 1) * HEAD_DIM)
        value_lanes = slice(2 * cols + h * HEAD_DIM, 2 * cols + (h + 1) * HEAD_DIM)
        for t in range(tiles):
            here = slice(t * TILE, (t + 1) * TILE)
            query = qkv_ref[here, lanes] * jnp.asarray(scale, low_type)
            seg_q = seg_col_ref[here, :]
            scores = []
            top = None
            for c in range(t + 1):
                there = slice(c * TILE, (c + 1) * TILE)
                s = dot_nt(query, qkv_ref[there, key_lanes])
                allowed = seg_q == seg_row_ref[:, there]
                if c == t:
                    allowed = allowed & (
                        lax.broadcasted_iota(jnp.int32, (TILE, TILE), 0)
                        >= lax.broadcasted_iota(jnp.int32, (TILE, TILE), 1)
                    )
                s = jnp.where(allowed, s, masked_score)
                scores.append(s)
                m = jnp.max(s, axis=1, keepdims=True)
                top = m if top is None else jnp.maximum(top, m)
            total = 0.0
            out = 0.0
            for c in range(t + 1):
                there = slice(c * TILE, (c + 1) * TILE)
                e = jnp.exp(scores[c] - top)
                total = total + jnp.sum(e, axis=1, keepdims=True)
                out = out + dot(e.astype(low_type), qkv_ref[there, value_lanes])
            out_ref[here, lanes] = (out / total).astype(low_type)
            lse_ref[here, h : h + 1] = top + jnp.log(total)
    for t in range(tiles):
        wanted = lax.broadcasted_iota(jnp.int32, (TILE, rows), 1)
        pick = jnp.where(wanted == place_col_ref[pl.ds(t * TILE, TILE), :], 1.0, 0.0).astype(low_type)
        part = dot(pick, out_ref[...]).astype(low_type)
        attended_ref[pl.ds(t * TILE, TILE), :] = part
        branch = dot_nt(part, weights_ref[:, 3 * cols : 4 * cols])
        if t * TILE < half:
            keep_ref[pl.ds(t * TILE, TILE), :] = branch
        else:
            send_ref[pl.ds(t * TILE - half, TILE), :] = branch.astype(low_type)

def attention_forward(near, far, norms, weights, bias, place, segment, place_col, segment_col):
    rows = 2 * near.shape[0]
    width = near.shape[1]
    cols = bias.shape[1] // 3
    heads = cols // HEAD_DIM
    shape = jax.ShapeDtypeStruct
    return pl.pallas_call(
        attention_forward_kernel,
        out_shape=(
            shape((rows // 2, width), f32),
            shape((rows // 2, width), low_type),
            shape((rows, width), low_type),
            shape((rows, cols), low_type),
            shape((rows, 3 * cols), low_type),
            shape((rows, cols), low_type),
            shape((rows, heads), f32),
        ),
        in_specs=[whole_spec()] * 9,
        out_specs=tuple([whole_spec()] * 7),
        scratch_shapes=[pltpu.VMEM((rows, 3 * cols), low_type)],
        compiler_params=pltpu.CompilerParams(vmem_limit_bytes=VMEM_BYTES),
        cost_estimate=LARGE,
    )(near, far, norms, weights, bias, place[None, :], place_col, segment[None, :], segment_col)

def attention_backward_kernel(
    near_ref, far_ref, weights_ref, place_row_ref, place_col_ref, seg_row_ref, seg_col_ref,
    qkv_ref, out_ref, lse_ref,
    keep_ref, send_ref, grads_ref, sums_ref,
    arrived, placed, grad_key, grad_value, moved,
):
    rows = arrived.shape[0]
    half = rows // 2
    cols = out_ref.shape[1]
    heads = cols // HEAD_DIM
    scale = 1.0 / math.sqrt(HEAD_DIM)
    tiles = rows // TILE
    for t in range(tiles):
        source = near_ref if t * TILE < half else far_ref
        part = source[pl.ds(t * TILE % half, TILE), :]
        arrived[pl.ds(t * TILE, TILE), :] = dot(
            part, weights_ref[:, 3 * cols : 4 * cols]
        ).astype(low_type)
    for t in range(tiles):
        wanted = lax.broadcasted_iota(jnp.int32, (TILE, rows), 0) + t * TILE
        pick = jnp.where(wanted == place_row_ref[...], 1.0, 0.0).astype(low_type)
        placed[pl.ds(t * TILE, TILE), :] = dot(pick, arrived[...]).astype(low_type)
    for h in range(heads):
        lanes = slice(h * HEAD_DIM, (h + 1) * HEAD_DIM)
        key_lanes = slice(cols + h * HEAD_DIM, cols + (h + 1) * HEAD_DIM)
        value_lanes = slice(2 * cols + h * HEAD_DIM, 2 * cols + (h + 1) * HEAD_DIM)
        grad_key[...] = jnp.zeros_like(grad_key)
        grad_value[...] = jnp.zeros_like(grad_value)
        for t in range(tiles):
            here = slice(t * TILE, (t + 1) * TILE)
            query = qkv_ref[here, lanes] * jnp.asarray(scale, low_type)
            grad = placed[here, lanes]
            row_total = jnp.sum(grad.astype(f32) * out_ref[here, lanes].astype(f32), axis=1, keepdims=True)
            seg_q = seg_col_ref[here, :]
            lse = lse_ref[here, h : h + 1]
            grad_query = 0.0
            for c in range(t + 1):
                there = slice(c * TILE, (c + 1) * TILE)
                key = qkv_ref[there, key_lanes]
                s = dot_nt(query, key)
                allowed = seg_q == seg_row_ref[:, there]
                if c == t:
                    allowed = allowed & (
                        lax.broadcasted_iota(jnp.int32, (TILE, TILE), 0)
                        >= lax.broadcasted_iota(jnp.int32, (TILE, TILE), 1)
                    )
                p = jnp.where(allowed, jnp.exp(s - lse), 0.0)
                dp = dot_nt(grad, qkv_ref[there, value_lanes])
                ds = (p * (dp - row_total)).astype(low_type)
                grad_query = grad_query + dot(ds, key)
                grad_key[there, :] += dot_tn(ds, query)
                grad_value[there, :] += dot_tn(p.astype(low_type), grad)
            moved[here, lanes] = (grad_query * scale).astype(low_type)
        moved[:, key_lanes] = grad_key[...].astype(low_type)
        moved[:, value_lanes] = grad_value[...].astype(low_type)
    sums_ref[...] = jnp.sum(moved[...].astype(f32), axis=0, keepdims=True)
    for t in range(tiles):
        wanted = lax.broadcasted_iota(jnp.int32, (TILE, rows), 1)
        pick = jnp.where(wanted == place_col_ref[pl.ds(t * TILE, TILE), :], 1.0, 0.0).astype(low_type)
        part = dot(pick, moved[...]).astype(low_type)
        grads_ref[pl.ds(t * TILE, TILE), :] = part
        normed = dot_nt(part, weights_ref[:, : 3 * cols])
        if t * TILE < half:
            keep_ref[pl.ds(t * TILE, TILE), :] = normed
        else:
            send_ref[pl.ds(t * TILE - half, TILE), :] = normed.astype(low_type)

def attention_backward(near, far, weights, place, segment, columns, qkv, out, lse):
    place_col, segment_col = columns
    rows = 2 * near.shape[0]
    width = near.shape[1]
    cols = out.shape[1]
    heads = cols // HEAD_DIM
    shape = jax.ShapeDtypeStruct
    return pl.pallas_call(
        attention_backward_kernel,
        out_shape=(
            shape((rows // 2, width), f32),
            shape((rows // 2, width), low_type),
            shape((rows, 3 * cols), low_type),
            shape((1, 3 * cols), f32),
        ),
        in_specs=[whole_spec()] * 10,
        out_specs=tuple([whole_spec()] * 4),
        scratch_shapes=[
            pltpu.VMEM((rows, cols), low_type),
            pltpu.VMEM((rows, cols), low_type),
            pltpu.VMEM((rows, HEAD_DIM), f32),
            pltpu.VMEM((rows, HEAD_DIM), f32),
            pltpu.VMEM((rows, 3 * cols), low_type),
        ],
        compiler_params=pltpu.CompilerParams(vmem_limit_bytes=VMEM_BYTES),
        cost_estimate=LARGE,
    )(near, far, weights, place[None, :], place_col, segment[None, :], segment_col, qkv, out, lse)

def mlp_kernel(normed_ref, grad_ref, weights_ref, bias_ref, active_ref, grad_up_ref, feed_ref, back_ref, sums_ref):
    rows, width = normed_ref.shape
    cols = bias_ref.shape[1]
    step = TILE
    total = 0.0
    c0 = math.sqrt(2.0 / math.pi)
    for t in range(rows // step):
        here = slice(t * step, (t + 1) * step)
        pre = dot(normed_ref[here, :], weights_ref[:, :cols]) + bias_ref[...]
        square = pre * pre
        bent = jnp.tanh(c0 * (pre + 0.044715 * (square * pre)))
        active_ref[here, :] = (0.5 * pre * (1.0 + bent)).astype(low_type)
        slope = 0.5 * (1.0 + bent) + 0.5 * pre * (1.0 - bent * bent) * (c0 * (1.0 + 0.134145 * square))
        grad = dot(grad_ref[here, :], weights_ref[:, cols:]) * slope
        grad_low = grad.astype(low_type)
        grad_up_ref[here, :] = grad_low
        total = total + jnp.sum(grad_low.astype(f32), axis=0, keepdims=True)
    sums_ref[...] = total
    for t in range(rows // step):
        here = slice(t * step, (t + 1) * step)
        back_ref[here, :] = dot_nt(grad_up_ref[here, :], weights_ref[:, :cols]).astype(back_ref.dtype)
        feed_ref[here, :] = dot_nt(active_ref[here, :], weights_ref[:, cols:]).astype(feed_ref.dtype)

def mlp(normed, grad, weights, bias, kind):
    rows, width = normed.shape
    cols = bias.shape[1]
    shape = jax.ShapeDtypeStruct
    return pl.pallas_call(
        mlp_kernel,
        out_shape=(
            shape((rows, cols), low_type),
            shape((rows, cols), low_type),
            shape((rows, width), kind),
            shape((rows, width), kind),
            shape((1, cols), f32),
        ),
        in_specs=[whole_spec()] * 4,
        out_specs=tuple([whole_spec()] * 5),
        compiler_params=pltpu.CompilerParams(vmem_limit_bytes=VMEM_BYTES),
        cost_estimate=MEDIUM,
    )(normed, grad, weights, bias)


def grads_kernel(groups, *refs):
    out_ref = refs[-1]
    for t in range(out_ref.shape[0] // TILE):
        rows = slice(t * TILE, (t + 1) * TILE)
        start = 0
        for group in groups:
            total = 0.0
            for left, right, at, count in group:
                total = total + dot_tn(refs[left][:, rows], refs[right][at : at + count, :])
            out_ref[rows, start : start + total.shape[1]] = total.astype(out_ref.dtype)
            start = start + total.shape[1]


def grads_of(*groups):
    width = groups[0][0][0].shape[1]
    cols = sum(right[0].shape[1] for _, right in groups)
    pieces = []
    plan = []
    for left, right in groups:
        start = len(pieces)
        pieces.extend((*left, *right))
        count = left[0].shape[0]
        fit = right[0].shape[0] // count
        plan.append(
            [
                (start + g, start + len(left) + g // fit, g % fit * count, count)
                for g in range(len(left))
            ]
        )
    return pl.pallas_call(
        functools.partial(grads_kernel, plan),
        out_shape=jax.ShapeDtypeStruct((width, cols), low_type),
        in_specs=[whole_spec()] * len(pieces),
        out_specs=whole_spec(),
        compiler_params=pltpu.CompilerParams(vmem_limit_bytes=VMEM_BYTES),
        cost_estimate=MEDIUM if cols > 1024 else SMALL,
    )(*pieces)


def slots_kernel(cols, slot_count, block_ref, *refs):
    *parts, out, held = refs
    rows = held.shape[0]
    start = 0
    for part in parts:
        held[:, start : start + part.shape[1]] = part[...]
        start = start + part.shape[1]
    for s in range(block_ref.shape[0]):
        block = block_ref[s]
        lanes = pl.ds(pl.multiple_of(jnp.maximum(block, 0) * cols, cols), cols)
        taken = held[:, lanes]
        at = s % slot_count * rows
        out[s // slot_count, at : at + rows, :] = jnp.where(block >= 0, taken, jnp.zeros_like(taken))


def to_slots(block_of, slot_count, cols, *parts):
    count = block_of.shape[0] // slot_count
    rows = parts[0].shape[0]
    width = sum(part.shape[1] for part in parts)
    return pl.pallas_call(
        functools.partial(slots_kernel, cols, slot_count),
        out_shape=jax.ShapeDtypeStruct((count, slot_count * rows, cols), low_type),
        in_specs=[pl.BlockSpec(memory_space=pltpu.SMEM)] + [whole_spec()] * len(parts),
        out_specs=whole_spec(),
        scratch_shapes=[pltpu.VMEM((rows, width), low_type)],
        compiler_params=pltpu.CompilerParams(vmem_limit_bytes=VMEM_BYTES),
        cost_estimate=SMALL,
    )(block_of, *parts)


def choose_kernel(cols, split, block_ref, first_ref, second_ref, *outs):
    for s, out in enumerate(outs):
        block = block_ref[s]

        @pl.when(block < 0)
        def _():
            out[...] = jnp.zeros_like(out)

        @pl.when((block >= 0) & (block < split))
        def _():
            lanes = pl.multiple_of(jnp.clip(block, 0, split - 1) * cols, cols)
            out[...] = first_ref[:, pl.ds(lanes, cols)]

        @pl.when(block >= split)
        def _():
            lanes = pl.multiple_of(jnp.maximum(block - split, 0) * cols, cols)
            out[...] = second_ref[:, pl.ds(lanes, cols)]


def choose_blocks(block_of, cols, first, second):
    slot_count = block_of.shape[0]
    return pl.pallas_call(
        functools.partial(choose_kernel, cols, 4),
        out_shape=tuple(
            [jax.ShapeDtypeStruct((first.shape[0], cols), low_type) for _ in range(slot_count)]
        ),
        in_specs=[pl.BlockSpec(memory_space=pltpu.SMEM), whole_spec(), whole_spec()],
        out_specs=tuple([whole_spec()] * slot_count),
        compiler_params=pltpu.CompilerParams(vmem_limit_bytes=VMEM_BYTES),
        cost_estimate=SMALL,
    )(block_of, first, second)


def precondition_kernel(
    order, place_ref, near_ref, far_ref, left_ref, right_ref, left_root_ref, right_root_ref, *refs
):
    new_left_ref, new_right_ref, direction_ref, square_ref, halfway_ref = refs
    count, parts, rows_part, cols = near_ref.shape
    width = parts * rows_part
    rows = left_ref.shape[1]
    place = place_ref[0]
    pieces = [
        ref[k].reshape(width, cols) for ref in (near_ref, far_ref) for k in range(count)
    ]
    lanes = [pl.ds(pl.multiple_of((place ^ j) * cols, cols), cols) for j in order]
    halfway = 0.0
    for at, piece in zip(lanes, pieces):
        halfway = halfway + dot_nt(piece, right_root_ref[0, :, at].astype(low_type))
    halfway_ref[...] = halfway.astype(low_type)
    total = 0.0
    for t in range(width // TILE):
        here = slice(t * TILE, (t + 1) * TILE)
        part = dot(left_root_ref[0, here, :].astype(low_type), halfway_ref[...])
        direction_ref[0, here, :] = part
        total = total + jnp.sum(part * part, axis=0, keepdims=True)
    square_ref[0] = total
    left = stat_decay * left_ref[0]
    groups = rows // rows_part
    for g, piece in enumerate(pieces):
        ref = near_ref if g < count else far_ref
        own = ref[g % count, pl.ds(place * groups, groups)].reshape(rows, cols)
        left = left + dot_nt(own, piece)
    new_left_ref[0] = left
    for at, piece in zip(lanes, pieces):
        new_right_ref[0, :, at] = stat_decay * right_ref[0, :, at] + dot_tn(pieces[0], piece)


def precondition(place, near, far, stats):
    slot_count, rows, width = stats[0].shape
    count, parts, held_rows, cols = near.shape
    rows_part = held_rows // slot_count
    shape = jax.ShapeDtypeStruct

    def of_slot(dims):
        return pl.BlockSpec((1,) + dims[1:], lambda s: (s, 0, 0))

    pieces_spec = pl.BlockSpec((count, parts, rows_part, cols), lambda s: (0, 0, s, 0))
    return pl.pallas_call(
        functools.partial(precondition_kernel, near_order(lax.axis_size("mp"))),
        grid=(slot_count,),
        out_shape=(
            shape(stats[0].shape, f32),
            shape(stats[1].shape, f32),
            shape((slot_count, width, cols), f32),
            shape((slot_count, 1, cols), f32),
        ),
        in_specs=[pl.BlockSpec(memory_space=pltpu.SMEM), pieces_spec, pieces_spec]
        + [of_slot(array.shape) for array in stats],
        out_specs=(
            of_slot(stats[0].shape),
            of_slot(stats[1].shape),
            of_slot((slot_count, width, cols)),
            of_slot((slot_count, 1, cols)),
        ),
        scratch_shapes=[pltpu.VMEM((width, cols), low_type)],
        compiler_params=pltpu.CompilerParams(vmem_limit_bytes=2 * VMEM_BYTES),
        cost_estimate=MEDIUM,
    )(place, near, far, *stats)


def give_back_kernel(slot_ref, near_ref, far_ref, *refs):
    out_ref = refs[-1]
    half = near_ref.shape[0]
    for t in range(out_ref.shape[1] // TILE):
        here = slice(t * TILE, (t + 1) * TILE)
        total = 0.0
        for start, source in ((0, near_ref), (half, far_ref)):
            wanted = lax.broadcasted_iota(jnp.int32, (TILE, half), 1) + start
            pick = jnp.where(wanted == slot_ref[here, :], 1.0, 0.0).astype(low_type)
            total = total + dot(pick, source[...])
        out_ref[0, here, :] = total.astype(low_type)


def give_back(micro, slots, near, far, micro_count, before):
    rows, width = 2 * near.shape[0], near.shape[1]

    def all_of(dims):
        return pl.BlockSpec(dims, lambda i: (0,) * len(dims))

    return [
        pl.pallas_call(
            give_back_kernel,
            grid=(1,),
            out_shape=jax.ShapeDtypeStruct((micro_count, rows, width), low_type),
            in_specs=[all_of((rows, 1)), all_of(near.shape), all_of(far.shape)]
            + [pl.BlockSpec(memory_space=pl.ANY)] * len(before),
            out_specs=pl.BlockSpec((1, rows, width), lambda i: (micro, 0, 0)),
            input_output_aliases={3 + k: k for k in range(len(before))},
            compiler_params=pltpu.CompilerParams(vmem_limit_bytes=VMEM_BYTES),
            cost_estimate=SMALL,
        )(slots[:, None], near, far, *before)
    ]


def swap(values, axis, bit):
    count = lax.axis_size(axis)
    return lax.ppermute(values, axis, [(i, i ^ bit) for i in range(count)])


def near_order(count):
    found = [0]
    bit = count // 2
    while bit >= 1:
        found = found + [j ^ bit for j in found]
        bit //= 2
    return found


def gather_chips(share):
    bit = lax.axis_size("mp") // 2
    while bit > 1:
        share = jnp.concatenate([share, swap(share, "mp", bit)], axis=0)
        bit //= 2
    return share


def other_core(values):
    return swap(values, "mp", 1)


def scatter_chips(keep, received):
    bit = 2
    count = lax.axis_size("mp")
    if bit == count:
        return keep + received.astype(f32)
    half = keep.shape[0] // 2
    sent = (keep[half:] + received[half:].astype(f32)).astype(low_type)
    got = swap(sent, "mp", bit)
    values = keep[:half] + received[:half].astype(f32)
    bit *= 2
    while bit < count:
        values = values + got.astype(f32)
        half = values.shape[0] // 2
        got = swap(values[half:].astype(low_type), "mp", bit)
        values, got = values[:half], got
        bit *= 2
    return values + got.astype(f32)


def after(values, others):
    return lax.optimization_barrier((values, others))


def together(*values):
    return lax.optimization_barrier(values)


def scatter_step(blocks, bit):
    index = lax.axis_index("dp") // bit % 2
    blocks = blocks.reshape(-1, 2, *blocks.shape[1:])
    mine = lax.dynamic_index_in_dim(blocks, index, 1, keepdims=False)
    other = lax.dynamic_index_in_dim(blocks, 1 - index, 1, keepdims=False)
    got = swap(other.astype(low_type), "dp", bit)
    return mine.astype(f32) + got.astype(f32)


def scatter_grads(blocks, bit):
    while bit < lax.axis_size("dp"):
        blocks = scatter_step(blocks, bit)
        bit *= 2
    return blocks[0].astype(low_type)


def sum_over(values, axis, bit=1):
    while bit < lax.axis_size(axis):
        values = values + swap(values, axis, bit)
        bit *= 2
    return values


def exchange(rows):
    return lax.all_to_all(rows, "dp", split_axis=0, concat_axis=0, tiled=True)


def on_device(
    tokens,
    cotangent,
    lengths,
    placement_ids,
    block_slot_index,
    matrices,
    norm_vectors,
    head_vectors,
    left_stats,
    right_stats,
    left_roots,
    right_roots,
    norm_state,
    head_state,
):
    data_count = lax.axis_size("dp")
    data_index = lax.axis_index("dp")
    model_count = lax.axis_size("mp")
    model_index = lax.axis_index("mp")
    micro_count, rows_here, model_width = tokens.shape
    piece_rows = rows_here // data_count
    sub_rows = piece_rows // model_count
    own_rows = rows_here // model_count
    blocks = matrices.shape[1]
    local_cols = matrices.shape[2]
    shard_rows = matrices.shape[0]
    ffn_count = (blocks - 4) // 2
    ffn_cols = ffn_count * local_cols

    matrices_low = matrices.astype(low_type)
    shipped_one = matrices_low[:, :4, :].reshape(shard_rows, 4 * local_cols)
    shipped_two = matrices_low[:, 4:, :].reshape(shard_rows, 2 * ffn_cols)
    lanes = 128
    norm_columns = jnp.swapaxes(norm_vectors.astype(low_type), 0, 1)
    shipped_one = jnp.concatenate(
        [shipped_one, jnp.pad(norm_columns, ((0, 0), (0, lanes - norm_columns.shape[1])))], axis=1
    )
    placement_ids, shipped_one = together(placement_ids, shipped_one)
    slot_count = left_stats.shape[0]
    all_slots = slot_count * data_count
    slot_match = block_slot_index[None, :] == jnp.arange(all_slots)[:, None]
    filled = jnp.any(slot_match, axis=1)
    block_of = jnp.sum(jnp.where(slot_match, jnp.arange(blocks)[None, :], 0), axis=1)
    block_of = jnp.where(filled, block_of, -1)
    own_blocks = lax.dynamic_slice_in_dim(block_of, data_index * slot_count, slot_count, 0)

    order = jnp.arange(rows_here)
    earlier = (order[:, None] < order[None, :]).astype(low_type)
    device_ids = jnp.arange(data_count)[:, None]
    near = near_order(model_count)
    slots_mine = []
    positions = []
    for micro in range(micro_count):
        dest_all = placement_ids[micro].reshape(data_count, rows_here)
        dest_mine = lax.dynamic_slice_in_dim(dest_all, data_index, 1, 0)
        target = dest_mine // rows_here
        to_each = target == device_ids
        to_me = (dest_all // rows_here) == data_index
        rank_both = dot(jnp.concatenate([to_each, to_me]).astype(low_type), earlier).astype(
            jnp.int32
        )
        rank_out = jnp.sum(jnp.where(to_each, rank_both[:data_count], 0), axis=0)
        slots_mine.append((rank_out, target[0]))
        rank_in = jnp.where(to_me, rank_both[data_count:], -1)
        place = jnp.sum(
            jnp.where(
                rank_in[:, None, :] == jnp.arange(piece_rows)[None, :, None],
                (dest_all - data_index * rows_here)[:, None, :],
                0,
            ),
            axis=2,
        )
        place = place.reshape(data_count, model_count, sub_rows).transpose(1, 0, 2)
        place = place.reshape(model_count, own_rows)[model_index ^ jnp.array(near)]
        positions.append(place.reshape(rows_here))

    def pick_rows(given):
        picked = []
        for micro in range(micro_count):
            rank, target = slots_mine[micro]
            here = (rank // sub_rows) == model_index
            slot = jnp.where(here, target * sub_rows + rank % sub_rows, -1)
            pick = (slot[None, :] == jnp.arange(own_rows)[:, None]).astype(low_type)
            rows = dot(pick, given[micro]).astype(low_type)
            picked.append(rows.reshape(data_count, sub_rows, model_width))
        return jnp.concatenate(picked, axis=1)

    def arrived(picked):
        got = exchange(picked).reshape(data_count, micro_count, sub_rows, model_width)
        return [got[:, i].reshape(own_rows, model_width) for i in range(micro_count)]

    def exchange_back(own):
        sent = [rows.reshape(data_count, 1, sub_rows, model_width) for rows in own]
        sent = jnp.concatenate(sent, axis=1)
        got = exchange(sent.reshape(data_count, -1, model_width))
        got = got.reshape(data_count, len(own), sub_rows, model_width)
        return [got[:, i].reshape(own_rows, model_width) for i in range(len(own))]

    def return_slots(micro):
        rank, target = slots_mine[micro]
        block = jnp.sum(
            jnp.where(
                ((rank // sub_rows) ^ model_index) == jnp.array(near)[:, None],
                jnp.arange(model_count)[:, None],
                0,
            ),
            axis=0,
        )
        return block * own_rows + target * sub_rows + rank % sub_rows

    micros = range(micro_count)
    bounds = [jnp.cumsum(lengths[i, 0]) for i in micros]
    segments = [
        jnp.sum((order[:, None] >= bounds[i][None, :]).astype(jnp.int32), axis=1) for i in micros
    ]
    bias_qkv = jnp.concatenate(
        [head_vectors[0], jnp.zeros((local_cols,), f32), head_vectors[1]]
    )[None]
    bias_up = head_vectors[2:].reshape(1, -1)
    half = rows_here // 2
    halves = (slice(0, half), slice(half, rows_here))

    def attend(i, near, far):
        return attention_forward(
            near, far, norms[:2], weights_one, bias_qkv, positions[i], segments[i], *columns[i]
        )

    def second_share(hidden):
        return layer_norm(hidden, norms[3], norms[4]).astype(low_type)

    def second_back(i, hidden, grad_normed):
        hidden_part, gain_rows = norm_back(hidden, norms[3], grad_normed)
        grad_hidden = grad_out[i] + hidden_part
        sums = [
            jnp.sum(grad_hidden, axis=0),
            jnp.sum(gain_rows, axis=0),
            jnp.sum(grad_normed, axis=0),
            jnp.sum(grad_out[i], axis=0),
        ]
        return grad_hidden, grad_hidden.astype(low_type), jnp.stack(sums)

    def attend_back(i, near, far, kept):
        _, qkv, out, lse = kept
        return attention_backward(
            near, far, weights_one, positions[i], segments[i], columns[i], qkv, out, lse
        )

    def first_back(i, grad_hidden, grad_normed):
        rows_part, gain_rows = norm_back(rows_own[i], norms[0], grad_normed)
        sums = [jnp.sum(gain_rows, axis=0), jnp.sum(grad_normed, axis=0)]
        return (grad_hidden + rows_part).astype(low_type), jnp.stack(sums)

    picked, shipped_one = together(pick_rows(tokens), shipped_one)
    gathered = lax.all_gather(shipped_one, "dp", axis=0, tiled=True)
    x_0, x_1 = arrived(picked)
    rows_0, rows_1 = x_0.astype(f32), x_1.astype(f32)
    rows_own = (rows_0, rows_1)
    columns = [(positions[i][:, None], segments[i][:, None]) for i in micros]
    x_0, columns = together(x_0, columns)
    x_0 = gather_chips(x_0)
    x_1 = gather_chips(x_1)
    keep = [(positions[i][:own_rows] < bounds[i][-2])[:, None] for i in micros]
    picked, x_0 = together(pick_rows(cotangent), x_0)
    g_0, g_1 = (jnp.where(k, g, 0).astype(low_type) for g, k in zip(arrived(picked), keep))
    grad_out = (g_0.astype(f32), g_1.astype(f32))
    xf_0 = other_core(x_0)
    xf_1 = other_core(x_1)
    gathered, shipped_two, xf_0, xf_1, g_0, g_1 = together(
        gathered, shipped_two, xf_0, xf_1, g_0, g_1
    )
    weights_one = gathered
    norms = jnp.swapaxes(gathered[:, 4 * local_cols :], 0, 1)[:6].astype(f32)
    weights_two = lax.all_gather(shipped_two, "dp", axis=0, tiled=True)

    keep_0, send_0, normed_0, *kept_0 = attend(0, x_0, xf_0)
    g_0 = gather_chips(g_0)
    keep_0, send_0, g_0, g_1 = together(keep_0, send_0, g_0, g_1)
    core_0, gf_0, g_1 = together(other_core(send_0), other_core(g_0), g_1)
    branch_0 = scatter_chips(keep_0, core_0)
    keep_1, send_1, normed_1, *kept_1 = attend(1, x_1, xf_1)
    g_1 = gather_chips(g_1)
    keep_1, send_1, branch_0, g_1 = together(keep_1, send_1, branch_0, g_1)
    hidden_0 = rows_0 + branch_0 + norms[2]
    z_0, core_1, gf_1 = together(second_share(hidden_0), other_core(send_1), other_core(g_1))
    branch_1 = scatter_chips(keep_1, core_1)
    z_0 = gather_chips(z_0)
    z_0, branch_1, weights_two, gf_0, gf_1 = together(z_0, branch_1, weights_two, gf_0, gf_1)
    hidden_1 = rows_1 + branch_1 + norms[2]
    z_1, z_0 = together(second_share(hidden_1), z_0)

    zf_0 = other_core(z_0)
    near_parts = mlp(z_0, g_0, weights_two, bias_up, f32)
    z_1 = gather_chips(z_1)
    zf_0, near_parts = together(zf_0, near_parts)
    far_parts = mlp(zf_0, gf_0, weights_two, bias_up, low_type)
    active_0, grad_up_0, feed_0, back_0, up_sums_0 = zip(near_parts, far_parts)
    z_1, back_0, feed_0 = together(z_1, back_0, feed_0)
    zf_1 = other_core(z_1)
    core_0 = other_core(back_0[1])
    near_parts = mlp(z_1, g_1, weights_two, bias_up, f32)
    zf_1, core_0, near_parts = together(zf_1, core_0, near_parts)
    back_0 = scatter_chips(back_0[0], core_0)
    core_feed_0 = other_core(feed_0[1])
    far_parts = mlp(zf_1, gf_1, weights_two, bias_up, low_type)
    active_1, grad_up_1, feed_1, back_1, up_sums_1 = zip(near_parts, far_parts)
    back_0, back_1, feed_1, core_feed_0 = together(back_0, back_1, feed_1, core_feed_0)
    hidden_grad_0, h_0, second_sums_0 = second_back(0, hidden_0, back_0)
    h_0, grad_up_1, back_1 = together(h_0, grad_up_1, back_1)
    h_0 = gather_chips(h_0)
    grads_two = grads_of(
        ([z_0, zf_0, z_1, zf_1], [*grad_up_0, *grad_up_1]),
        ([g_0, gf_0, g_1, gf_1], [*active_0, *active_1]),
    )
    core_1 = other_core(back_1[1])
    grads_two, h_0, core_1, core_feed_0 = together(grads_two, h_0, core_1, core_feed_0)
    summed_two = lax.psum_scatter(grads_two, "dp", scatter_dimension=0, tiled=True)
    chosen = choose_blocks(own_blocks, local_cols, weights_one, weights_two)
    hf_0, chosen, core_1, core_feed_0 = together(other_core(h_0), chosen, core_1, core_feed_0)

    back_1 = scatter_chips(back_1[0], core_1)
    output_0 = scatter_chips(feed_0[0], core_feed_0)
    keep_0, send_0, grad_qkv_0, sums_0 = attend_back(0, h_0, hf_0, kept_0)
    core_feed_1 = other_core(feed_1[1])
    keep_0, send_0, back_1, output_0, core_feed_1 = together(
        keep_0, send_0, back_1, output_0, core_feed_1
    )
    hidden_grad_1, h_1, second_sums_1 = second_back(1, hidden_1, back_1)
    h_1, keep_0, send_0, output_0 = together(h_1, keep_0, send_0, output_0)
    h_1 = gather_chips(h_1)
    core_0 = other_core(send_0)
    output_0 = (hidden_0 + output_0 + norms[5]).astype(low_type)
    h_1, core_0, output_0, core_feed_1 = together(h_1, core_0, output_0, core_feed_1)
    output_0 = exchange_back([output_0])[0]
    hf_1, core_0, core_feed_1 = together(other_core(h_1), core_0, core_feed_1)
    normed_back_0 = scatter_chips(keep_0, core_0)
    output_1 = scatter_chips(feed_1[0], core_feed_1)
    grads_out = grads_of(([h_0, hf_0, h_1, hf_1], [kept_0[0], kept_1[0]]))
    hf_1, grads_out = together(hf_1, grads_out)
    blocks_out = scatter_step(grads_out.reshape(data_count, shard_rows, local_cols), 1)
    keep_1, send_1, grad_qkv_1, sums_1 = attend_back(1, h_1, hf_1, kept_1)
    keep_1, send_1, normed_back_0, output_1, output_0, summed_two, blocks_out = together(
        keep_1, send_1, normed_back_0, output_1, output_0, summed_two, blocks_out
    )
    core_1 = other_core(send_1)
    grads_qkv = grads_of(([normed_0, normed_1], [grad_qkv_0, grad_qkv_1]))
    core_1, grads_qkv = together(core_1, grads_qkv)
    normed_back_1 = scatter_chips(keep_1, core_1)
    input_0, first_sums_0 = first_back(0, hidden_grad_0, normed_back_0)
    output_1 = (hidden_1 + output_1 + norms[5]).astype(low_type)
    input_0, output_1 = exchange_back([input_0, output_1])
    cut = 3 * local_cols // 2 // 128 * 128
    grads_one = [
        scatter_step(part.reshape(data_count, shard_rows, -1), 1)
        for part in (grads_qkv[:, :cut], grads_qkv[:, cut:])
    ]
    blocks_out = scatter_step(blocks_out, 2)
    output_0 = gather_chips(output_0)
    normed_back_1, grads_one, input_0, output_1, output_0, blocks_out = together(
        normed_back_1, grads_one, input_0, output_1, output_0, blocks_out
    )
    input_0, output_1 = gather_chips(input_0), gather_chips(output_1)
    input_1, first_sums_1 = first_back(1, hidden_grad_1, normed_back_1)
    summed_one = [scatter_grads(part, 2) for part in (*grads_one,)]
    summed_one.append(scatter_grads(blocks_out, 4))
    norm_grads_own = jnp.concatenate(
        [first_sums_0 + first_sums_1, second_sums_0 + second_sums_1], axis=0
    )
    qkv_sums = sums_0 + sums_1
    up_sums = [*up_sums_0, *up_sums_1]

    summed_one, input_1, norm_grads_own = together(summed_one, input_1, norm_grads_own)
    owned = exchange(
        to_slots(block_of, slot_count, local_cols, *summed_one, summed_two)
    )
    stats = (left_stats, right_stats, left_roots, right_roots)
    place = model_index.astype(jnp.int32).reshape(1)
    returns = [return_slots(i) for i in micros]
    outputs_given = give_back(0, returns[0], output_0, other_core(output_0), micro_count, [])
    inputs_given = give_back(0, returns[0], input_0, other_core(input_0), micro_count, [])
    outputs_given = give_back(
        1, returns[1], output_1, other_core(output_1), micro_count, outputs_given
    )
    norm_grads_sum = sum_over(norm_grads_own, "mp")
    owned, outputs_given, inputs_given, norm_grads_sum, input_1 = together(
        owned, outputs_given, inputs_given, norm_grads_sum, input_1
    )
    input_1 = exchange_back([input_1])[0]
    head_own = jnp.concatenate(
        [
            qkv_sums[:, :local_cols],
            qkv_sums[:, 2 * local_cols :],
            sum(up_sums).reshape(ffn_count, local_cols),
        ],
        axis=0,
    )
    vectors = jnp.concatenate([norm_grads_sum, head_own], axis=1)
    owned_grads = owned.reshape(data_count, slot_count, shard_rows, local_cols)
    owned_grads = jnp.swapaxes(owned_grads, 1, 2).reshape(model_width, slot_count, local_cols)
    owned_grads = owned_grads.astype(f32)
    near_part = gather_chips(owned[None])
    near_part, input_1, owned_grads = together(near_part, input_1, owned_grads)
    far_part = other_core(near_part)
    new_left, new_right, directions, squares = precondition(place, near_part, far_part, stats)
    input_1, squares = together(input_1, squares)
    squares = jnp.sum(squares, axis=(1, 2))
    square_total = sum_over(squares.reshape(1, slot_count), "mp")[0]
    square_total, input_1 = together(square_total, input_1)
    input_1 = gather_chips(input_1)
    vectors, input_1 = together(vectors, input_1)
    vectors = sum_over(vectors, "dp")
    inputs_given = give_back(
        1, returns[1], input_1, other_core(input_1), micro_count, inputs_given
    )[0]
    outputs_given = outputs_given[0]
    norm_all = vectors[:, :model_width]
    head_total = vectors[:, model_width:]
    norm_cols = norm_vectors.shape[1]
    norm_total = lax.dynamic_slice_in_dim(norm_all, data_index * norm_cols, norm_cols, 1)
    factor = lax.rsqrt(square_total / (model_width * model_width) + mean_eps)
    updated_blocks = jnp.stack(
        [
            chosen[s].astype(f32) - matrix_rate * factor[s] * directions[s]
            for s in range(slot_count)
        ],
        axis=1,
    )
    new_norm_state = stat_decay * norm_state + norm_total * norm_total
    new_norm_vectors = norm_vectors - vector_rate * norm_total / (
        jnp.sqrt(new_norm_state) + diag_eps
    )
    new_head_state = stat_decay * head_state + head_total * head_total
    new_head_vectors = head_vectors - vector_rate * head_total / (
        jnp.sqrt(new_head_state) + diag_eps
    )
    return (
        outputs_given,
        inputs_given,
        owned_grads,
        new_left,
        new_right,
        updated_blocks,
        norm_total,
        new_norm_state,
        new_norm_vectors,
        head_total,
        new_head_state,
        new_head_vectors,
    )


def solution(mesh):
    placed = (
        P(None, "dp", None),
        P(None, "dp", None),
        P(None, "dp", None),
        P(),
        P(),
        P("dp", None, "mp"),
        P(None, "dp"),
        P(None, "mp"),
        P("dp", "mp", None),
        P("dp", "mp", None),
        P("dp", None, None),
        P("dp", "mp", None),
        P(None, "dp"),
        P(None, "mp"),
    )
    return jax.shard_map(
        on_device,
        mesh=mesh,
        in_specs=placed,
        out_specs=(
            P(None, "dp", None),
            P(None, "dp", None),
            P(None, "dp", "mp"),
            P("dp", "mp", None),
            P("dp", "mp", None),
            P(None, "dp", "mp"),
            P(None, "dp"),
            P(None, "dp"),
            P(None, "dp"),
            P(None, "mp"),
            P(None, "mp"),
            P(None, "mp"),
        ),
        check_vma=False,
    )
```
